32 devices in a mesh: img: 8 (over z, y), seq: 4 (over x, core).
Axes of the slice: x: 2, y: 2, z: 4, core: 2. Of those that a mesh axis runs over, the one named last changes fastest.
Arguments:
- tokens: bfloat16 [8, 732, 1152], P('img', 'seq'), may hold values from -6 to 6
- offsets: int32 [8], P('img'), may hold values from 0 to 3
- w_qkv: bfloat16 [1152, 3456], P(('img', 'seq'))
- w_out: bfloat16 [1152, 1152], P(('img', 'seq')), may hold values from -4 to 4
- w_fc1: bfloat16 [1152, 4304], P(('img', 'seq')), may hold values from -0.1875 to 0.1875
- w_fc2: bfloat16 [1152, 4304], P(('img', 'seq')), may hold values from -0.09375 to 0.09375
- gains: bfloat16 [1152, 2], P(('img', 'seq')), may hold values from 0.25 to 1.75
- biases: bfloat16 [1152, 6], P(('img', 'seq')), may hold values from -3 to 3
- fc1_bias: bfloat16 [4304], replicated, may hold values from -3 to 3
- cotangent: bfloat16 [8, 732, 1152], P('img', 'seq'), may hold values from -6 to 6
Outputs:
- mixed: float32 [8, 732, 1152], P('img', 'seq')
- grad_tokens: float32 [8, 732, 1152], P('img', 'seq')
- grad_qkv: float32 [1152, 3456], P(('img', 'seq'))
- grad_out: float32 [1152, 1152], P(('img', 'seq'))
- grad_fc1: float32 [1152, 4304], P(('img', 'seq'))
- grad_fc2: float32 [1152, 4304], P(('img', 'seq'))
- grad_gains: float32 [1152, 2], P(('img', 'seq'))
- grad_biases: float32 [1152, 6], P(('img', 'seq'))
- grad_fc1_bias: float32 [4304], replicated
The draws below stay inside these ranges and needn't reach their ends.
Inputs may be any that keep to these rules, and one draw needn't show every extreme that they name: Image i's real tokens are positions offsets[i] to offsets[i] + 728.
All inputs are finite; a program needn't handle non-finite values.
Results may differ from the reference program's by a relative error of at most 0.012.
Values may be sent and summed in bfloat16 or wider, within the bound.
A program may use at most 256 MiB of HBM per device.

```python
import jax
import jax.numpy as jnp
from jax import lax

D = 1152
HEADS = 16
HD = 72
FF = 4304
VALID = 729
LEN = 732
IMAGE_TOTAL = 8


def draw_w_qkv(key, part):
    drawn = jax.random.normal(key, (D, 3 * D), jnp.float32) * D ** (-0.5)
    return drawn.astype(jnp.bfloat16)


def with_ends(entries, rng, smallest, top_value):
    place = [jax.random.randint(jax.random.fold_in(rng, axis), (), 0, length) for axis, length in enumerate(entries.shape)]
    longest = entries.shape.index(max(entries.shape))
    beside = place[:longest] + [(place[longest] + 1) % entries.shape[longest]] + place[longest + 1:]
    return entries.at[tuple(place)].set(smallest).at[tuple(beside)].set(top_value)


def block_scale(own_key, shape, pieces, least, top_value):
    def one(position, blocks):
        heights = jax.random.uniform(jax.random.fold_in(jax.random.fold_in(own_key, 6), position), (blocks,), jnp.float32, least / len(pieces), top_value / len(pieces))
        return jnp.repeat(jnp.exp(heights), shape[position] // blocks).reshape((-1,) + (1,) * (len(shape) - position - 1))

    level = one(*pieces[0])
    for cut in pieces[1:]:
        level = level * one(*cut)
    return level


def gaussian(key, dims, width, limit, split=(), held_as=jnp.bfloat16):
    array = jax.random.normal(key, dims, jnp.float32) * width
    if len(split) > 0:
        array = block_scale(key, dims, split, -0.22, 0.18) * array
    return jnp.clip(array, min=-limit, max=limit).astype(held_as)


def setup_inputs(seed: int = 0) -> dict:
    key_list = jax.random.split(jax.random.key(seed), 11)
    tokens = gaussian(key_list[0], (IMAGE_TOTAL, LEN, D), 1.0, 6.0, ((0, 8), (1, 4)))
    offsets = with_ends(jax.random.randint(key_list[1], (IMAGE_TOTAL,), 0, LEN - VALID + 1), jax.random.fold_in(key_list[1], 1), 0, LEN - VALID).astype(jnp.int32)
    w_qkv = draw_w_qkv(jax.random.fold_in(key_list[10], 71), 0)
    w_out = gaussian(key_list[3], (D, D), (max(D // 512, 1)) ** -0.5, 4.0, ((0, 32),))
    w_fc1 = gaussian(key_list[4], (D, FF), D ** -0.5, 0.1875, ((0, 32),))
    w_fc2 = gaussian(key_list[5], (D, FF), FF ** -0.5, 0.09375, ((0, 32),))
    gains = jnp.clip(1.0 + 0.15 * jax.random.normal(key_list[6], (D, 2), jnp.float32), 0.25, 1.75).astype(jnp.bfloat16)
    biases = gaussian(key_list[7], (D, 6), 0.5, 3.0, ((0, 32),))
    fc1_bias = gaussian(key_list[8], (FF,), 0.5, 3.0)
    cotangent = gaussian(key_list[9], (IMAGE_TOTAL, LEN, D), 1.0, 6.0, ((0, 8), (1, 4)))
    return dict(tokens=tokens, offsets=offsets, w_qkv=w_qkv, w_out=w_out, w_fc1=w_fc1, w_fc2=w_fc2, gains=gains, biases=biases, fc1_bias=fc1_bias, cotangent=cotangent)


@jax.custom_vjp
def low(v):
    return lax.optimization_barrier(v.astype(jnp.bfloat16)).astype(jnp.float32)

@jax.custom_vjp
def low_back(v):
    return v

def low_keep(v):
    return (low(v), None)

def low_pass(kept, grad):
    return (grad,)

def back_keep(v):
    return (v, None)

def back_low(kept, grad):
    return (low(grad),)
low.defvjp(low_keep, low_pass)
low_back.defvjp(back_keep, back_low)
masked_score = -1000000000.0
norm_epsilon = 1e-06
highest = lax.Precision.HIGHEST

def layer_norm(values, gain_col, bias_col):
    average = lax.optimization_barrier(jnp.mean(values, -1, keepdims=True))
    centered = values - average
    variance = lax.optimization_barrier(jnp.mean(centered * centered, -1, keepdims=True))
    return centered * lax.rsqrt(variance + norm_epsilon) * gain_col + bias_col

def forward(inputs, starts, params):
    w_qkv, w_out, w_fc1, w_fc2, gain_cols, bias_cols, fc1_bias = params
    group = inputs.shape[0]
    positions = jnp.arange(LEN, dtype=jnp.int32)
    valid = (positions[None, :] >= starts[:, None]) & (positions[None, :] < starts[:, None] + VALID)
    flat_rows = inputs.reshape(-1, D)
    h_one = low(layer_norm(flat_rows, gain_cols[:, 0], bias_cols[:, 0]))
    qkv_bias = jnp.concatenate([bias_cols[:, 1], jnp.zeros_like(bias_cols[:, 1]), bias_cols[:, 2]])
    projected = jnp.dot(h_one, w_qkv, precision=highest) + qkv_bias
    projected = low(low_back(projected))
    queries = projected[:, :D].reshape(group, LEN, HEADS, HD)
    key_rows = projected[:, D:2 * D].reshape(group, LEN, HEADS, HD)
    value_rows = projected[:, 2 * D:].reshape(group, LEN, HEADS, HD)
    scores = jnp.einsum('gqhd,gkhd->ghqk', queries, key_rows, precision=highest) * HD ** (-0.5)
    scores = low_back(scores)
    scores = jnp.where(valid[:, None, None, :], scores, masked_score)
    maxima = lax.optimization_barrier(jnp.max(scores, -1, keepdims=True))
    exponent = jnp.exp(scores - maxima)
    probs = exponent / lax.optimization_barrier(jnp.sum(exponent, -1, keepdims=True))
    attended = jnp.einsum('ghqk,gkhd->gqhd', low(probs), value_rows, precision=highest).reshape(-1, D)
    attended = low(low_back(attended))
    branch_one = low_back(jnp.dot(attended, w_out, precision=highest) + bias_cols[:, 3])
    middle = flat_rows + branch_one
    h_two = low(layer_norm(middle, gain_cols[:, 1], bias_cols[:, 4]))
    preact = low_back(jnp.dot(h_two, w_fc1, precision=highest) + fc1_bias)
    activated = low(jax.nn.gelu(preact, approximate=True))
    branch_two = low_back(jnp.dot(activated, w_fc2.T, precision=highest) + bias_cols[:, 5])
    row_valid = valid.reshape(-1, 1).astype(jnp.float32)
    return (row_valid * (middle + branch_two)).reshape(inputs.shape)

def reference(tokens, offsets, w_qkv, w_out, w_fc1, w_fc2, gains, biases, fc1_bias, cotangent):
    params = (w_qkv.astype(jnp.float32), w_out.astype(jnp.float32), w_fc1.astype(jnp.float32), w_fc2.astype(jnp.float32), gains.astype(jnp.float32), biases.astype(jnp.float32), fc1_bias.astype(jnp.float32))
    count = tokens.shape[0]
    inputs = tokens.astype(jnp.float32).reshape(count // 2, 2, LEN, D)
    cots = cotangent.astype(jnp.float32).reshape(count // 2, 2, LEN, D)
    starts = offsets.astype(jnp.int32).reshape(count // 2, 2)

    def scan_step(totals, group_item):
        group_in, group_cot, group_starts = group_item
        result, pull = jax.vjp(lambda inner, weights: forward(inner, group_starts, weights), group_in, params)
        grad_in, grad_params = pull(group_cot)
        totals = tuple((a + b for a, b in zip(totals, grad_params)))
        return (totals, (result, grad_in))
    zero_grads = tuple((jnp.zeros_like(p) for p in params))
    grad_totals, (outputs, grad_inputs) = lax.scan(scan_step, zero_grads, (inputs, cots, starts))
    return (outputs.reshape(count, LEN, D), grad_inputs.reshape(count, LEN, D), grad_totals[0], grad_totals[1], grad_totals[2], grad_totals[3], grad_totals[4], grad_totals[5], grad_totals[6])
```

```python
from functools import partial

import jax
import jax.numpy as jnp
from jax import lax
from jax.experimental import pallas as pl
from jax.experimental.pallas import tpu as pltpu
from jax.sharding import PartitionSpec as P

HEADS = 16
VALID = 729


masked_score = -1000000000.0
norm_epsilon = 1e-06


def layer_norm(values, gain_col, bias_col):
    average = jnp.mean(values, -1, keepdims=True)
    centered = values - average
    variance = jnp.mean(centered * centered, -1, keepdims=True)
    return centered * lax.rsqrt(variance + norm_epsilon) * gain_col + bias_col


def row_dot(left, right):
    return lax.dot_general(
        left, right, (((0,), (0,)), ((), ())), preferred_element_type=jnp.float32
    )


def last_dot(left, right):
    return lax.dot_general(
        left, right, (((1,), (1,)), ((), ())), preferred_element_type=jnp.float32
    )


def split_heads(tensor, images_here, count, head_count, head_dim):
    return tensor.reshape(images_here, count, head_count, head_dim).transpose(2, 0, 1, 3)


def join_heads(tensor):
    head_count, images_here, count, head_dim = tensor.shape
    return tensor.transpose(1, 2, 0, 3).reshape(images_here, count, head_count * head_dim)


VMEM_BYTES = 62 * 2**20
MESH_IDS = pl.DeviceIdType.MESH
F32 = jnp.float32
BF16 = jnp.bfloat16
LANES = 128
PIECE = 48
BLOCK = 192
HEAD_ROWS = 80
NN = (((1,), (0,)), ((), ()))
NT = (((1,), (1,)), ((), ()))
TN = (((0,), (0,)), ((), ()))


def mm(left, right, dims):
    return lax.dot_general(left, right, dims, preferred_element_type=F32)


def normalize(values):
    average = jnp.mean(values, -1, keepdims=True)
    centered = values - average
    variance = jnp.mean(centered * centered, -1, keepdims=True)
    inverse = lax.rsqrt(variance + norm_epsilon)
    return centered * inverse, inverse


def norm_back(grad, gain, hat, inverse):
    scaled = grad * gain
    first = jnp.mean(scaled, -1, keepdims=True)
    second = jnp.mean(scaled * hat, -1, keepdims=True)
    return inverse * (scaled - first - hat * second)


def lane_ids(rows):
    return lax.broadcasted_iota(jnp.int32, (rows, LANES), 1)


def lane_window(tiles, start, width, lanes):
    tile, offset = divmod(start, LANES)
    if offset == 0:
        return tiles[tile]
    first = pltpu.roll(tiles[tile], LANES - offset, 1)
    if offset + width <= LANES:
        return first
    second = pltpu.roll(tiles[tile + 1], LANES - offset, 1)
    return jnp.where(lanes < LANES - offset, first, second)


def layer_kernel(
    dims,
    off_ref, pq, po, p1, p2, tok, cot, fb_ref,
    o_mixed, o_gtok, o_fq, o_fo, o_f1, o_f2, o_sm, o_sh,
    wq, wo, w1, w2, rq, ro, r1, r2, tmp,
    xs, gc, h1, h2, act, gp, dg, qkv, attm, att_t, gatt, gpj, lse,
    g1, g2, go, gq, y1, y2, yo, yq, z1, z2, zo, zq, f1, f2, fo, fq,
    sb_a, cr_a, xr_a, sb_b, cr_b, xr_b, pf, prm, bh, sms, smr, shs, shr,
    ssem, rsem, lsem,
):
    slice_len, d, hd, f, qw, n_z = dims
    scale = hd ** (-0.5)
    mask_low = masked_score / scale
    chunk = 256
    rows = 4 * BLOCK
    i, s = lax.axis_index("img"), lax.axis_index("seq")
    z, y = lax.div(i, 2), lax.rem(i, 2)
    x, c = lax.div(s, 2), lax.rem(s, 2)
    k = 2 * c + x
    cy = c == y
    core_peer = (i, x * 2 + 1 - c)
    x_peer = (i, (1 - x) * 2 + c)
    y_peer = (z * 2 + 1 - y, s)
    rb = wq.shape[0] // (2 * n_z)
    own = rb // 4

    def z_at(t):
        return lax.rem(z + t + n_z, n_z)

    def z_dev(t):
        return (z_at(t) * 2 + y, s)

    def s_at(t):
        return lax.rem(s + t + 4, 4)

    count = [0]

    def take(n=1):
        first = count[0]
        count[0] += n
        return first

    def copy(src, dst, index, device):
        return pltpu.make_async_remote_copy(
            src, dst, ssem.at[index], rsem.at[index], device_id=device, device_id_type=MESH_IDS
        )

    sends = []

    def send(src, dst, index, device):
        made = copy(src, dst, index, device)
        made.start()
        sends.append(made)

    def token_rows(j):
        return pl.ds(pl.multiple_of(j * BLOCK, BLOCK), BLOCK)

    def img_rows(b):
        return pl.ds(pl.multiple_of(b * rb, 16), rb)

    barrier = pltpu.get_barrier_semaphore()
    partners = [(i, s_at(t)) for t in (1, 2, 3)] + [z_dev(t) for t in range(1, n_z)] + [y_peer]
    for partner in partners:
        pl.semaphore_signal(barrier, inc=1, device_id=partner, device_id_type=MESH_IDS)
    pl.semaphore_wait(barrier, len(partners))

    class Gather:
        def __init__(self, piece, recv, full, local_index):
            self.piece, self.recv, self.full = piece, recv, full
            self.width = full.shape[1]
            self.sp, self.sz, self.sy = take(4), take(n_z), take(n_z)
            self.local = local_index

        def pieces(self):
            pltpu.make_async_copy(self.piece.at[s], self.recv.at[s], lsem.at[self.local]).start()
            for t in (1, 2, 3):
                to = s_at(t)
                send(self.piece.at[to], self.recv.at[s], self.sp + t, (i, to))

        def assemble(self):
            pltpu.make_async_copy(self.piece.at[s], self.recv.at[s], lsem.at[self.local]).wait()
            for t in (1, 2, 3):
                came = self.recv.at[s_at(-t)]
                copy(came, came, self.sp + t, (i, s_at(-t))).wait_recv()
            part = rb // 4
            for j in range(4):
                tmp[part * j : part * j + PIECE, 0 : self.width] = self.recv[j].astype(F32)
            self.full[img_rows(i), :] = tmp[0:rb, 0 : self.width].astype(BF16)

        def block(self, t, side):
            return self.full.at[img_rows(z_at(-t) * 2 + side)]

        def along_z(self):
            own = self.block(0, y)
            for t in range(1, n_z):
                send(own, own, self.sz + t, z_dev(t))
            send(own, own, self.sy, y_peer)

        def forward(self):
            for t in range(1, n_z):
                came = self.block(t, y)
                copy(came, came, self.sz + t, z_dev(-t)).wait_recv()
                send(came, came, self.sy + t, y_peer)

        def finish(self):
            for t in range(n_z):
                came = self.block(t, 1 - y)
                copy(came, came, self.sy + t, y_peer).wait_recv()

    gather_q = Gather(pq, rq, wq, 0)
    gather_1 = Gather(p1, r1, w1, 1)
    gather_2 = Gather(p2, r2, w2, 2)
    o_piece, o_z, o_y = take(), take(n_z), take(n_z)

    def head_block(array, t):
        return array.at[pl.ds(pl.multiple_of(z_at(-t) * LANES, LANES), HEAD_ROWS)]

    def o_start():
        @pl.when(cy)
        def _():
            pltpu.make_async_copy(po, ro.at[c], lsem.at[3]).start()

        @pl.when(jnp.logical_not(cy))
        def _():
            copy(po, ro.at[c], o_piece, core_peer).start()

    def o_assemble():
        for h in range(4):
            wo[h * LANES + HEAD_ROWS : (h + 1) * LANES, :] = jnp.zeros((LANES - HEAD_ROWS, d), BF16)

        @pl.when(cy)
        def _():
            pltpu.make_async_copy(po, ro.at[c], lsem.at[3]).wait()
            copy(po, ro.at[1 - c], o_piece, core_peer).wait_recv()
            for j in range(2):
                tmp[own * j : own * j + PIECE, :] = ro[j].astype(F32)
            wo[pl.ds(pl.multiple_of(z * LANES, LANES), HEAD_ROWS), :] = tmp[0:HEAD_ROWS, :].astype(BF16)

    def o_along_z():
        @pl.when(cy)
        def _():
            mine = head_block(wo, 0)
            for t in range(1, n_z):
                copy(mine, mine, o_z + t, z_dev(t)).start()
            copy(mine, mine, o_y, y_peer).start()

    def o_forward():
        @pl.when(cy)
        def _():
            for t in range(1, n_z):
                came = head_block(wo, t)
                copy(came, came, o_z + t, z_dev(-t)).wait_recv()
                copy(came, came, o_y + t, y_peer).start()

    def o_finish():
        @pl.when(jnp.logical_not(cy))
        def _():
            for t in range(n_z):
                came = head_block(wo, t)
                copy(came, came, o_y + t, y_peer).wait_recv()

    def o_sent():
        @pl.when(jnp.logical_not(cy))
        def _():
            copy(po, ro.at[c], o_piece, core_peer).wait_send()

        @pl.when(cy)
        def _():
            mine = head_block(wo, 0)
            for t in range(1, n_z):
                copy(mine, mine, o_z + t, z_dev(t)).wait_send()
            for t in range(n_z):
                came = head_block(wo, t)
                copy(came, came, o_y + t, y_peer).wait_send()

    class TokenGather:
        def __init__(self, full):
            self.full = full
            self.sx, self.sc, self.sd = take(), take(), take()

        def at(self, j):
            return self.full.at[token_rows(j)]

        def start(self, own):
            self.own = own
            copy(own, self.at(s), self.sx, x_peer).start()
            copy(own, self.at(s), self.sc, core_peer).start()

        def forward(self):
            across = self.at((1 - x) * 2 + c)
            copy(across, across, self.sx, x_peer).wait_recv()
            copy(across, across, self.sd, core_peer).start()

        def finish(self):
            for index, j in ((self.sc, x * 2 + 1 - c), (self.sd, (1 - x) * 2 + 1 - c)):
                copy(self.at(j), self.at(j), index, core_peer).wait_recv()
            copy(self.own, self.at(s), self.sx, x_peer).wait_send()
            copy(self.own, self.at(s), self.sc, core_peer).wait_send()
            across = self.at((1 - x) * 2 + c)
            copy(across, across, self.sd, core_peer).wait_send()

    def seq_sum_start(partial, sb, cr):
        first = take(2)
        last = take()

        def step(t, carry):
            away = t < 2
            j = jnp.where(away, 2 * t + 1 - c, jnp.where(t == 2, 2 * (1 - x) + c, s))
            part = partial(j)

            @pl.when(away)
            def _():
                sb[t] = part.astype(BF16)
                copy(sb.at[t], cr.at[t], first + t, core_peer).start()

            @pl.when(t >= 2)
            def _():
                pf[t - 2] = part

            return carry

        lax.fori_loop(0, 4, step, 0)
        return first, last

    def seq_sum_across(handle, sb, cr, xr):
        first, last = handle
        there = 1 - x
        copy(cr.at[there], cr.at[there], first + there, core_peer).wait_recv()
        sb[2] = (pf[0] + cr[there].astype(F32)).astype(BF16)
        copy(sb.at[2], xr, last, x_peer).start()

    def seq_sum_finish(handle, sb, cr, xr):
        first, last = handle
        copy(cr.at[x], cr.at[x], first + x, core_peer).wait_recv()
        copy(xr, xr, last, x_peer).wait_recv()
        for t in range(2):
            copy(sb.at[t], cr.at[t], first + t, core_peer).wait_send()
        copy(sb.at[2], xr, last, x_peer).wait_send()
        return pf[1] + cr[x].astype(F32) + xr[...].astype(F32)

    class Reduce:
        def __init__(self, grad, yr, zr, fs, out):
            self.grad, self.yr, self.zr, self.fs, self.out = grad, yr, zr, fs, out
            self.width = grad.shape[1]
            self.sy, self.sz, self.sp = take(n_z), take(n_z), take(4)

        def at(self, t, side):
            return img_rows(z_at(t) * 2 + side)

        def across_y(self):
            for t in (*range(1, n_z), 0):
                send(self.grad.at[self.at(t, 1 - y)], self.yr.at[t], self.sy + t, y_peer)

        def along_z(self):
            for t in range(1, n_z):
                copy(self.yr.at[t], self.yr.at[t], self.sy + t, y_peer).wait_recv()
                mine = self.at(t, y)
                self.grad[mine, :] = (self.grad[mine, :].astype(F32) + self.yr[t].astype(F32)).astype(BF16)
                send(self.grad.at[mine], self.zr.at[t - 1], self.sz + t, z_dev(t))

        def pieces(self):
            copy(self.yr.at[0], self.yr.at[0], self.sy, y_peer).wait_recv()
            total = self.grad[self.at(0, y), :].astype(F32) + self.yr[0].astype(F32)
            for t in range(1, n_z):
                came = self.zr.at[t - 1]
                copy(came, came, self.sz + t, z_dev(-t)).wait_recv()
                total += self.zr[t - 1].astype(F32)
            tmp[0:rb, 0 : self.width] = total
            part = rb // 4
            for j in range(4):
                self.fs[j] = tmp[part * j : part * j + PIECE, 0 : self.width].astype(BF16)
            pltpu.make_async_copy(self.fs.at[s], self.out.at[s], lsem.at[4]).start()
            for t in (1, 2, 3):
                to = s_at(t)
                send(self.fs.at[to], self.out.at[s], self.sp + t, (i, to))
            pltpu.make_async_copy(self.fs.at[s], self.out.at[s], lsem.at[4]).wait()

        def finish(self):
            for t in (1, 2, 3):
                came = self.out.at[s_at(-t)]
                copy(came, came, self.sp + t, (i, s_at(-t))).wait_recv()

    reduce_2 = Reduce(g2, y2, z2, f2, o_f2)
    reduce_1 = Reduce(g1, y1, z1, f1, o_f1)
    reduce_q = Reduce(gq, yq, zq, fq, o_fq)
    ro_y, ro_z, ro_p = take(n_z), take(n_z), take()

    def ro_across_y():
        @pl.when(jnp.logical_not(cy))
        def _():
            for t in (*range(1, n_z), 0):
                copy(head_block(go, -t), yo.at[t], ro_y + t, y_peer).start()

    def ro_along_z():
        @pl.when(cy)
        def _():
            for t in range(1, n_z):
                copy(yo.at[t], yo.at[t], ro_y + t, y_peer).wait_recv()
                mine = pl.ds(pl.multiple_of(z_at(t) * LANES, LANES), HEAD_ROWS)
                go[mine, :] = (go[mine, :].astype(F32) + yo[t].astype(F32)).astype(BF16)
                copy(go.at[mine], zo.at[t - 1], ro_z + t, z_dev(t)).start()

    def ro_pieces():
        @pl.when(cy)
        def _():
            copy(yo.at[0], yo.at[0], ro_y, y_peer).wait_recv()
            mine = pl.ds(pl.multiple_of(z * LANES, LANES), HEAD_ROWS)
            total = go[mine, :].astype(F32) + yo[0].astype(F32)
            for t in range(1, n_z):
                copy(zo.at[t - 1], zo.at[t - 1], ro_z + t, z_dev(-t)).wait_recv()
                total += zo[t - 1].astype(F32)
            tmp[0:HEAD_ROWS, :] = total
            for j in range(2):
                fo[j] = tmp[own * j : own * j + PIECE, :].astype(BF16)
            pltpu.make_async_copy(fo.at[c], o_fo, lsem.at[5]).start()
            copy(fo.at[1 - c], o_fo, ro_p, core_peer).start()
            pltpu.make_async_copy(fo.at[c], o_fo, lsem.at[5]).wait()

    def ro_finish():
        @pl.when(cy)
        def _():
            for t in range(1, n_z):
                copy(head_block(go, -t), zo.at[t - 1], ro_z + t, z_dev(t)).wait_send()
            copy(fo.at[1 - c], o_fo, ro_p, core_peer).wait_send()

        @pl.when(jnp.logical_not(cy))
        def _():
            for t in range(n_z):
                copy(head_block(go, -t), yo.at[t], ro_y + t, y_peer).wait_send()
            copy(o_fo, o_fo, ro_p, core_peer).wait_recv()

    def real_rows(j, width):
        t = lax.broadcasted_iota(jnp.int32, (BLOCK, width), 0)
        position = j * slice_len + t
        return (t < slice_len) & (position >= off_ref[0]) & (position < off_ref[0] + VALID)

    tokens_in, cot_in = TokenGather(xs), TokenGather(gc)
    gather_q.pieces()
    pltpu.make_async_copy(tok, xs.at[token_rows(s)], lsem.at[6]).start()
    pltpu.make_async_copy(cot, gc.at[token_rows(s)], lsem.at[7]).start()
    tokens_in.start(tok)
    o_start()
    gather_1.pieces()
    gather_2.pieces()
    cot_in.start(cot)
    sms[0] = jnp.zeros(sms.shape[1:], F32)
    shs[0] = jnp.zeros(shs.shape[1:], F32)
    tmp[...] = jnp.zeros(tmp.shape, F32)

    gather_q.assemble()
    gather_q.along_z()
    tokens_in.forward()
    o_assemble()
    gather_1.assemble()
    gather_2.assemble()
    gather_q.forward()
    o_along_z()
    gather_1.along_z()
    cot_in.forward()
    pltpu.make_async_copy(tok, xs.at[token_rows(s)], lsem.at[6]).wait()
    pltpu.make_async_copy(cot, gc.at[token_rows(s)], lsem.at[7]).wait()
    tokens_in.finish()
    cot_in.finish()

    def mask_cotangent(j, carry):
        kept = gc[token_rows(j), :].astype(F32)
        gc[token_rows(j), :] = jnp.where(real_rows(j, d), kept, 0.0).astype(BF16)
        return carry

    lax.fori_loop(0, 4, mask_cotangent, 0)
    gather_q.finish()

    packed = 3 * 4 * hd
    base = packed // LANES * LANES
    columns = wq[:, base : base + LANES].astype(F32)
    prm[...] = columns.T[packed - base : packed - base + 8, :]
    one_lane = lane_ids(1)
    for which, row in ((0, 3), (1, 4)):
        tiles = [prm[row : row + 1, LANES * t : LANES * (t + 1)] for t in range(d // LANES)]
        for head in range(d // hd):
            bh[which, head : head + 1, :] = lane_window(tiles, head * hd, hd, one_lane)
    gain_one, gain_two, shift_one = prm[0:1, :], prm[1:2, :], prm[2:3, :]
    bias_out, shift_two, bias_two = prm[5:6, :], prm[6:7, :], prm[7:8, :]

    lanes = lane_ids(BLOCK)

    def project(j, carry):
        hat, _ = normalize(xs[token_rows(j), :].astype(F32))
        low = (hat * gain_one + shift_one).astype(BF16)
        h1[token_rows(j), :] = low
        wide = mm(low, wq[...], NN)
        tiles = [wide[:, LANES * t : LANES * (t + 1)] for t in range(qw // LANES)]
        key_low = jnp.where(real_rows(j, LANES), 0.0, mask_low)
        for n in range(12):
            kind, head = divmod(n, 4)
            part = lane_window(tiles, n * hd, hd, lanes)
            if kind != 1:
                part = part + bh[kind // 2, pl.ds(4 * head + k, 1), :]
            beside = key_low if kind == 1 else jnp.ones_like(part)
            part = jnp.where(lanes < hd, part, jnp.where(lanes == hd, beside, 0.0))
            qkv[n, token_rows(j), :] = part.astype(BF16)
        return carry

    lax.fori_loop(0, 4, project, 0)

    sublanes = lax.broadcasted_iota(jnp.int32, (LANES, chunk), 0)

    def attend(step, carry):
        head, part = lax.div(step, rows // chunk), lax.rem(step, rows // chunk)
        at = pl.ds(pl.multiple_of(part * chunk, chunk), chunk)
        scores = mm(qkv[4 + head], qkv[head, at, :], NT)
        top = jnp.max(scores, 0, keepdims=True)
        weights = jnp.exp((scores - top) * scale).astype(BF16)
        summed = mm(qkv[8 + head], weights, TN)
        total = summed[hd : hd + 1, :]
        result = jnp.where(sublanes < hd, summed / total, 0.0)
        att_t[head, :, at] = result.astype(BF16)
        attm[at, pl.ds(pl.multiple_of(head * LANES, LANES), LANES)] = result.T.astype(BF16)
        lse[head, :, at] = top * scale + jnp.log(total)
        return carry

    lax.fori_loop(0, 4 * (rows // chunk), attend, 0)

    o_forward()
    o_finish()
    sum_one = seq_sum_start(lambda j: mm(attm[token_rows(j), :], wo[...], NN), sb_a, cr_a)
    seq_sum_across(sum_one, sb_a, cr_a, xr_a)
    branch = seq_sum_finish(sum_one, sb_a, cr_a, xr_a)
    o_mixed[...] = xs[token_rows(s), :].astype(F32) + branch + bias_out
    hat, _ = normalize(o_mixed[...])
    h2[token_rows(s), :] = (hat * gain_two + shift_two).astype(BF16)
    h2_in = TokenGather(h2)
    h2_in.start(h2.at[token_rows(s)])
    h2_in.forward()
    gather_1.forward()
    gather_2.along_z()
    h2_in.finish()
    gather_1.finish()

    slope = (2.0 / 3.141592653589793) ** 0.5

    def widen(j, carry):
        pre = mm(h2[token_rows(j), :], w1[...], NN) + fb_ref[...]
        square = pre * pre
        curve = jnp.tanh(slope * pre * (1.0 + 0.044715 * square))
        half = 0.5 + 0.5 * curve
        act[token_rows(j), :] = (pre * half).astype(BF16)
        dg[token_rows(j), :] = half + 0.5 * slope * pre * (1.0 - curve * curve) * (1.0 + 0.134145 * square)
        return carry

    lax.fori_loop(0, 4, widen, 0)

    def column_products(left, right, out):
        def step(t, carry):
            at = pl.ds(pl.multiple_of(t * LANES, LANES), LANES)
            out[at, :] = mm(left[:, at], right[...], TN).astype(BF16)
            return carry

        lax.fori_loop(0, left.shape[1] // LANES, step, 0)

    column_products(gc, act, g2)
    gather_2.forward()
    reduce_2.across_y()
    gather_2.finish()

    def hidden_back(j):
        at = token_rows(j)
        low = (mm(gc[at, :], w2[...], NN) * dg[at, :]).astype(BF16)
        gp[at, :] = low
        column = jnp.sum(low.astype(F32), 0, keepdims=True)
        sms[0, pl.ds(8 + s, 1), :] += column
        return mm(low, w1[...], NT)

    sum_two = seq_sum_start(hidden_back, sb_a, cr_a)
    seq_sum_across(sum_two, sb_a, cr_a, xr_a)
    column_products(h2, gp, g1)
    reduce_2.along_z()
    reduce_1.across_y()
    grad_h = seq_sum_finish(sum_two, sb_a, cr_a, xr_a)
    hat, inverse = normalize(o_mixed[...])
    kept = gc[token_rows(s), :].astype(F32)
    grad_x = kept + norm_back(grad_h, gain_two, hat, inverse)
    o_gtok[...] = grad_x
    low = grad_x.astype(BF16)
    sms[0, 1:2, :] = jnp.sum(grad_h * hat, 0, keepdims=True)
    sms[0, 4:5, :] = jnp.sum(grad_h, 0, keepdims=True)
    sms[0, 5:6, :] = jnp.sum(kept, 0, keepdims=True)
    sms[0, 3:4, :] = jnp.sum(low.astype(F32), 0, keepdims=True)
    gc[token_rows(s), :] = low
    gb_in = TokenGather(gc)
    gb_in.start(gc.at[token_rows(s)])
    gb_in.forward()

    sum_three = seq_sum_start(lambda j: mm(act[token_rows(j), :], w2[...], NT), sb_b, cr_b)
    gb_in.finish()
    seq_sum_across(sum_three, sb_b, cr_b, xr_b)

    def attended_back(j, carry):
        wide = mm(gc[token_rows(j), :], wo[...], NT).astype(BF16)
        for head in range(4):
            gatt[head, token_rows(j), :] = wide[:, head * LANES : (head + 1) * LANES]
        return carry

    lax.fori_loop(0, 4, attended_back, 0)
    branch = seq_sum_finish(sum_three, sb_b, cr_b, xr_b)
    o_mixed[...] = jnp.where(real_rows(s, d), o_mixed[...] + branch + bias_two, 0.0)

    def out_products(head, carry):
        at = pl.ds(pl.multiple_of(head * LANES, LANES), LANES)
        go[at, :] = mm(att_t[head], gc[...], NN).astype(BF16)
        return carry

    lax.fori_loop(0, 4, out_products, 0)
    ro_across_y()
    reduce_1.along_z()
    reduce_2.pieces()

    wide_lanes = lane_ids(rows)
    chunk_lanes = lane_ids(chunk)

    def attend_back(head, carry):
        grad_k = jnp.zeros((rows, LANES), F32)
        grad_v = jnp.zeros((rows, LANES), F32)
        grad_q = []
        for part in range(rows // chunk):
            at = slice(part * chunk, (part + 1) * chunk)
            query, grad_out = qkv[head, at, :], gatt[head, at, :]
            scores = mm(qkv[4 + head], query, NT)
            probs = jnp.exp(scores * scale - lse[head, :, at])
            grad_p = mm(qkv[8 + head], grad_out, NT)
            delta = jnp.sum(probs * grad_p, 0, keepdims=True)
            grad_s = (probs * (grad_p - delta)).astype(BF16)
            grad_k += mm(grad_s, query, NN)
            grad_v += mm(probs.astype(BF16), grad_out, NN)
            grad_q.append(mm(qkv[4 + head], grad_s, TN))
        for part in range(rows // chunk):
            at = slice(part * chunk, (part + 1) * chunk)
            low = jnp.where(chunk_lanes < hd, grad_q[part].T * scale, 0.0).astype(BF16)
            qkv[head, at, :] = low
            shs[0, pl.ds(4 * head + k, 1), :] += jnp.sum(low.astype(F32), 0, keepdims=True)
        qkv[4 + head] = jnp.where(wide_lanes < hd, grad_k * scale, 0.0).astype(BF16)
        low = grad_v.astype(BF16)
        qkv[8 + head] = low
        shs[0, pl.ds(16 + 4 * head + k, 1), :] = jnp.sum(low.astype(F32), 0, keepdims=True)
        return carry

    lax.fori_loop(0, 4, attend_back, 0)

    def pack(j, carry):
        tiles = [None] * (qw // LANES)
        for n in range(12):
            tile, offset = divmod(n * hd, LANES)
            part = qkv[n, token_rows(j), :].astype(F32)
            if offset:
                part = pltpu.roll(part, offset, 1)
            ends = [(tile, lanes >= offset)]
            if offset + hd > LANES:
                ends.append((tile + 1, lanes < offset + hd - LANES))
            for to, where in ends:
                kept = jnp.where(where, part, 0.0)
                tiles[to] = kept if tiles[to] is None else tiles[to] + kept
        for to, tile in enumerate(tiles):
            gpj[token_rows(j), LANES * to : LANES * (to + 1)] = tile.astype(BF16)
        return carry

    lax.fori_loop(0, 4, pack, 0)
    column_products(h1, gpj, gq)
    reduce_q.across_y()
    ro_along_z()

    def tokens_back(j):
        part = mm(gpj[token_rows(j), :], wq[...], NT)
        hat, _ = normalize(xs[token_rows(j), :].astype(F32))
        sms[0, 0:1, :] += jnp.sum(part * hat, 0, keepdims=True)
        sms[0, 2:3, :] += jnp.sum(part, 0, keepdims=True)
        return part

    sum_four = seq_sum_start(tokens_back, sb_a, cr_a)
    sm_at, sh_at = take(7), take(7)

    def vectors(stage, slots, devices):
        for slot, device in zip(slots, devices, strict=True):
            send(sms.at[stage], smr.at[slot], sm_at + slot, device)
            send(shs.at[stage], shr.at[slot], sh_at + slot, device)

    def vectors_sum(stage, slots, devices):
        for slot, device in zip(slots, devices, strict=True):
            copy(smr.at[slot], smr.at[slot], sm_at + slot, device).wait_recv()
            copy(shr.at[slot], shr.at[slot], sh_at + slot, device).wait_recv()
        total, heads = sms[stage], shs[stage]
        for slot in slots:
            total += smr[slot]
            heads += shr[slot]
        return total, heads

    vectors(0, (0,), (y_peer,))
    seq_sum_across(sum_four, sb_a, cr_a, xr_a)
    reduce_1.pieces()
    sms[1], shs[1] = vectors_sum(0, (0,), (y_peer,))
    vectors(1, (1, 2, 3), [z_dev(t) for t in (1, 2, 3)])
    reduce_q.along_z()
    sms[2], shs[2] = vectors_sum(1, (1, 2, 3), [z_dev(-t) for t in (1, 2, 3)])
    vectors(2, (4, 5, 6), [(i, s_at(t)) for t in (1, 2, 3)])
    grad_h = seq_sum_finish(sum_four, sb_a, cr_a, xr_a)
    hat, inverse = normalize(xs[token_rows(s), :].astype(F32))
    o_gtok[...] += norm_back(grad_h, gain_one, hat, inverse)
    ro_pieces()
    o_sm[...], o_sh[...] = vectors_sum(2, (4, 5, 6), [(i, s_at(-t)) for t in (1, 2, 3)])
    reduce_q.pieces()
    reduce_2.finish()
    reduce_1.finish()
    ro_finish()
    o_sent()
    reduce_q.finish()
    for made in sends:
        made.wait_send()


def whole_layer(tokens, offsets, w_qkv, w_out, w_fc1, w_fc2, gains, biases, fc1_bias, cotangent):
    _, slice_len, d = tokens.shape
    hd = d // HEADS
    own, wide = w_fc1.shape
    f = wide // 4
    f_pad = -(-f // LANES) * LANES
    packed = 12 * hd
    qw = -(-(packed + 8) // LANES) * LANES
    n_z = lax.axis_size("img") // 2
    rb = own * 4
    rows = 4 * BLOCK
    seq = lax.axis_index("seq")

    def grow(array, *shape):
        return jnp.pad(array, [(0, to - at) for at, to in zip(array.shape, shape, strict=True)])

    heads = w_qkv.reshape(own, 3, n_z, 2, 2, hd).transpose(4, 3, 0, 1, 2, 5).reshape(4, own, packed)
    vectors = jnp.broadcast_to(jnp.concatenate([gains, biases], 1)[None], (4, own, 8))
    pq = grow(jnp.concatenate([heads, vectors], 2), 4, PIECE, qw)
    p1, p2 = (grow(w.reshape(own, 4, f).transpose(1, 0, 2), 4, PIECE, f_pad) for w in (w_fc1, w_fc2))
    po = grow(w_out, PIECE, d)
    tok, cot = grow(tokens[0], BLOCK, d), grow(cotangent[0], BLOCK, d)
    fb = grow(lax.dynamic_slice(fc1_bias.astype(F32), (seq * f,), (f,))[None], 1, f_pad)

    hbm = pl.BlockSpec(memory_space=pl.ANY)
    vmem = pl.BlockSpec(memory_space=pltpu.VMEM)
    outs = [
        ((BLOCK, d), F32, vmem),
        ((BLOCK, d), F32, vmem),
        ((4, PIECE, qw), BF16, hbm),
        ((PIECE, d), BF16, hbm),
        ((4, PIECE, f_pad), BF16, hbm),
        ((4, PIECE, f_pad), BF16, hbm),
        ((16, d), F32, vmem),
        ((32, LANES), F32, vmem),
    ]
    low = [
        (d, qw), (4 * LANES, d), (d, f_pad), (d, f_pad),
        (4, PIECE, qw), (2, PIECE, d), (4, PIECE, f_pad), (4, PIECE, f_pad),
    ]
    scratch = [pltpu.VMEM(shape, BF16) for shape in low]
    scratch += [pltpu.VMEM((160, max(d, f_pad)), F32)]
    scratch += [pltpu.VMEM((rows, w), BF16) for w in (d, d, d, d, f_pad, f_pad)]
    scratch += [pltpu.VMEM((rows, f_pad), F32)]
    scratch += [
        pltpu.VMEM((12, rows, LANES), BF16),
        pltpu.VMEM((rows, 4 * LANES), BF16),
        pltpu.VMEM((4, LANES, rows), BF16),
        pltpu.VMEM((4, rows, LANES), BF16),
        pltpu.VMEM((rows, qw), BF16),
        pltpu.VMEM((4, 1, rows), F32),
    ]
    scratch += [pltpu.VMEM(shape, BF16) for shape in ((d, f_pad), (d, f_pad), (4 * LANES, d), (d, qw))]
    scratch += [pltpu.VMEM((n_z, h, w), BF16) for h, w in ((rb, f_pad), (rb, f_pad), (HEAD_ROWS, d), (rb, qw))]
    scratch += [pltpu.VMEM((n_z - 1, h, w), BF16) for h, w in ((rb, f_pad), (rb, f_pad), (HEAD_ROWS, d), (rb, qw))]
    scratch += [pltpu.VMEM((n, PIECE, w), BF16) for n, w in ((4, f_pad), (4, f_pad), (2, d), (4, qw))]
    for _ in range(2):
        scratch += [pltpu.VMEM((n, BLOCK, d), BF16) for n in (3, 2)] + [pltpu.VMEM((BLOCK, d), BF16)]
    scratch += [
        pltpu.VMEM((2, BLOCK, d), F32),
        pltpu.VMEM((8, d), F32),
        pltpu.VMEM((2, 16, LANES), F32),
        pltpu.VMEM((3, 16, d), F32),
        pltpu.VMEM((7, 16, d), F32),
        pltpu.VMEM((3, 32, LANES), F32),
        pltpu.VMEM((7, 32, LANES), F32),
        pltpu.SemaphoreType.DMA((160,)),
        pltpu.SemaphoreType.DMA((160,)),
        pltpu.SemaphoreType.DMA((8,)),
    ]
    mixed, grad_tokens, gq, go, g1, g2, small, by_head = pl.pallas_call(
        partial(layer_kernel, (slice_len, d, hd, f, qw, n_z)),
        out_shape=[jax.ShapeDtypeStruct(shape, kind) for shape, kind, _ in outs],
        in_specs=[pl.BlockSpec(memory_space=pltpu.SMEM)] + [hbm] * 6 + [vmem],
        out_specs=[spec for _, _, spec in outs],
        scratch_shapes=scratch,
        compiler_params=pltpu.CompilerParams(
            collective_id=0, has_side_effects=True, vmem_limit_bytes=VMEM_BYTES
        ),
    )(offsets, pq, po, p1, p2, tok, cot, fb)

    mixed, grad_tokens = mixed[None, :slice_len], grad_tokens[None, :slice_len]
    grad_qkv = (
        gq[:, :own, :packed]
        .reshape(2, 2, own, 3, n_z, hd)
        .transpose(2, 3, 4, 1, 0, 5)
        .reshape(own, 3 * d)
        .astype(F32)
    )
    grad_out = go[:own].astype(F32)
    grad_fc1, grad_fc2 = (g[:, :own, :f].transpose(1, 0, 2).reshape(own, wide).astype(F32) for g in (g1, g2))
    start = (lax.axis_index("img") * 4 + seq) * own
    mine = lax.dynamic_slice(small[:8], (0, start), (8, own))
    query_value = lax.dynamic_slice(by_head[:, :hd].reshape(2, d), (0, start), (2, own))
    grad_gains = mine[:2].T
    grad_biases = jnp.stack([mine[2], query_value[0], query_value[1], mine[3], mine[4], mine[5]], 1)
    grad_fc1_bias = small[8:12, :f].reshape(wide)
    return mixed, grad_tokens, grad_qkv, grad_out, grad_fc1, grad_fc2, grad_gains, grad_biases, grad_fc1_bias


def local(tokens, offsets, w_qkv, w_out, w_fc1, w_fc2, gains, biases, fc1_bias, cotangent):
    images_here, slice_len, model_width = tokens.shape
    head_count = HEADS
    head_dim = model_width // head_count
    length = slice_len * lax.axis_size("seq")
    row_count = images_here * slice_len
    score_scale = head_dim ** (-0.5)
    gathered = (
        lax.all_gather(w_qkv, ("img", "seq"), axis=0, tiled=True),
        lax.all_gather(w_out, ("img", "seq"), axis=0, tiled=True),
        lax.all_gather(w_fc1, ("img", "seq"), axis=0, tiled=True),
        lax.all_gather(w_fc2, ("img", "seq"), axis=0, tiled=True),
        lax.all_gather(gains, ("img", "seq"), axis=0, tiled=True),
        lax.all_gather(biases, ("img", "seq"), axis=0, tiled=True),
    )
    wide_qkv, wide_out, wide_fc1, wide_fc2, gain_all, bias_all = gathered
    gain_cols = gain_all.astype(jnp.float32)
    bias_cols = bias_all.astype(jnp.float32)
    starts = offsets[:, None]
    positions = lax.axis_index("seq") * slice_len + jnp.arange(slice_len, dtype=jnp.int32)
    own_valid = (positions[None, :] >= starts) & (positions[None, :] < starts + VALID)
    row_valid = own_valid.astype(jnp.float32)
    key_pos = jnp.arange(length, dtype=jnp.int32)
    key_valid = (key_pos[None, :] >= starts) & (key_pos[None, :] < starts + VALID)
    inputs = tokens.astype(jnp.float32).reshape(row_count, model_width)
    h_one, norm_one_back = jax.vjp(layer_norm, inputs, gain_cols[:, 0], bias_cols[:, 0])
    h_one_low = h_one.astype(jnp.bfloat16)
    qkv_bias = jnp.concatenate([bias_cols[:, 1], jnp.zeros_like(bias_cols[:, 1]), bias_cols[:, 2]])
    projected = (
        jnp.dot(h_one_low, wide_qkv, preferred_element_type=jnp.float32) + qkv_bias
    ).astype(jnp.bfloat16)
    query_rows = projected[:, :model_width]
    key_rows = projected[:, model_width : 2 * model_width].reshape(
        images_here, slice_len, model_width
    )
    value_rows = projected[:, 2 * model_width :].reshape(images_here, slice_len, model_width)
    keys_all, values_all = (
        lax.all_gather(key_rows, "seq", axis=1, tiled=True),
        lax.all_gather(value_rows, "seq", axis=1, tiled=True),
    )
    query_heads = split_heads(query_rows, images_here, slice_len, head_count, head_dim)
    key_heads = split_heads(keys_all, images_here, length, head_count, head_dim)
    value_heads = split_heads(values_all, images_here, length, head_count, head_dim)

    def head_scores(head_query_rows, head_key_rows, mask):
        scores = (
            jnp.einsum(
                "asl,aul->asu", head_query_rows, head_key_rows, preferred_element_type=jnp.float32
            )
            * score_scale
        )
        return jnp.where(mask[:, None, :], scores, masked_score)

    def forward_head(head_args):
        head_query_rows, head_key_rows, head_value_rows = head_args
        scores = head_scores(head_query_rows, head_key_rows, key_valid)
        maxima = jnp.max(scores, -1, keepdims=True)
        exponent = jnp.exp(scores - maxima)
        totals_row = jnp.sum(exponent, -1, keepdims=True)
        probs = exponent / totals_row
        attended_head = jnp.einsum(
            "owz,ozf->owf",
            probs.astype(jnp.bfloat16),
            head_value_rows,
            preferred_element_type=jnp.float32,
        )
        return (attended_head, maxima[..., 0] + jnp.log(totals_row[..., 0]))

    attended_heads, log_total = lax.map(forward_head, (query_heads, key_heads, value_heads))
    attended = join_heads(attended_heads).reshape(row_count, model_width).astype(jnp.bfloat16)
    middle = (
        inputs + jnp.dot(attended, wide_out, preferred_element_type=jnp.float32) + bias_cols[:, 3]
    )
    h_two, norm_two_back = jax.vjp(layer_norm, middle, gain_cols[:, 1], bias_cols[:, 4])
    h_two_low = h_two.astype(jnp.bfloat16)
    preact = jnp.dot(h_two_low, wide_fc1, preferred_element_type=jnp.float32) + fc1_bias.astype(
        jnp.float32
    )
    activated, gelu_back = jax.vjp(partial(jax.nn.gelu, approximate=True), preact)
    activated_low = activated.astype(jnp.bfloat16)
    branch_two = last_dot(activated_low, wide_fc2) + bias_cols[:, 5]
    valid_rows = row_valid.reshape(row_count, 1)
    mixed = (valid_rows * (middle + branch_two)).reshape(images_here, slice_len, model_width)
    wide_qkv, wide_out, wide_fc1, wide_fc2 = (
        lax.all_gather(w_qkv, ("img", "seq"), axis=0, tiled=True),
        lax.all_gather(w_out, ("img", "seq"), axis=0, tiled=True),
        lax.all_gather(w_fc1, ("img", "seq"), axis=0, tiled=True),
        lax.all_gather(w_fc2, ("img", "seq"), axis=0, tiled=True),
    )
    grad_output = cotangent.astype(jnp.float32).reshape(row_count, model_width) * valid_rows
    grad_branch = grad_output.astype(jnp.bfloat16)
    grad_bias_two = jnp.sum(grad_branch.astype(jnp.float32), 0)
    grad_fc2_local = row_dot(grad_branch, activated_low)
    grad_activated = jnp.dot(grad_branch, wide_fc2, preferred_element_type=jnp.float32)
    (grad_preact,) = gelu_back(grad_activated)
    preact_low = grad_preact.astype(jnp.bfloat16)
    grad_hidden_bias = jnp.sum(preact_low.astype(jnp.float32), 0)
    grad_fc1_local = row_dot(h_two_low, preact_low)
    grad_h_two = last_dot(preact_low, wide_fc1)
    grad_middle_norm, grad_gain_two, grad_shift_two = norm_two_back(grad_h_two)
    grad_middle = grad_output + grad_middle_norm
    grad_branch_one = grad_middle.astype(jnp.bfloat16)
    grad_out_bias = jnp.sum(grad_branch_one.astype(jnp.float32), 0)
    output_gradient_shard = row_dot(attended, grad_branch_one)
    grad_attended = last_dot(grad_branch_one, wide_out).astype(jnp.bfloat16)
    grad_att_heads = split_heads(grad_attended, images_here, slice_len, head_count, head_dim)

    def backward_head(head_args):
        head_query_rows, head_key_rows, head_value_rows, head_gradient, total_head = head_args
        scores = head_scores(head_query_rows, head_key_rows, key_valid)
        probs = jnp.exp(scores - total_head[..., None])
        grad_probs = jnp.einsum(
            "asl,aul->asu", head_gradient, head_value_rows, preferred_element_type=jnp.float32
        )
        grad_scores = probs * (grad_probs - jnp.sum(probs * grad_probs, -1, keepdims=True))
        reduced_scores = grad_scores.astype(jnp.bfloat16)
        grad_query = (
            jnp.einsum(
                "owz,ozf->owf", reduced_scores, head_key_rows, preferred_element_type=jnp.float32
            )
            * score_scale
        )
        grad_key = (
            jnp.einsum(
                "xzl,xzv->xlv", reduced_scores, head_query_rows, preferred_element_type=jnp.float32
            )
            * score_scale
        )
        grad_value = jnp.einsum(
            "xzl,xzv->xlv",
            probs.astype(jnp.bfloat16),
            head_gradient,
            preferred_element_type=jnp.float32,
        )
        return (grad_query, grad_key, grad_value)

    grad_q_heads, grad_k_heads, grad_v_heads = lax.map(
        backward_head, (query_heads, key_heads, value_heads, grad_att_heads, log_total)
    )
    key_gradient_rows, grad_values = (
        lax.psum_scatter(
            join_heads(grad_k_heads).astype(jnp.bfloat16), "seq", scatter_dimension=1, tiled=True
        ).astype(jnp.float32),
        lax.psum_scatter(
            join_heads(grad_v_heads).astype(jnp.bfloat16), "seq", scatter_dimension=1, tiled=True
        ).astype(jnp.float32),
    )
    grad_projected = jnp.concatenate(
        [
            join_heads(grad_q_heads).reshape(row_count, model_width),
            key_gradient_rows.reshape(row_count, model_width),
            grad_values.reshape(row_count, model_width),
        ],
        1,
    ).astype(jnp.bfloat16)
    grad_query_bias = jnp.sum(grad_projected[:, :model_width].astype(jnp.float32), 0)
    grad_value_bias = jnp.sum(grad_projected[:, 2 * model_width :].astype(jnp.float32), 0)
    grad_qkv_local = row_dot(h_one_low, grad_projected)
    grad_h_one = last_dot(grad_projected, wide_qkv)
    grad_input_norm, grad_gain_one, grad_shift_one = norm_one_back(grad_h_one)
    grad_tokens = (grad_middle + grad_input_norm).reshape(images_here, slice_len, model_width)
    grad_gain_local = jnp.stack([grad_gain_one, grad_gain_two], 1)
    grad_bias_local = jnp.stack(
        [
            grad_shift_one,
            grad_query_bias,
            grad_value_bias,
            grad_out_bias,
            grad_shift_two,
            grad_bias_two,
        ],
        1,
    )
    owned = (
        lax.psum_scatter(grad_qkv_local, ("img", "seq"), scatter_dimension=0, tiled=True),
        lax.psum_scatter(output_gradient_shard, ("img", "seq"), scatter_dimension=0, tiled=True),
        lax.psum_scatter(grad_fc1_local, ("img", "seq"), scatter_dimension=0, tiled=True),
        lax.psum_scatter(grad_fc2_local, ("img", "seq"), scatter_dimension=0, tiled=True),
        lax.psum_scatter(grad_gain_local, ("img", "seq"), scatter_dimension=0, tiled=True),
        lax.psum_scatter(grad_bias_local, ("img", "seq"), scatter_dimension=0, tiled=True),
    )
    hidden_bias_total = lax.psum(grad_hidden_bias, ("img", "seq"))
    return (
        mixed,
        grad_tokens,
        owned[0],
        owned[1],
        owned[2],
        owned[3],
        owned[4],
        owned[5],
        hidden_bias_total,
    )


def solution(mesh):
    in_specs = (
        P("img", "seq", None),
        P("img"),
        P(("img", "seq"), None),
        P(("img", "seq"), None),
        P(("img", "seq"), None),
        P(("img", "seq"), None),
        P(("img", "seq"), None),
        P(("img", "seq"), None),
        P(),
        P("img", "seq", None),
    )
    out_specs = (
        P("img", "seq", None),
        P("img", "seq", None),
        P(("img", "seq"), None),
        P(("img", "seq"), None),
        P(("img", "seq"), None),
        P(("img", "seq"), None),
        P(("img", "seq"), None),
        P(("img", "seq"), None),
        P(),
    )
    shards = mesh.shape["img"] * mesh.shape["seq"]
    fits = mesh.shape["seq"] == 4 and shards == 2 * HEADS
    plan = whole_layer if fits else local
    return jax.shard_map(plan, mesh=mesh, in_specs=in_specs, out_specs=out_specs, check_vma=False)
```

```python
from functools import partial

import jax
import jax.numpy as jnp
from jax import lax
from jax.experimental import pallas as pl
from jax.experimental.pallas import tpu as pltpu
from jax.sharding import PartitionSpec as P

HEADS = 16
VALID = 729


masked_score = -1000000000.0
norm_epsilon = 1e-06


def layer_norm(values, gain_col, bias_col):
    average = jnp.mean(values, -1, keepdims=True)
    centered = values - average
    variance = jnp.mean(centered * centered, -1, keepdims=True)
    return centered * lax.rsqrt(variance + norm_epsilon) * gain_col + bias_col


def row_dot(left, right):
    return lax.dot_general(
        left, right, (((0,), (0,)), ((), ())), preferred_element_type=jnp.float32
    )


def last_dot(left, right):
    return lax.dot_general(
        left, right, (((1,), (1,)), ((), ())), preferred_element_type=jnp.float32
    )


def split_heads(tensor, images_here, count, head_count, head_dim):
    return tensor.reshape(images_here, count, head_count, head_dim).transpose(2, 0, 1, 3)


def join_heads(tensor):
    head_count, images_here, count, head_dim = tensor.shape
    return tensor.transpose(1, 2, 0, 3).reshape(images_here, count, head_count * head_dim)


VMEM_BYTES = 62 * 2**20
MESH_IDS = pl.DeviceIdType.MESH
F32 = jnp.float32
BF16 = jnp.bfloat16
LANES = 128
PIECE = 48
BLOCK = 192
HEAD_ROWS = 80
NN = (((1,), (0,)), ((), ()))
NT = (((1,), (1,)), ((), ()))
TN = (((0,), (0,)), ((), ()))


def mm(left, right, dims):
    return lax.dot_general(left, right, dims, preferred_element_type=F32)


def normalize(values):
    average = jnp.mean(values, -1, keepdims=True)
    centered = values - average
    variance = jnp.mean(centered * centered, -1, keepdims=True)
    inverse = lax.rsqrt(variance + norm_epsilon)
    return centered * inverse, inverse


def norm_back(grad, gain, hat, inverse):
    scaled = grad * gain
    first = jnp.mean(scaled, -1, keepdims=True)
    second = jnp.mean(scaled * hat, -1, keepdims=True)
    return inverse * (scaled - first - hat * second)


def lane_ids(rows):
    return lax.broadcasted_iota(jnp.int32, (rows, LANES), 1)


def lane_window(tiles, start, width, lanes):
    tile, offset = divmod(start, LANES)
    if offset == 0:
        return tiles[tile]
    first = pltpu.roll(tiles[tile], LANES - offset, 1)
    if offset + width <= LANES:
        return first
    second = pltpu.roll(tiles[tile + 1], LANES - offset, 1)
    return jnp.where(lanes < LANES - offset, first, second)


def layer_kernel(
    dims,
    off_ref, pq, po, p1, p2, tok, cot, fb_ref,
    o_mixed, o_gtok, o_fq, o_fo, o_f1, o_f2, o_sm, o_sh,
    wq, wo, w1, w2, rq, ro, r1, r2, tmp,
    xs, gc, h1, h2, act, gp, dg, qkv, attm, att_t, gatt, gpj, lse,
    g1, g2, go, gq, y1, y2, yo, yq, z1, z2, zo, zq,
    sb_a, cr_a, xr_a, sb_b, cr_b, xr_b, pf, prm, bh, sms, smr, shs, shr,
    ssem, rsem, lsem,
):
    slice_len, d, hd, f, qw, n_z = dims
    scale = hd ** (-0.5)
    mask_low = masked_score / scale
    chunk = 256
    rows = 4 * BLOCK
    i, s = lax.axis_index("img"), lax.axis_index("seq")
    z, y = lax.div(i, 2), lax.rem(i, 2)
    x, c = lax.div(s, 2), lax.rem(s, 2)
    k = 2 * c + x
    cy = c == y
    core_peer = (i, x * 2 + 1 - c)
    x_peer = (i, (1 - x) * 2 + c)
    y_peer = (z * 2 + 1 - y, s)
    rb = wq.shape[0] // (2 * n_z)
    own = rb // 4

    def z_at(t):
        return lax.rem(z + t + n_z, n_z)

    def z_dev(t):
        return (z_at(t) * 2 + y, s)

    def z_to(zt):
        return (zt * 2 + y, s)

    near = (
        z,
        jnp.where(z == 0, 1, z - 1),
        jnp.where(z == 0, 2, jnp.where(z == 3, 1, z + 1)),
        jnp.where(z <= 1, 3, 0),
    )
    middle = (z == 1) | (z == 2)
    end = jnp.where(z == 1, 0, 3)

    def s_at(t):
        return lax.rem(s + t + 4, 4)

    count = [0]

    def take(n=1):
        first = count[0]
        count[0] += n
        return first

    def copy(src, dst, index, device, at=None):
        return pltpu.make_async_remote_copy(
            src, dst, ssem.at[index], rsem.at[index if at is None else at], device_id=device, device_id_type=MESH_IDS
        )

    sends = []

    def send(src, dst, index, device, at=None):
        made = copy(src, dst, index, device, at)
        made.start()
        sends.append(made)

    def token_rows(j):
        return pl.ds(pl.multiple_of(j * BLOCK, BLOCK), BLOCK)

    def img_rows(b):
        return pl.ds(pl.multiple_of(b * rb, 16), rb)

    barrier = pltpu.get_barrier_semaphore()
    partners = [(i, s_at(t)) for t in (1, 2, 3)] + [z_dev(t) for t in range(1, n_z)] + [y_peer]
    for partner in partners:
        pl.semaphore_signal(barrier, inc=1, device_id=partner, device_id_type=MESH_IDS)
    pl.semaphore_wait(barrier, len(partners))

    class Gather:
        def __init__(self, piece, recv, full, local_index):
            self.piece, self.recv, self.full = piece, recv, full
            self.width = full.shape[1]
            self.sp, self.sz, self.sy = take(4), take(n_z), take(n_z)
            self.local = local_index

        def pieces(self):
            pltpu.make_async_copy(self.piece.at[s], self.recv.at[s], lsem.at[self.local]).start()
            for t in (1, 2, 3):
                to = s_at(t)
                send(self.piece.at[to], self.recv.at[s], self.sp + t, (i, to))

        def assemble(self):
            pltpu.make_async_copy(self.piece.at[s], self.recv.at[s], lsem.at[self.local]).wait()
            for t in (1, 2, 3):
                came = self.recv.at[s_at(-t)]
                copy(came, came, self.sp + t, (i, s_at(-t))).wait_recv()
            part = rb // 4
            for j in range(4):
                tmp[part * j : part * j + PIECE, 0 : self.width] = self.recv[j].astype(F32)
            self.full[img_rows(i), :] = tmp[0:rb, 0 : self.width].astype(BF16)

        def block(self, zb, side):
            return self.full.at[img_rows(zb * 2 + side)]

        def along_z(self):
            own = self.block(z, y)
            for u in (1, 2):
                send(own, own, self.sz + u, z_to(near[u]), self.sz + z)

            @pl.when(middle)
            def _():
                copy(own, own, self.sz + 3, z_to(near[3]), self.sz + z).start()

        def across_y(self):
            own = self.block(z, y)
            send(own, own, self.sy, y_peer, self.sy + z)

        def forward(self, *steps):
            for u in steps:
                zb = near[u]
                came = self.block(zb, y)
                copy(came, came, self.sz, z_to(zb), self.sz + zb).wait_recv()
                send(came, came, self.sy + u, y_peer, self.sy + zb)
                if u == 3:

                    @pl.when(middle)
                    def _():
                        copy(came, came, self.sz, z_to(end), self.sz + zb).start()

        def finish(self):
            for zb in range(n_z):
                came = self.block(zb, 1 - y)
                copy(came, came, self.sy, y_peer, self.sy + zb).wait_recv()

        def sent(self):
            @pl.when(middle)
            def _():
                own, came = self.block(z, y), self.block(near[3], y)
                copy(own, own, self.sz + 3, z_to(near[3]), self.sz + z).wait_send()
                copy(came, came, self.sz, z_to(end), self.sz + near[3]).wait_send()

    gather_q = Gather(pq, rq, wq, 0)
    gather_1 = Gather(p1, r1, w1, 1)
    gather_2 = Gather(p2, r2, w2, 2)
    o_piece, o_z, o_y = take(), take(n_z), take(n_z)

    def head_block(array, t):
        return array.at[pl.ds(pl.multiple_of(z_at(-t) * LANES, LANES), HEAD_ROWS)]

    def o_start():
        @pl.when(cy)
        def _():
            pltpu.make_async_copy(po, ro.at[c], lsem.at[3]).start()

        @pl.when(jnp.logical_not(cy))
        def _():
            copy(po, ro.at[c], o_piece, core_peer).start()

    def o_assemble():
        for h in range(4):
            wo[h * LANES + HEAD_ROWS : (h + 1) * LANES, :] = jnp.zeros((LANES - HEAD_ROWS, d), BF16)

        @pl.when(cy)
        def _():
            pltpu.make_async_copy(po, ro.at[c], lsem.at[3]).wait()
            copy(po, ro.at[1 - c], o_piece, core_peer).wait_recv()
            for j in range(2):
                tmp[own * j : own * j + PIECE, :] = ro[j].astype(F32)
            wo[pl.ds(pl.multiple_of(z * LANES, LANES), HEAD_ROWS), :] = tmp[0:HEAD_ROWS, :].astype(BF16)

    def o_along_z():
        @pl.when(cy)
        def _():
            mine = head_block(wo, 0)
            for t in range(1, n_z):
                copy(mine, mine, o_z + t, z_dev(t)).start()
            copy(mine, mine, o_y, y_peer).start()

    def o_forward():
        @pl.when(cy)
        def _():
            for t in range(1, n_z):
                came = head_block(wo, t)
                copy(came, came, o_z + t, z_dev(-t)).wait_recv()
                copy(came, came, o_y + t, y_peer).start()

    def o_finish():
        @pl.when(jnp.logical_not(cy))
        def _():
            for t in range(n_z):
                came = head_block(wo, t)
                copy(came, came, o_y + t, y_peer).wait_recv()

    def o_sent():
        @pl.when(jnp.logical_not(cy))
        def _():
            copy(po, ro.at[c], o_piece, core_peer).wait_send()

        @pl.when(cy)
        def _():
            mine = head_block(wo, 0)
            for t in range(1, n_z):
                copy(mine, mine, o_z + t, z_dev(t)).wait_send()
            for t in range(n_z):
                came = head_block(wo, t)
                copy(came, came, o_y + t, y_peer).wait_send()

    class TokenGather:
        def __init__(self, full):
            self.full = full
            self.sx, self.sc, self.sd = take(), take(), take()

        def at(self, j):
            return self.full.at[token_rows(j)]

        def start(self, own):
            self.own = own
            copy(own, self.at(s), self.sx, x_peer).start()
            copy(own, self.at(s), self.sc, core_peer).start()

        def forward(self):
            across = self.at((1 - x) * 2 + c)
            copy(across, across, self.sx, x_peer).wait_recv()
            copy(across, across, self.sd, core_peer).start()

        def finish(self):
            for index, j in ((self.sc, x * 2 + 1 - c), (self.sd, (1 - x) * 2 + 1 - c)):
                copy(self.at(j), self.at(j), index, core_peer).wait_recv()
            copy(self.own, self.at(s), self.sx, x_peer).wait_send()
            copy(self.own, self.at(s), self.sc, core_peer).wait_send()
            across = self.at((1 - x) * 2 + c)
            copy(across, across, self.sd, core_peer).wait_send()

    def seq_sum_start(partial, sb, cr):
        first = take(2)
        last = take()

        def step(t, carry):
            away = t < 2
            j = jnp.where(away, 2 * t + 1 - c, jnp.where(t == 2, 2 * (1 - x) + c, s))
            part = partial(j)

            @pl.when(away)
            def _():
                sb[t] = part.astype(BF16)
                copy(sb.at[t], cr.at[t], first + t, core_peer).start()

            @pl.when(t >= 2)
            def _():
                pf[t - 2] = part

            return carry

        lax.fori_loop(0, 4, step, 0)
        return first, last

    def seq_sum_across(handle, sb, cr, xr):
        first, last = handle
        there = 1 - x
        copy(cr.at[there], cr.at[there], first + there, core_peer).wait_recv()
        sb[2] = (pf[0] + cr[there].astype(F32)).astype(BF16)
        copy(sb.at[2], xr, last, x_peer).start()

    def seq_sum_finish(handle, sb, cr, xr):
        first, last = handle
        copy(cr.at[x], cr.at[x], first + x, core_peer).wait_recv()
        copy(xr, xr, last, x_peer).wait_recv()
        for t in range(2):
            copy(sb.at[t], cr.at[t], first + t, core_peer).wait_send()
        copy(sb.at[2], xr, last, x_peer).wait_send()
        return pf[1] + cr[x].astype(F32) + xr[...].astype(F32)

    class Reduce:
        def __init__(self, grad, yr, zr, fs, out):
            self.grad, self.yr, self.zr, self.fs, self.out = grad, yr, zr, fs, out
            self.width = grad.shape[1]
            self.sy, self.sz, self.sp = take(n_z), take(n_z), take(4)

        def at(self, zb, side):
            return img_rows(zb * 2 + side)

        def across_y(self):
            for u in (3, 2, 1, 0):
                rows_there = self.grad.at[self.at(near[u], 1 - y)]
                send(rows_there, self.yr.at[u], self.sy + u, y_peer)

        def along_z(self, *steps):
            for u in steps:
                copy(self.yr.at[u], self.yr.at[u], self.sy + u, y_peer).wait_recv()
                mine = self.at(near[u], y)
                self.grad[mine, :] = (self.grad[mine, :].astype(F32) + self.yr[u].astype(F32)).astype(BF16)
                if u < 3:
                    send(self.grad.at[mine], self.zr.at[z], self.sz + u, z_to(near[u]), self.sz + z)
                else:

                    @pl.when(jnp.logical_not(middle))
                    def _():
                        self.far().start()

        def far(self):
            rows_far = self.grad.at[self.at(near[3], y)]
            return copy(rows_far, self.zr.at[near[1]], self.sz + 3, z_to(near[1]), self.sz + near[1])

        def onward(self):
            rows_far = self.grad.at[self.at(near[3], y)]
            return copy(rows_far, self.zr.at[z], self.sz + 3, z_to(near[3]), self.sz + z)

        def relay(self):
            @pl.when(middle)
            def _():
                mine = self.at(near[3], y)
                copy(self.zr.at[z], self.zr.at[z], self.sz, z_to(end), self.sz + z).wait_recv()
                self.grad[mine, :] = (self.grad[mine, :].astype(F32) + self.zr[z].astype(F32)).astype(BF16)
                self.onward().start()

        def came_z(self, u):
            zb = near[u]
            copy(self.zr.at[zb], self.zr.at[zb], self.sz, z_to(zb), self.sz + zb).wait_recv()
            tmp[0:rb, 0 : self.width] += self.zr[zb].astype(F32)

        def pieces(self):
            copy(self.yr.at[0], self.yr.at[0], self.sy, y_peer).wait_recv()
            tmp[0:rb, 0 : self.width] = self.grad[self.at(z, y), :].astype(F32) + self.yr[0].astype(F32)
            self.came_z(1)
            self.came_z(2)

            @pl.when(middle)
            def _():
                self.came_z(3)

            part = rb // 4
            for j in range(4):
                self.fs[j] = tmp[part * j : part * j + PIECE, 0 : self.width].astype(BF16)
            pltpu.make_async_copy(self.fs.at[s], self.out.at[s], lsem.at[4]).start()
            for t in (1, 2, 3):
                to = s_at(t)
                send(self.fs.at[to], self.out.at[s], self.sp + t, (i, to))
            pltpu.make_async_copy(self.fs.at[s], self.out.at[s], lsem.at[4]).wait()

        def sent(self):
            @pl.when(middle)
            def _():
                self.onward().wait_send()

            @pl.when(jnp.logical_not(middle))
            def _():
                self.far().wait_send()

        def finish(self):
            for t in (1, 2, 3):
                came = self.out.at[s_at(-t)]
                copy(came, came, self.sp + t, (i, s_at(-t))).wait_recv()

    reduce_2 = Reduce(g2, y2, z2, r2, o_f2)
    reduce_1 = Reduce(g1, y1, z1, r1, o_f1)
    reduce_q = Reduce(gq, yq, zq, rq, o_fq)
    ro_y, ro_z, ro_p = take(n_z), take(n_z), take()

    def ro_across_y():
        @pl.when(jnp.logical_not(cy))
        def _():
            for t in (*range(1, n_z), 0):
                copy(head_block(go, -t), yo.at[t], ro_y + t, y_peer).start()

    def ro_along_z():
        @pl.when(cy)
        def _():
            for t in range(1, n_z):
                copy(yo.at[t], yo.at[t], ro_y + t, y_peer).wait_recv()
                mine = pl.ds(pl.multiple_of(z_at(t) * LANES, LANES), HEAD_ROWS)
                go[mine, :] = (go[mine, :].astype(F32) + yo[t].astype(F32)).astype(BF16)
                copy(go.at[mine], zo.at[t - 1], ro_z + t, z_dev(t)).start()

    def ro_pieces():
        @pl.when(cy)
        def _():
            copy(yo.at[0], yo.at[0], ro_y, y_peer).wait_recv()
            mine = pl.ds(pl.multiple_of(z * LANES, LANES), HEAD_ROWS)
            total = go[mine, :].astype(F32) + yo[0].astype(F32)
            for t in range(1, n_z):
                copy(zo.at[t - 1], zo.at[t - 1], ro_z + t, z_dev(-t)).wait_recv()
                total += zo[t - 1].astype(F32)
            tmp[0:HEAD_ROWS, :] = total
            for j in range(2):
                ro[j] = tmp[own * j : own * j + PIECE, :].astype(BF16)
            pltpu.make_async_copy(ro.at[c], o_fo, lsem.at[5]).start()
            copy(ro.at[1 - c], o_fo, ro_p, core_peer).start()
            pltpu.make_async_copy(ro.at[c], o_fo, lsem.at[5]).wait()

    def ro_finish():
        @pl.when(cy)
        def _():
            for t in range(1, n_z):
                copy(head_block(go, -t), zo.at[t - 1], ro_z + t, z_dev(t)).wait_send()
            copy(ro.at[1 - c], o_fo, ro_p, core_peer).wait_send()

        @pl.when(jnp.logical_not(cy))
        def _():
            for t in range(n_z):
                copy(head_block(go, -t), yo.at[t], ro_y + t, y_peer).wait_send()
            copy(o_fo, o_fo, ro_p, core_peer).wait_recv()

    def real_rows(j, width):
        t = lax.broadcasted_iota(jnp.int32, (BLOCK, width), 0)
        position = j * slice_len + t
        return (t < slice_len) & (position >= off_ref[0]) & (position < off_ref[0] + VALID)

    tokens_in, cot_in = TokenGather(xs), TokenGather(gc)
    gather_q.pieces()
    pltpu.make_async_copy(tok, xs.at[token_rows(s)], lsem.at[6]).start()
    pltpu.make_async_copy(cot, gc.at[token_rows(s)], lsem.at[7]).start()
    tokens_in.start(tok)
    o_start()
    gather_1.pieces()
    gather_2.pieces()
    cot_in.start(cot)
    sms[0] = jnp.zeros(sms.shape[1:], F32)
    shs[0] = jnp.zeros(shs.shape[1:], F32)
    tmp[...] = jnp.zeros(tmp.shape, F32)

    gather_q.assemble()
    gather_q.along_z()
    gather_q.across_y()
    o_assemble()
    tokens_in.forward()
    gather_q.forward(1)
    gather_1.assemble()
    gather_q.forward(2, 3)
    o_along_z()
    gather_1.along_z()
    gather_1.across_y()
    gather_2.assemble()
    gather_2.across_y()
    pltpu.make_async_copy(tok, xs.at[token_rows(s)], lsem.at[6]).wait()
    tokens_in.finish()
    def mask_cotangent(j, carry):
        kept = gc[token_rows(j), :].astype(F32)
        gc[token_rows(j), :] = jnp.where(real_rows(j, d), kept, 0.0).astype(BF16)
        return carry

    gather_q.finish()

    packed = 3 * 4 * hd
    base = packed // LANES * LANES
    columns = wq[:, base : base + LANES].astype(F32)
    prm[...] = columns.T[packed - base : packed - base + 8, :]
    one_lane = lane_ids(1)
    for which, row in ((0, 3), (1, 4)):
        tiles = [prm[row : row + 1, LANES * t : LANES * (t + 1)] for t in range(d // LANES)]
        for head in range(d // hd):
            bh[which, head : head + 1, :] = lane_window(tiles, head * hd, hd, one_lane)
    gain_one, gain_two, shift_one = prm[0:1, :], prm[1:2, :], prm[2:3, :]
    bias_out, shift_two, bias_two = prm[5:6, :], prm[6:7, :], prm[7:8, :]

    lanes = lane_ids(BLOCK)

    def project(j, carry):
        hat, _ = normalize(xs[token_rows(j), :].astype(F32))
        low = (hat * gain_one + shift_one).astype(BF16)
        h1[token_rows(j), :] = low
        wide = mm(low, wq[...], NN)
        tiles = [wide[:, LANES * t : LANES * (t + 1)] for t in range(qw // LANES)]
        key_low = jnp.where(real_rows(j, LANES), 0.0, mask_low)
        for n in range(12):
            kind, head = divmod(n, 4)
            part = lane_window(tiles, n * hd, hd, lanes)
            if kind != 1:
                part = part + bh[kind // 2, pl.ds(4 * head + k, 1), :]
            beside = key_low if kind == 1 else jnp.ones_like(part)
            part = jnp.where(lanes < hd, part, jnp.where(lanes == hd, beside, 0.0))
            qkv[n, token_rows(j), :] = part.astype(BF16)
        return carry

    lax.fori_loop(0, 4, project, 0)
    o_forward()

    sublanes = lax.broadcasted_iota(jnp.int32, (LANES, chunk), 0)

    def attend(step, carry):
        head, part = lax.div(step, rows // chunk), lax.rem(step, rows // chunk)
        at = pl.ds(pl.multiple_of(part * chunk, chunk), chunk)
        scores = mm(qkv[4 + head], qkv[head, at, :], NT)
        top = jnp.max(scores, 0, keepdims=True)
        weights = jnp.exp((scores - top) * scale).astype(BF16)
        summed = mm(qkv[8 + head], weights, TN)
        total = summed[hd : hd + 1, :]
        result = jnp.where(sublanes < hd, summed / total, 0.0)
        att_t[head, :, at] = result.astype(BF16)
        attm[at, pl.ds(pl.multiple_of(head * LANES, LANES), LANES)] = result.T.astype(BF16)
        lse[head, :, at] = top * scale + jnp.log(total)
        return carry

    lax.fori_loop(0, 4 * (rows // chunk), attend, 0)

    gather_1.forward(1)
    cot_in.forward()
    pltpu.make_async_copy(cot, gc.at[token_rows(s)], lsem.at[7]).wait()
    cot_in.finish()
    lax.fori_loop(0, 4, mask_cotangent, 0)

    gather_1.forward(2)
    o_finish()
    sum_one = seq_sum_start(lambda j: mm(attm[token_rows(j), :], wo[...], NN), sb_a, cr_a)
    seq_sum_across(sum_one, sb_a, cr_a, xr_a)
    gather_1.forward(3)
    gather_2.along_z()
    branch = seq_sum_finish(sum_one, sb_a, cr_a, xr_a)
    o_mixed[...] = xs[token_rows(s), :].astype(F32) + branch + bias_out
    hat, _ = normalize(o_mixed[...])
    h2[token_rows(s), :] = (hat * gain_two + shift_two).astype(BF16)
    h2_in = TokenGather(h2)
    h2_in.start(h2.at[token_rows(s)])
    gather_2.forward(1)
    h2_in.forward()
    gather_2.forward(2, 3)
    h2_in.finish()
    gather_1.finish()

    slope = (2.0 / 3.141592653589793) ** 0.5

    def widen(j, carry):
        pre = mm(h2[token_rows(j), :], w1[...], NN) + fb_ref[...]
        square = pre * pre
        curve = jnp.tanh(slope * pre * (1.0 + 0.044715 * square))
        half = 0.5 + 0.5 * curve
        act[token_rows(j), :] = (pre * half).astype(BF16)
        dg[token_rows(j), :] = half + 0.5 * slope * pre * (1.0 - curve * curve) * (1.0 + 0.134145 * square)
        return carry

    lax.fori_loop(0, 4, widen, 0)

    def column_products(left, right, out):
        def step(t, carry):
            at = pl.ds(pl.multiple_of(t * LANES, LANES), LANES)
            out[at, :] = mm(left[:, at], right[...], TN).astype(BF16)
            return carry

        lax.fori_loop(0, left.shape[1] // LANES, step, 0)

    column_products(gc, act, g2)
    reduce_2.across_y()
    gather_2.finish()

    def hidden_back(j):
        at = token_rows(j)
        low = (mm(gc[at, :], w2[...], NN) * dg[at, :]).astype(BF16)
        gp[at, :] = low
        column = jnp.sum(low.astype(F32), 0, keepdims=True)
        sms[0, pl.ds(8 + s, 1), :] += column
        return mm(low, w1[...], NT)

    sum_two = seq_sum_start(hidden_back, sb_a, cr_a)
    seq_sum_across(sum_two, sb_a, cr_a, xr_a)
    column_products(h2, gp, g1)
    reduce_1.across_y()
    reduce_2.along_z(3)
    reduce_2.along_z(2)
    grad_h = seq_sum_finish(sum_two, sb_a, cr_a, xr_a)
    hat, inverse = normalize(o_mixed[...])
    kept = gc[token_rows(s), :].astype(F32)
    grad_x = kept + norm_back(grad_h, gain_two, hat, inverse)
    o_gtok[...] = grad_x
    low = grad_x.astype(BF16)
    sms[0, 1:2, :] = jnp.sum(grad_h * hat, 0, keepdims=True)
    sms[0, 4:5, :] = jnp.sum(grad_h, 0, keepdims=True)
    sms[0, 5:6, :] = jnp.sum(kept, 0, keepdims=True)
    sms[0, 3:4, :] = jnp.sum(low.astype(F32), 0, keepdims=True)
    gc[token_rows(s), :] = low
    gb_in = TokenGather(gc)
    gb_in.start(gc.at[token_rows(s)])

    sum_three = seq_sum_start(lambda j: mm(act[token_rows(j), :], w2[...], NT), sb_b, cr_b)
    seq_sum_across(sum_three, sb_b, cr_b, xr_b)
    reduce_2.along_z(1)
    gb_in.forward()
    gb_in.finish()

    def attended_back(j, carry):
        wide = mm(gc[token_rows(j), :], wo[...], NT).astype(BF16)
        for head in range(4):
            gatt[head, token_rows(j), :] = wide[:, head * LANES : (head + 1) * LANES]
        return carry

    lax.fori_loop(0, 4, attended_back, 0)

    def out_products(head, carry):
        at = pl.ds(pl.multiple_of(head * LANES, LANES), LANES)
        go[at, :] = mm(att_t[head], gc[...], NN).astype(BF16)
        return carry

    lax.fori_loop(0, 4, out_products, 0)
    ro_across_y()
    reduce_2.relay()
    branch = seq_sum_finish(sum_three, sb_b, cr_b, xr_b)
    o_mixed[...] = jnp.where(real_rows(s, d), o_mixed[...] + branch + bias_two, 0.0)

    wide_lanes = lane_ids(rows)
    chunk_lanes = lane_ids(chunk)

    def attend_back(head, carry):
        grad_k = jnp.zeros((rows, LANES), F32)
        grad_v = jnp.zeros((rows, LANES), F32)
        grad_q = []
        for part in range(rows // chunk):
            at = slice(part * chunk, (part + 1) * chunk)
            query, grad_out = qkv[head, at, :], gatt[head, at, :]
            scores = mm(qkv[4 + head], query, NT)
            probs = jnp.exp(scores * scale - lse[head, :, at])
            grad_p = mm(qkv[8 + head], grad_out, NT)
            delta = jnp.sum(probs * grad_p, 0, keepdims=True)
            grad_s = (probs * (grad_p - delta)).astype(BF16)
            grad_k += mm(grad_s, query, NN)
            grad_v += mm(probs.astype(BF16), grad_out, NN)
            grad_q.append(mm(qkv[4 + head], grad_s, TN))
        for part in range(rows // chunk):
            at = slice(part * chunk, (part + 1) * chunk)
            low = jnp.where(chunk_lanes < hd, grad_q[part].T * scale, 0.0).astype(BF16)
            qkv[head, at, :] = low
            shs[0, pl.ds(4 * head + k, 1), :] += jnp.sum(low.astype(F32), 0, keepdims=True)
        qkv[4 + head] = jnp.where(wide_lanes < hd, grad_k * scale, 0.0).astype(BF16)
        low = grad_v.astype(BF16)
        qkv[8 + head] = low
        shs[0, pl.ds(16 + 4 * head + k, 1), :] = jnp.sum(low.astype(F32), 0, keepdims=True)
        return carry

    reduce_1.along_z(3)
    lax.fori_loop(0, 2, attend_back, 0)
    reduce_1.along_z(2)
    lax.fori_loop(2, 4, attend_back, 0)
    reduce_1.along_z(1)
    reduce_1.relay()

    def pack(j, carry):
        tiles = [None] * (qw // LANES)
        for n in range(12):
            tile, offset = divmod(n * hd, LANES)
            part = qkv[n, token_rows(j), :].astype(F32)
            if offset:
                part = pltpu.roll(part, offset, 1)
            ends = [(tile, lanes >= offset)]
            if offset + hd > LANES:
                ends.append((tile + 1, lanes < offset + hd - LANES))
            for to, where in ends:
                kept = jnp.where(where, part, 0.0)
                tiles[to] = kept if tiles[to] is None else tiles[to] + kept
        for to, tile in enumerate(tiles):
            gpj[token_rows(j), LANES * to : LANES * (to + 1)] = tile.astype(BF16)
        return carry

    lax.fori_loop(0, 4, pack, 0)
    column_products(h1, gpj, gq)
    reduce_q.across_y()
    ro_along_z()
    reduce_2.pieces()

    def tokens_back(j):
        part = mm(gpj[token_rows(j), :], wq[...], NT)
        hat, _ = normalize(xs[token_rows(j), :].astype(F32))
        sms[0, 0:1, :] += jnp.sum(part * hat, 0, keepdims=True)
        sms[0, 2:3, :] += jnp.sum(part, 0, keepdims=True)
        return part

    sum_four = seq_sum_start(tokens_back, sb_a, cr_a)
    sm_at, sh_at = take(7), take(7)

    def vectors(stage, slots, devices):
        for slot, device in zip(slots, devices, strict=True):
            send(sms.at[stage], smr.at[slot], sm_at + slot, device)
            send(shs.at[stage], shr.at[slot], sh_at + slot, device)

    def vectors_sum(stage, slots, devices):
        for slot, device in zip(slots, devices, strict=True):
            copy(smr.at[slot], smr.at[slot], sm_at + slot, device).wait_recv()
            copy(shr.at[slot], shr.at[slot], sh_at + slot, device).wait_recv()
        total, heads = sms[stage], shs[stage]
        for slot in slots:
            total += smr[slot]
            heads += shr[slot]
        return total, heads

    vectors(0, (0,), (y_peer,))
    seq_sum_across(sum_four, sb_a, cr_a, xr_a)
    sms[1], shs[1] = vectors_sum(0, (0,), (y_peer,))
    vectors(1, (1, 2, 3), [z_dev(t) for t in (1, 2, 3)])
    reduce_1.pieces()
    reduce_q.along_z(3)
    sms[2], shs[2] = vectors_sum(1, (1, 2, 3), [z_dev(-t) for t in (1, 2, 3)])
    vectors(2, (4, 5, 6), [(i, s_at(t)) for t in (1, 2, 3)])
    grad_h = seq_sum_finish(sum_four, sb_a, cr_a, xr_a)
    hat, inverse = normalize(xs[token_rows(s), :].astype(F32))
    o_gtok[...] += norm_back(grad_h, gain_one, hat, inverse)
    reduce_q.along_z(2, 1)
    reduce_q.relay()
    ro_pieces()
    o_sm[...], o_sh[...] = vectors_sum(2, (4, 5, 6), [(i, s_at(-t)) for t in (1, 2, 3)])
    reduce_q.pieces()
    reduce_2.finish()
    reduce_1.finish()
    ro_finish()
    o_sent()
    reduce_q.finish()
    for part in (gather_q, gather_1, gather_2, reduce_q, reduce_1, reduce_2):
        part.sent()
    for made in sends:
        made.wait_send()


def whole_layer(tokens, offsets, w_qkv, w_out, w_fc1, w_fc2, gains, biases, fc1_bias, cotangent):
    _, slice_len, d = tokens.shape
    hd = d // HEADS
    own, wide = w_fc1.shape
    f = wide // 4
    f_pad = -(-f // LANES) * LANES
    packed = 12 * hd
    qw = -(-(packed + 8) // LANES) * LANES
    n_z = lax.axis_size("img") // 2
    rb = own * 4
    rows = 4 * BLOCK
    seq = lax.axis_index("seq")

    def grow(array, *shape):
        return jnp.pad(array, [(0, to - at) for at, to in zip(array.shape, shape, strict=True)])

    heads = w_qkv.reshape(own, 3, n_z, 2, 2, hd).transpose(4, 3, 0, 1, 2, 5).reshape(4, own, packed)
    vectors = jnp.broadcast_to(jnp.concatenate([gains, biases], 1)[None], (4, own, 8))
    pq = grow(jnp.concatenate([heads, vectors], 2), 4, PIECE, qw)
    p1, p2 = (grow(w.reshape(own, 4, f).transpose(1, 0, 2), 4, PIECE, f_pad) for w in (w_fc1, w_fc2))
    po = grow(w_out, PIECE, d)
    tok, cot = grow(tokens[0], BLOCK, d), grow(cotangent[0], BLOCK, d)
    fb = grow(lax.dynamic_slice(fc1_bias.astype(F32), (seq * f,), (f,))[None], 1, f_pad)

    hbm = pl.BlockSpec(memory_space=pl.ANY)
    vmem = pl.BlockSpec(memory_space=pltpu.VMEM)
    outs = [
        ((BLOCK, d), F32, vmem),
        ((BLOCK, d), F32, vmem),
        ((4, PIECE, qw), BF16, hbm),
        ((PIECE, d), BF16, hbm),
        ((4, PIECE, f_pad), BF16, hbm),
        ((4, PIECE, f_pad), BF16, hbm),
        ((16, d), F32, vmem),
        ((32, LANES), F32, vmem),
    ]
    low = [
        (d, qw), (4 * LANES, d), (d, f_pad), (d, f_pad),
        (4, PIECE, qw), (2, PIECE, d), (4, PIECE, f_pad), (4, PIECE, f_pad),
    ]
    scratch = [pltpu.VMEM(shape, BF16) for shape in low]
    scratch += [pltpu.VMEM((160, max(d, f_pad)), F32)]
    scratch += [pltpu.VMEM((rows, w), BF16) for w in (d, d, d, d, f_pad, f_pad)]
    scratch += [pltpu.VMEM((rows, f_pad), F32)]
    scratch += [
        pltpu.VMEM((12, rows, LANES), BF16),
        pltpu.VMEM((rows, 4 * LANES), BF16),
        pltpu.VMEM((4, LANES, rows), BF16),
        pltpu.VMEM((4, rows, LANES), BF16),
        pltpu.VMEM((rows, qw), BF16),
        pltpu.VMEM((4, 1, rows), F32),
    ]
    scratch += [pltpu.VMEM(shape, BF16) for shape in ((d, f_pad), (d, f_pad), (4 * LANES, d), (d, qw))]
    scratch += [pltpu.VMEM((n_z, h, w), BF16) for h, w in ((rb, f_pad), (rb, f_pad), (HEAD_ROWS, d), (rb, qw))]
    scratch += [pltpu.VMEM((n_z, h, w), BF16) for h, w in ((rb, f_pad), (rb, f_pad), (HEAD_ROWS, d), (rb, qw))]
    for _ in range(2):
        scratch += [pltpu.VMEM((n, BLOCK, d), BF16) for n in (3, 2)] + [pltpu.VMEM((BLOCK, d), BF16)]
    scratch += [
        pltpu.VMEM((2, BLOCK, d), F32),
        pltpu.VMEM((8, d), F32),
        pltpu.VMEM((2, 16, LANES), F32),
        pltpu.VMEM((3, 16, d), F32),
        pltpu.VMEM((7, 16, d), F32),
        pltpu.VMEM((3, 32, LANES), F32),
        pltpu.VMEM((7, 32, LANES), F32),
        pltpu.SemaphoreType.DMA((160,)),
        pltpu.SemaphoreType.DMA((160,)),
        pltpu.SemaphoreType.DMA((8,)),
    ]
    mixed, grad_tokens, gq, go, g1, g2, small, by_head = pl.pallas_call(
        partial(layer_kernel, (slice_len, d, hd, f, qw, n_z)),
        out_shape=[jax.ShapeDtypeStruct(shape, kind) for shape, kind, _ in outs],
        in_specs=[pl.BlockSpec(memory_space=pltpu.SMEM)] + [hbm] * 6 + [vmem],
        out_specs=[spec for _, _, spec in outs],
        scratch_shapes=scratch,
        compiler_params=pltpu.CompilerParams(
            collective_id=0, has_side_effects=True, vmem_limit_bytes=VMEM_BYTES
        ),
    )(offsets, pq, po, p1, p2, tok, cot, fb)

    mixed, grad_tokens = mixed[None, :slice_len], grad_tokens[None, :slice_len]
    grad_qkv = (
        gq[:, :own, :packed]
        .reshape(2, 2, own, 3, n_z, hd)
        .transpose(2, 3, 4, 1, 0, 5)
        .reshape(own, 3 * d)
        .astype(F32)
    )
    grad_out = go[:own].astype(F32)
    grad_fc1, grad_fc2 = (g[:, :own, :f].transpose(1, 0, 2).reshape(own, wide).astype(F32) for g in (g1, g2))
    start = (lax.axis_index("img") * 4 + seq) * own
    mine = lax.dynamic_slice(small[:8], (0, start), (8, own))
    query_value = lax.dynamic_slice(by_head[:, :hd].reshape(2, d), (0, start), (2, own))
    grad_gains = mine[:2].T
    grad_biases = jnp.stack([mine[2], query_value[0], query_value[1], mine[3], mine[4], mine[5]], 1)
    grad_fc1_bias = small[8:12, :f].reshape(wide)
    return mixed, grad_tokens, grad_qkv, grad_out, grad_fc1, grad_fc2, grad_gains, grad_biases, grad_fc1_bias


def local(tokens, offsets, w_qkv, w_out, w_fc1, w_fc2, gains, biases, fc1_bias, cotangent):
    images_here, slice_len, model_width = tokens.shape
    head_count = HEADS
    head_dim = model_width // head_count
    length = slice_len * lax.axis_size("seq")
    row_count = images_here * slice_len
    score_scale = head_dim ** (-0.5)
    gathered = (
        lax.all_gather(w_qkv, ("img", "seq"), axis=0, tiled=True),
        lax.all_gather(w_out, ("img", "seq"), axis=0, tiled=True),
        lax.all_gather(w_fc1, ("img", "seq"), axis=0, tiled=True),
        lax.all_gather(w_fc2, ("img", "seq"), axis=0, tiled=True),
        lax.all_gather(gains, ("img", "seq"), axis=0, tiled=True),
        lax.all_gather(biases, ("img", "seq"), axis=0, tiled=True),
    )
    wide_qkv, wide_out, wide_fc1, wide_fc2, gain_all, bias_all = gathered
    gain_cols = gain_all.astype(jnp.float32)
    bias_cols = bias_all.astype(jnp.float32)
    starts = offsets[:, None]
    positions = lax.axis_index("seq") * slice_len + jnp.arange(slice_len, dtype=jnp.int32)
    own_valid = (positions[None, :] >= starts) & (positions[None, :] < starts + VALID)
    row_valid = own_valid.astype(jnp.float32)
    key_pos = jnp.arange(length, dtype=jnp.int32)
    key_valid = (key_pos[None, :] >= starts) & (key_pos[None, :] < starts + VALID)
    inputs = tokens.astype(jnp.float32).reshape(row_count, model_width)
    h_one, norm_one_back = jax.vjp(layer_norm, inputs, gain_cols[:, 0], bias_cols[:, 0])
    h_one_low = h_one.astype(jnp.bfloat16)
    qkv_bias = jnp.concatenate([bias_cols[:, 1], jnp.zeros_like(bias_cols[:, 1]), bias_cols[:, 2]])
    projected = (
        jnp.dot(h_one_low, wide_qkv, preferred_element_type=jnp.float32) + qkv_bias
    ).astype(jnp.bfloat16)
    query_rows = projected[:, :model_width]
    key_rows = projected[:, model_width : 2 * model_width].reshape(
        images_here, slice_len, model_width
    )
    value_rows = projected[:, 2 * model_width :].reshape(images_here, slice_len, model_width)
    keys_all, values_all = (
        lax.all_gather(key_rows, "seq", axis=1, tiled=True),
        lax.all_gather(value_rows, "seq", axis=1, tiled=True),
    )
    query_heads = split_heads(query_rows, images_here, slice_len, head_count, head_dim)
    key_heads = split_heads(keys_all, images_here, length, head_count, head_dim)
    value_heads = split_heads(values_all, images_here, length, head_count, head_dim)

    def head_scores(head_query_rows, head_key_rows, mask):
        scores = (
            jnp.einsum(
                "asl,aul->asu", head_query_rows, head_key_rows, preferred_element_type=jnp.float32
            )
            * score_scale
        )
        return jnp.where(mask[:, None, :], scores, masked_score)

    def forward_head(head_args):
        head_query_rows, head_key_rows, head_value_rows = head_args
        scores = head_scores(head_query_rows, head_key_rows, key_valid)
        maxima = jnp.max(scores, -1, keepdims=True)
        exponent = jnp.exp(scores - maxima)
        totals_row = jnp.sum(exponent, -1, keepdims=True)
        probs = exponent / totals_row
        attended_head = jnp.einsum(
            "owz,ozf->owf",
            probs.astype(jnp.bfloat16),
            head_value_rows,
            preferred_element_type=jnp.float32,
        )
        return (attended_head, maxima[..., 0] + jnp.log(totals_row[..., 0]))

    attended_heads, log_total = lax.map(forward_head, (query_heads, key_heads, value_heads))
    attended = join_heads(attended_heads).reshape(row_count, model_width).astype(jnp.bfloat16)
    middle = (
        inputs + jnp.dot(attended, wide_out, preferred_element_type=jnp.float32) + bias_cols[:, 3]
    )
    h_two, norm_two_back = jax.vjp(layer_norm, middle, gain_cols[:, 1], bias_cols[:, 4])
    h_two_low = h_two.astype(jnp.bfloat16)
    preact = jnp.dot(h_two_low, wide_fc1, preferred_element_type=jnp.float32) + fc1_bias.astype(
        jnp.float32
    )
    activated, gelu_back = jax.vjp(partial(jax.nn.gelu, approximate=True), preact)
    activated_low = activated.astype(jnp.bfloat16)
    branch_two = last_dot(activated_low, wide_fc2) + bias_cols[:, 5]
    valid_rows = row_valid.reshape(row_count, 1)
    mixed = (valid_rows * (middle + branch_two)).reshape(images_here, slice_len, model_width)
    wide_qkv, wide_out, wide_fc1, wide_fc2 = (
        lax.all_gather(w_qkv, ("img", "seq"), axis=0, tiled=True),
        lax.all_gather(w_out, ("img", "seq"), axis=0, tiled=True),
        lax.all_gather(w_fc1, ("img", "seq"), axis=0, tiled=True),
        lax.all_gather(w_fc2, ("img", "seq"), axis=0, tiled=True),
    )
    grad_output = cotangent.astype(jnp.float32).reshape(row_count, model_width) * valid_rows
    grad_branch = grad_output.astype(jnp.bfloat16)
    grad_bias_two = jnp.sum(grad_branch.astype(jnp.float32), 0)
    grad_fc2_local = row_dot(grad_branch, activated_low)
    grad_activated = jnp.dot(grad_branch, wide_fc2, preferred_element_type=jnp.float32)
    (grad_preact,) = gelu_back(grad_activated)
    preact_low = grad_preact.astype(jnp.bfloat16)
    grad_hidden_bias = jnp.sum(preact_low.astype(jnp.float32), 0)
    grad_fc1_local = row_dot(h_two_low, preact_low)
    grad_h_two = last_dot(preact_low, wide_fc1)
    grad_middle_norm, grad_gain_two, grad_shift_two = norm_two_back(grad_h_two)
    grad_middle = grad_output + grad_middle_norm
    grad_branch_one = grad_middle.astype(jnp.bfloat16)
    grad_out_bias = jnp.sum(grad_branch_one.astype(jnp.float32), 0)
    output_gradient_shard = row_dot(attended, grad_branch_one)
    grad_attended = last_dot(grad_branch_one, wide_out).astype(jnp.bfloat16)
    grad_att_heads = split_heads(grad_attended, images_here, slice_len, head_count, head_dim)

    def backward_head(head_args):
        head_query_rows, head_key_rows, head_value_rows, head_gradient, total_head = head_args
        scores = head_scores(head_query_rows, head_key_rows, key_valid)
        probs = jnp.exp(scores - total_head[..., None])
        grad_probs = jnp.einsum(
            "asl,aul->asu", head_gradient, head_value_rows, preferred_element_type=jnp.float32
        )
        grad_scores = probs * (grad_probs - jnp.sum(probs * grad_probs, -1, keepdims=True))
        reduced_scores = grad_scores.astype(jnp.bfloat16)
        grad_query = (
            jnp.einsum(
                "owz,ozf->owf", reduced_scores, head_key_rows, preferred_element_type=jnp.float32
            )
            * score_scale
        )
        grad_key = (
            jnp.einsum(
                "xzl,xzv->xlv", reduced_scores, head_query_rows, preferred_element_type=jnp.float32
            )
            * score_scale
        )
        grad_value = jnp.einsum(
            "xzl,xzv->xlv",
            probs.astype(jnp.bfloat16),
            head_gradient,
            preferred_element_type=jnp.float32,
        )
        return (grad_query, grad_key, grad_value)

    grad_q_heads, grad_k_heads, grad_v_heads = lax.map(
        backward_head, (query_heads, key_heads, value_heads, grad_att_heads, log_total)
    )
    key_gradient_rows, grad_values = (
        lax.psum_scatter(
            join_heads(grad_k_heads).astype(jnp.bfloat16), "seq", scatter_dimension=1, tiled=True
        ).astype(jnp.float32),
        lax.psum_scatter(
            join_heads(grad_v_heads).astype(jnp.bfloat16), "seq", scatter_dimension=1, tiled=True
        ).astype(jnp.float32),
    )
    grad_projected = jnp.concatenate(
        [
            join_heads(grad_q_heads).reshape(row_count, model_width),
            key_gradient_rows.reshape(row_count, model_width),
            grad_values.reshape(row_count, model_width),
        ],
        1,
    ).astype(jnp.bfloat16)
    grad_query_bias = jnp.sum(grad_projected[:, :model_width].astype(jnp.float32), 0)
    grad_value_bias = jnp.sum(grad_projected[:, 2 * model_width :].astype(jnp.float32), 0)
    grad_qkv_local = row_dot(h_one_low, grad_projected)
    grad_h_one = last_dot(grad_projected, wide_qkv)
    grad_input_norm, grad_gain_one, grad_shift_one = norm_one_back(grad_h_one)
    grad_tokens = (grad_middle + grad_input_norm).reshape(images_here, slice_len, model_width)
    grad_gain_local = jnp.stack([grad_gain_one, grad_gain_two], 1)
    grad_bias_local = jnp.stack(
        [
            grad_shift_one,
            grad_query_bias,
            grad_value_bias,
            grad_out_bias,
            grad_shift_two,
            grad_bias_two,
        ],
        1,
    )
    owned = (
        lax.psum_scatter(grad_qkv_local, ("img", "seq"), scatter_dimension=0, tiled=True),
        lax.psum_scatter(output_gradient_shard, ("img", "seq"), scatter_dimension=0, tiled=True),
        lax.psum_scatter(grad_fc1_local, ("img", "seq"), scatter_dimension=0, tiled=True),
        lax.psum_scatter(grad_fc2_local, ("img", "seq"), scatter_dimension=0, tiled=True),
        lax.psum_scatter(grad_gain_local, ("img", "seq"), scatter_dimension=0, tiled=True),
        lax.psum_scatter(grad_bias_local, ("img", "seq"), scatter_dimension=0, tiled=True),
    )
    hidden_bias_total = lax.psum(grad_hidden_bias, ("img", "seq"))
    return (
        mixed,
        grad_tokens,
        owned[0],
        owned[1],
        owned[2],
        owned[3],
        owned[4],
        owned[5],
        hidden_bias_total,
    )


def solution(mesh):
    in_specs = (
        P("img", "seq", None),
        P("img"),
        P(("img", "seq"), None),
        P(("img", "seq"), None),
        P(("img", "seq"), None),
        P(("img", "seq"), None),
        P(("img", "seq"), None),
        P(("img", "seq"), None),
        P(),
        P("img", "seq", None),
    )
    out_specs = (
        P("img", "seq", None),
        P("img", "seq", None),
        P(("img", "seq"), None),
        P(("img", "seq"), None),
        P(("img", "seq"), None),
        P(("img", "seq"), None),
        P(("img", "seq"), None),
        P(("img", "seq"), None),
        P(),
    )
    shards = mesh.shape["img"] * mesh.shape["seq"]
    fits = mesh.shape["seq"] == 4 and shards == 2 * HEADS
    plan = whole_layer if fits else local
    return jax.shard_map(plan, mesh=mesh, in_specs=in_specs, out_specs=out_specs, check_vma=False)
```

```python
from functools import partial

import jax
import jax.numpy as jnp
from jax import lax
from jax.experimental import pallas as pl
from jax.experimental.pallas import tpu as pltpu
from jax.sharding import PartitionSpec as P

HEADS = 16
VALID = 729


masked_score = -1000000000.0
norm_epsilon = 1e-06


def layer_norm(values, gain_col, bias_col):
    average = jnp.mean(values, -1, keepdims=True)
    centered = values - average
    variance = jnp.mean(centered * centered, -1, keepdims=True)
    return centered * lax.rsqrt(variance + norm_epsilon) * gain_col + bias_col


def row_dot(left, right):
    return lax.dot_general(
        left, right, (((0,), (0,)), ((), ())), preferred_element_type=jnp.float32
    )


def last_dot(left, right):
    return lax.dot_general(
        left, right, (((1,), (1,)), ((), ())), preferred_element_type=jnp.float32
    )


def split_heads(tensor, images_here, count, head_count, head_dim):
    return tensor.reshape(images_here, count, head_count, head_dim).transpose(2, 0, 1, 3)


def join_heads(tensor):
    head_count, images_here, count, head_dim = tensor.shape
    return tensor.transpose(1, 2, 0, 3).reshape(images_here, count, head_count * head_dim)


VMEM_BYTES = 62 * 2**20
MESH_IDS = pl.DeviceIdType.MESH
F32 = jnp.float32
BF16 = jnp.bfloat16
LANES = 128
SLIVER = 16
PIECE = 48
BLOCK = 192
HEAD_ROWS = 80
NN = (((1,), (0,)), ((), ()))
NT = (((1,), (1,)), ((), ()))
TN = (((0,), (0,)), ((), ()))


def mm(left, right, dims):
    return lax.dot_general(left, right, dims, preferred_element_type=F32)


def normalize(values):
    average = jnp.mean(values, -1, keepdims=True)
    centered = values - average
    variance = jnp.mean(centered * centered, -1, keepdims=True)
    inverse = lax.rsqrt(variance + norm_epsilon)
    return centered * inverse, inverse


def norm_back(grad, gain, hat, inverse):
    scaled = grad * gain
    first = jnp.mean(scaled, -1, keepdims=True)
    second = jnp.mean(scaled * hat, -1, keepdims=True)
    return inverse * (scaled - first - hat * second)


def lane_ids(rows):
    return lax.broadcasted_iota(jnp.int32, (rows, LANES), 1)


def lane_window(tiles, start, width, lanes):
    tile, offset = divmod(start, LANES)
    if offset == 0:
        return tiles[tile]
    first = pltpu.roll(tiles[tile], LANES - offset, 1)
    if offset + width <= LANES:
        return first
    second = pltpu.roll(tiles[tile + 1], LANES - offset, 1)
    return jnp.where(lanes < LANES - offset, first, second)


def layer_kernel(
    dims,
    off_ref, pq, po, p1, p2, tok, cot, fb_ref,
    o_mixed, o_gtok, o_fq, o_fo, o_f1, o_f2, o_sm, o_sh,
    wq, wo, w1, w2, rq, ro, r1, r2, tmp,
    xs, gc, h1, h2, act, gp, dg, qkv, attm, att_t, gatt, gpj, lse,
    g1, g2, go, gq, y1, y2, yo, yq, z1, z2, zo, zq, s1, s2,
    sb_a, cr_a, xr_a, sb_b, cr_b, xr_b, pf, prm, bh, sms, smr, shs, shr,
    ssem, rsem, lsem,
):
    slice_len, d, hd, f, qw, n_z = dims
    scale = hd ** (-0.5)
    mask_low = masked_score / scale
    chunk = 256
    rows = 4 * BLOCK
    i, s = lax.axis_index("img"), lax.axis_index("seq")
    z, y = lax.div(i, 2), lax.rem(i, 2)
    x, c = lax.div(s, 2), lax.rem(s, 2)
    k = 2 * c + x
    cy = c == y
    core_peer = (i, x * 2 + 1 - c)
    x_peer = (i, (1 - x) * 2 + c)
    y_peer = (z * 2 + 1 - y, s)
    rb = wq.shape[0] // (2 * n_z)
    own = rb // 4

    def z_at(t):
        return lax.rem(z + t + n_z, n_z)

    def z_dev(t):
        return (z_at(t) * 2 + y, s)

    def z_to(zt):
        return (zt * 2 + y, s)

    near = (
        z,
        jnp.where(z == 0, 1, z - 1),
        jnp.where(z == 0, 2, jnp.where(z == 3, 1, z + 1)),
        jnp.where(z <= 1, 3, 0),
    )
    middle = (z == 1) | (z == 2)
    end = jnp.where(z == 1, 0, 3)

    def s_at(t):
        return lax.rem(s + t + 4, 4)

    count = [0]

    def take(n=1):
        first = count[0]
        count[0] += n
        return first

    def copy(src, dst, index, device, at=None):
        return pltpu.make_async_remote_copy(
            src, dst, ssem.at[index], rsem.at[index if at is None else at], device_id=device, device_id_type=MESH_IDS
        )

    sends = []

    def send(src, dst, index, device, at=None):
        made = copy(src, dst, index, device, at)
        made.start()
        sends.append(made)

    def token_rows(j):
        return pl.ds(pl.multiple_of(j * BLOCK, BLOCK), BLOCK)

    def img_rows(b):
        return pl.ds(pl.multiple_of(b * rb, 16), rb)

    def most_rows(b, most=rb - SLIVER):
        return pl.ds(pl.multiple_of(b * rb, 16), most)

    def sliver_rows(b):
        return pl.ds(pl.multiple_of(b * rb + rb - SLIVER, 16), SLIVER)

    barrier = pltpu.get_barrier_semaphore()
    partners = [(i, s_at(t)) for t in (1, 2, 3)] + [z_dev(t) for t in range(1, n_z)] + [y_peer]
    for partner in partners:
        pl.semaphore_signal(barrier, inc=1, device_id=partner, device_id_type=MESH_IDS)
    pl.semaphore_wait(barrier, len(partners))

    class Gather:
        def __init__(self, piece, recv, full, local_index):
            self.piece, self.recv, self.full = piece, recv, full
            self.width = full.shape[1]
            self.sp, self.sz, self.sy, self.ss = take(4), take(n_z), take(n_z), take(n_z)
            self.local = local_index

        def pieces(self):
            pltpu.make_async_copy(self.piece.at[s], self.recv.at[s], lsem.at[self.local]).start()
            for t in (1, 2, 3):
                to = s_at(t)
                send(self.piece.at[to], self.recv.at[s], self.sp + t, (i, to))

        def assemble(self):
            pltpu.make_async_copy(self.piece.at[s], self.recv.at[s], lsem.at[self.local]).wait()
            for t in (1, 2, 3):
                came = self.recv.at[s_at(-t)]
                copy(came, came, self.sp + t, (i, s_at(-t))).wait_recv()
            part = rb // 4
            for j in range(4):
                tmp[part * j : part * j + PIECE, 0 : self.width] = self.recv[j].astype(F32)
            self.full[img_rows(i), :] = tmp[0:rb, 0 : self.width].astype(BF16)

        def block(self, zb, side):
            return self.full.at[img_rows(zb * 2 + side)]

        def most(self, zb, side):
            return self.full.at[most_rows(zb * 2 + side)]

        def sliver(self, zb, side):
            return self.full.at[sliver_rows(zb * 2 + side)]

        def slivers(self):
            whole, part = self.block(z, 1 - y), self.sliver(z, 1 - y)
            copy(whole, whole, self.sy, y_peer, self.sy + z).wait_recv()
            for u in (1, 2, 3):
                send(part, part, self.ss + u, z_to(near[u]), self.ss + z)

        def along_z(self):
            own = self.block(z, y)
            for u in (1, 2):
                send(own, own, self.sz + u, z_to(near[u]), self.sz + z)

            @pl.when(middle)
            def _():
                copy(own, own, self.sz + 3, z_to(near[3]), self.sz + z).start()

        def across_y(self):
            own = self.block(z, y)
            send(own, own, self.sy, y_peer, self.sy + z)

        def forward(self, *steps):
            for u in steps:
                zb = near[u]
                came = self.block(zb, y)
                copy(came, came, self.sz, z_to(zb), self.sz + zb).wait_recv()
                came = self.most(zb, y)
                copy(came, came, self.sy + u, y_peer, self.sy + zb).start()

        def relay(self):
            @pl.when(middle)
            def _():
                came = self.block(near[3], y)
                copy(came, came, self.sz, z_to(end), self.sz + near[3]).wait_recv()
                copy(came, came, self.sz, z_to(end), self.sz + near[3]).start()
                came = self.most(near[3], y)
                copy(came, came, self.sy + 3, y_peer, self.sy + near[3]).start()

        def forward_far(self):
            @pl.when(jnp.logical_not(middle))
            def _():
                self.forward(3)

        def finish(self):
            for u in (1, 2, 3):
                zb = near[u]
                came = self.most(zb, 1 - y)
                copy(came, came, self.sy, y_peer, self.sy + zb).wait_recv()
                came = self.sliver(zb, 1 - y)
                copy(came, came, self.ss, z_to(zb), self.ss + zb).wait_recv()

        def sent(self):
            @pl.when(middle)
            def _():
                own, came = self.block(z, y), self.block(near[3], y)
                copy(own, own, self.sz + 3, z_to(near[3]), self.sz + z).wait_send()
                copy(came, came, self.sz, z_to(end), self.sz + near[3]).wait_send()

            for u in (1, 2, 3):
                came = self.most(near[u], y)
                copy(came, came, self.sy + u, y_peer, self.sy + near[u]).wait_send()

    gather_q = Gather(pq, rq, wq, 0)
    gather_1 = Gather(p1, r1, w1, 1)
    gather_2 = Gather(p2, r2, w2, 2)
    o_piece, o_z, o_y = take(), take(n_z), take(n_z)

    def head_block(array, t):
        return array.at[pl.ds(pl.multiple_of(z_at(-t) * LANES, LANES), HEAD_ROWS)]

    def o_start():
        @pl.when(cy)
        def _():
            pltpu.make_async_copy(po, ro.at[c], lsem.at[3]).start()

        @pl.when(jnp.logical_not(cy))
        def _():
            copy(po, ro.at[c], o_piece, core_peer).start()

    def o_assemble():
        for h in range(4):
            wo[h * LANES + HEAD_ROWS : (h + 1) * LANES, :] = jnp.zeros((LANES - HEAD_ROWS, d), BF16)

        @pl.when(cy)
        def _():
            pltpu.make_async_copy(po, ro.at[c], lsem.at[3]).wait()
            copy(po, ro.at[1 - c], o_piece, core_peer).wait_recv()
            for j in range(2):
                tmp[own * j : own * j + PIECE, :] = ro[j].astype(F32)
            wo[pl.ds(pl.multiple_of(z * LANES, LANES), HEAD_ROWS), :] = tmp[0:HEAD_ROWS, :].astype(BF16)

    def o_along_z():
        @pl.when(cy)
        def _():
            mine = head_block(wo, 0)
            for t in range(1, n_z):
                copy(mine, mine, o_z + t, z_dev(t)).start()
            copy(mine, mine, o_y, y_peer).start()

    def o_forward():
        @pl.when(cy)
        def _():
            for t in range(1, n_z):
                came = head_block(wo, t)
                copy(came, came, o_z + t, z_dev(-t)).wait_recv()
                copy(came, came, o_y + t, y_peer).start()

    def o_finish():
        @pl.when(jnp.logical_not(cy))
        def _():
            for t in range(n_z):
                came = head_block(wo, t)
                copy(came, came, o_y + t, y_peer).wait_recv()

    def o_sent():
        @pl.when(jnp.logical_not(cy))
        def _():
            copy(po, ro.at[c], o_piece, core_peer).wait_send()

        @pl.when(cy)
        def _():
            mine = head_block(wo, 0)
            for t in range(1, n_z):
                copy(mine, mine, o_z + t, z_dev(t)).wait_send()
            for t in range(n_z):
                came = head_block(wo, t)
                copy(came, came, o_y + t, y_peer).wait_send()

    class TokenGather:
        def __init__(self, full):
            self.full = full
            self.sx, self.sc, self.sd = take(), take(), take()

        def at(self, j):
            return self.full.at[token_rows(j)]

        def start(self, own):
            self.own = own
            copy(own, self.at(s), self.sx, x_peer).start()
            copy(own, self.at(s), self.sc, core_peer).start()

        def forward(self):
            across = self.at((1 - x) * 2 + c)
            copy(across, across, self.sx, x_peer).wait_recv()
            copy(across, across, self.sd, core_peer).start()

        def finish(self):
            for index, j in ((self.sc, x * 2 + 1 - c), (self.sd, (1 - x) * 2 + 1 - c)):
                copy(self.at(j), self.at(j), index, core_peer).wait_recv()
            copy(self.own, self.at(s), self.sx, x_peer).wait_send()
            copy(self.own, self.at(s), self.sc, core_peer).wait_send()
            across = self.at((1 - x) * 2 + c)
            copy(across, across, self.sd, core_peer).wait_send()

    def seq_sum_start(partial, sb, cr):
        first = take(2)
        last = take()

        def step(t, carry):
            away = t < 2
            j = jnp.where(away, 2 * t + 1 - c, jnp.where(t == 2, 2 * (1 - x) + c, s))
            part = partial(j)

            @pl.when(away)
            def _():
                sb[t] = part.astype(BF16)
                copy(sb.at[t], cr.at[t], first + t, core_peer).start()

            @pl.when(t >= 2)
            def _():
                pf[t - 2] = part

            return carry

        lax.fori_loop(0, 4, step, 0)
        return first, last

    def seq_sum_across(handle, sb, cr, xr):
        first, last = handle
        there = 1 - x
        copy(cr.at[there], cr.at[there], first + there, core_peer).wait_recv()
        sb[2] = (pf[0] + cr[there].astype(F32)).astype(BF16)
        copy(sb.at[2], xr, last, x_peer).start()

    def seq_sum_finish(handle, sb, cr, xr):
        first, last = handle
        copy(cr.at[x], cr.at[x], first + x, core_peer).wait_recv()
        copy(xr, xr, last, x_peer).wait_recv()
        for t in range(2):
            copy(sb.at[t], cr.at[t], first + t, core_peer).wait_send()
        copy(sb.at[2], xr, last, x_peer).wait_send()
        return pf[1] + cr[x].astype(F32) + xr[...].astype(F32)

    class Reduce:
        def __init__(self, grad, yr, zr, zs, fs, out):
            self.grad, self.yr, self.zr, self.zs, self.fs, self.out = grad, yr, zr, zs, fs, out
            self.most = rb if zs is None else rb - SLIVER
            self.width = grad.shape[1]
            self.sy, self.sz, self.sp, self.ss = take(n_z), take(n_z), take(4), take(n_z)

        def at(self, zb, side):
            return img_rows(zb * 2 + side)

        def across_y(self):
            for u in (3, 2, 1):
                b = near[u] * 2 + 1 - y
                send(self.grad.at[most_rows(b, self.most)], self.yr.at[u, 0 : self.most], self.sy + u, y_peer)
                if self.zs is not None:
                    send(self.grad.at[sliver_rows(b)], self.zs.at[z], self.ss + u, z_to(near[u]), self.ss + z)
            if self.zs is None:
                send(self.grad.at[img_rows(z * 2 + 1 - y)], self.yr.at[0], self.sy, y_peer)

        def across_last(self):
            b = z * 2 + 1 - y
            part = self.grad[sliver_rows(b), :].astype(F32)
            for u in (1, 2, 3):
                zb = near[u]
                copy(self.zs.at[zb], self.zs.at[zb], self.ss, z_to(zb), self.ss + zb).wait_recv()
                part += self.zs[zb].astype(F32)
            self.grad[sliver_rows(b), :] = part.astype(BF16)
            send(self.grad.at[img_rows(b)], self.yr.at[0], self.sy, y_peer)

        def along_z(self, *steps):
            for u in steps:
                came = self.yr.at[u, 0 : self.most]
                copy(came, came, self.sy + u, y_peer).wait_recv()
                mine, most = self.at(near[u], y), most_rows(near[u] * 2 + y, self.most)
                added = self.yr[u, 0 : self.most, :].astype(F32)
                self.grad[most, :] = (self.grad[most, :].astype(F32) + added).astype(BF16)
                if u < 3:
                    send(self.grad.at[mine], self.zr.at[z], self.sz + u, z_to(near[u]), self.sz + z)
                else:

                    @pl.when(jnp.logical_not(middle))
                    def _():
                        self.far().start()

        def far(self):
            rows_far = self.grad.at[self.at(near[3], y)]
            return copy(rows_far, self.zr.at[near[1]], self.sz + 3, z_to(near[1]), self.sz + near[1])

        def onward(self):
            rows_far = self.grad.at[self.at(near[3], y)]
            return copy(rows_far, self.zr.at[z], self.sz + 3, z_to(near[3]), self.sz + z)

        def relay(self):
            @pl.when(middle)
            def _():
                mine = self.at(near[3], y)
                copy(self.zr.at[z], self.zr.at[z], self.sz, z_to(end), self.sz + z).wait_recv()
                self.grad[mine, :] = (self.grad[mine, :].astype(F32) + self.zr[z].astype(F32)).astype(BF16)
                self.onward().start()

        def came_z(self, u):
            zb = near[u]
            copy(self.zr.at[zb], self.zr.at[zb], self.sz, z_to(zb), self.sz + zb).wait_recv()
            tmp[0:rb, 0 : self.width] += self.zr[zb].astype(F32)

        def pieces(self):
            copy(self.yr.at[0], self.yr.at[0], self.sy, y_peer).wait_recv()
            tmp[0:rb, 0 : self.width] = self.grad[self.at(z, y), :].astype(F32) + self.yr[0].astype(F32)
            self.came_z(1)
            self.came_z(2)

            @pl.when(middle)
            def _():
                self.came_z(3)

            part = rb // 4
            for j in range(4):
                self.fs[j] = tmp[part * j : part * j + PIECE, 0 : self.width].astype(BF16)
            pltpu.make_async_copy(self.fs.at[s], self.out.at[s], lsem.at[4]).start()
            for t in (1, 2, 3):
                to = s_at(t)
                send(self.fs.at[to], self.out.at[s], self.sp + t, (i, to))
            pltpu.make_async_copy(self.fs.at[s], self.out.at[s], lsem.at[4]).wait()

        def sent(self):
            @pl.when(middle)
            def _():
                self.onward().wait_send()

            @pl.when(jnp.logical_not(middle))
            def _():
                self.far().wait_send()

        def finish(self):
            for t in (1, 2, 3):
                came = self.out.at[s_at(-t)]
                copy(came, came, self.sp + t, (i, s_at(-t))).wait_recv()

    reduce_2 = Reduce(g2, y2, z2, s2, r2, o_f2)
    reduce_1 = Reduce(g1, y1, z1, s1, r1, o_f1)
    reduce_q = Reduce(gq, yq, zq, None, rq, o_fq)
    ro_y, ro_z, ro_p = take(n_z), take(n_z), take()

    def ro_across_y():
        @pl.when(jnp.logical_not(cy))
        def _():
            for t in (*range(1, n_z), 0):
                copy(head_block(go, -t), yo.at[t], ro_y + t, y_peer).start()

    def ro_along_z():
        @pl.when(cy)
        def _():
            for t in range(1, n_z):
                copy(yo.at[t], yo.at[t], ro_y + t, y_peer).wait_recv()
                mine = pl.ds(pl.multiple_of(z_at(t) * LANES, LANES), HEAD_ROWS)
                go[mine, :] = (go[mine, :].astype(F32) + yo[t].astype(F32)).astype(BF16)
                copy(go.at[mine], zo.at[t - 1], ro_z + t, z_dev(t)).start()

    def ro_pieces():
        @pl.when(cy)
        def _():
            copy(yo.at[0], yo.at[0], ro_y, y_peer).wait_recv()
            mine = pl.ds(pl.multiple_of(z * LANES, LANES), HEAD_ROWS)
            total = go[mine, :].astype(F32) + yo[0].astype(F32)
            for t in range(1, n_z):
                copy(zo.at[t - 1], zo.at[t - 1], ro_z + t, z_dev(-t)).wait_recv()
                total += zo[t - 1].astype(F32)
            tmp[0:HEAD_ROWS, :] = total
            for j in range(2):
                ro[j] = tmp[own * j : own * j + PIECE, :].astype(BF16)
            pltpu.make_async_copy(ro.at[c], o_fo, lsem.at[5]).start()
            copy(ro.at[1 - c], o_fo, ro_p, core_peer).start()
            pltpu.make_async_copy(ro.at[c], o_fo, lsem.at[5]).wait()

    def ro_finish():
        @pl.when(cy)
        def _():
            for t in range(1, n_z):
                copy(head_block(go, -t), zo.at[t - 1], ro_z + t, z_dev(t)).wait_send()
            copy(ro.at[1 - c], o_fo, ro_p, core_peer).wait_send()

        @pl.when(jnp.logical_not(cy))
        def _():
            for t in range(n_z):
                copy(head_block(go, -t), yo.at[t], ro_y + t, y_peer).wait_send()
            copy(o_fo, o_fo, ro_p, core_peer).wait_recv()

    def real_rows(j, width):
        t = lax.broadcasted_iota(jnp.int32, (BLOCK, width), 0)
        position = j * slice_len + t
        return (t < slice_len) & (position >= off_ref[0]) & (position < off_ref[0] + VALID)

    tokens_in, cot_in = TokenGather(xs), TokenGather(gc)
    gather_q.pieces()
    pltpu.make_async_copy(tok, xs.at[token_rows(s)], lsem.at[6]).start()
    pltpu.make_async_copy(cot, gc.at[token_rows(s)], lsem.at[7]).start()
    tokens_in.start(tok)
    o_start()
    gather_1.pieces()
    gather_2.pieces()
    cot_in.start(cot)
    sms[0] = jnp.zeros(sms.shape[1:], F32)
    shs[0] = jnp.zeros(shs.shape[1:], F32)
    tmp[...] = jnp.zeros(tmp.shape, F32)

    gather_q.assemble()
    gather_q.along_z()
    gather_q.across_y()
    o_assemble()
    o_along_z()
    gather_q.forward(1)
    tokens_in.forward()
    gather_1.assemble()
    gather_q.slivers()
    gather_q.forward(2)
    gather_q.relay()
    gather_1.along_z()
    gather_1.across_y()
    gather_2.assemble()
    gather_q.forward_far()
    o_forward()
    gather_2.across_y()
    cot_in.forward()
    pltpu.make_async_copy(tok, xs.at[token_rows(s)], lsem.at[6]).wait()
    tokens_in.finish()
    def mask_cotangent(j, carry):
        kept = gc[token_rows(j), :].astype(F32)
        gc[token_rows(j), :] = jnp.where(real_rows(j, d), kept, 0.0).astype(BF16)
        return carry

    gather_q.finish()

    packed = 3 * 4 * hd
    base = packed // LANES * LANES
    columns = wq[:, base : base + LANES].astype(F32)
    prm[...] = columns.T[packed - base : packed - base + 8, :]
    one_lane = lane_ids(1)
    for which, row in ((0, 3), (1, 4)):
        tiles = [prm[row : row + 1, LANES * t : LANES * (t + 1)] for t in range(d // LANES)]
        for head in range(d // hd):
            bh[which, head : head + 1, :] = lane_window(tiles, head * hd, hd, one_lane)
    gain_one, gain_two, shift_one = prm[0:1, :], prm[1:2, :], prm[2:3, :]
    bias_out, shift_two, bias_two = prm[5:6, :], prm[6:7, :], prm[7:8, :]

    lanes = lane_ids(BLOCK)

    def project(j, carry):
        hat, _ = normalize(xs[token_rows(j), :].astype(F32))
        low = (hat * gain_one + shift_one).astype(BF16)
        h1[token_rows(j), :] = low
        wide = mm(low, wq[...], NN)
        tiles = [wide[:, LANES * t : LANES * (t + 1)] for t in range(qw // LANES)]
        key_low = jnp.where(real_rows(j, LANES), 0.0, mask_low)
        for n in range(12):
            kind, head = divmod(n, 4)
            part = lane_window(tiles, n * hd, hd, lanes)
            if kind != 1:
                part = part + bh[kind // 2, pl.ds(4 * head + k, 1), :]
            beside = key_low if kind == 1 else jnp.ones_like(part)
            part = jnp.where(lanes < hd, part, jnp.where(lanes == hd, beside, 0.0))
            qkv[n, token_rows(j), :] = part.astype(BF16)
        return carry

    lax.fori_loop(0, 4, project, 0)
    gather_1.slivers()
    gather_2.along_z()
    sublanes = lax.broadcasted_iota(jnp.int32, (LANES, chunk), 0)

    def attend(step, carry):
        head, part = lax.div(step, rows // chunk), lax.rem(step, rows // chunk)
        at = pl.ds(pl.multiple_of(part * chunk, chunk), chunk)
        scores = mm(qkv[4 + head], qkv[head, at, :], NT)
        top = jnp.max(scores, 0, keepdims=True)
        weights = jnp.exp((scores - top) * scale).astype(BF16)
        summed = mm(qkv[8 + head], weights, TN)
        total = summed[hd : hd + 1, :]
        result = jnp.where(sublanes < hd, summed / total, 0.0)
        att_t[head, :, at] = result.astype(BF16)
        attm[at, pl.ds(pl.multiple_of(head * LANES, LANES), LANES)] = result.T.astype(BF16)
        lse[head, :, at] = top * scale + jnp.log(total)
        return carry

    lax.fori_loop(0, 2 * (rows // chunk), attend, 0)
    gather_1.forward(1)
    lax.fori_loop(2 * (rows // chunk), 4 * (rows // chunk), attend, 0)
    gather_1.relay()
    gather_2.slivers()

    pltpu.make_async_copy(cot, gc.at[token_rows(s)], lsem.at[7]).wait()
    cot_in.finish()
    lax.fori_loop(0, 4, mask_cotangent, 0)

    gather_1.forward(2)
    o_finish()
    sum_one = seq_sum_start(lambda j: mm(attm[token_rows(j), :], wo[...], NN), sb_a, cr_a)
    seq_sum_across(sum_one, sb_a, cr_a, xr_a)
    gather_1.forward_far()
    branch = seq_sum_finish(sum_one, sb_a, cr_a, xr_a)
    o_mixed[...] = xs[token_rows(s), :].astype(F32) + branch + bias_out
    hat, _ = normalize(o_mixed[...])
    h2[token_rows(s), :] = (hat * gain_two + shift_two).astype(BF16)
    h2_in = TokenGather(h2)
    h2_in.start(h2.at[token_rows(s)])
    gather_2.forward(1)
    h2_in.forward()
    gather_2.forward(2)
    gather_2.relay()
    h2_in.finish()
    gather_1.finish()

    slope = (2.0 / 3.141592653589793) ** 0.5

    def widen(j, carry):
        pre = mm(h2[token_rows(j), :], w1[...], NN) + fb_ref[...]
        square = pre * pre
        curve = jnp.tanh(slope * pre * (1.0 + 0.044715 * square))
        half = 0.5 + 0.5 * curve
        act[token_rows(j), :] = (pre * half).astype(BF16)
        dg[token_rows(j), :] = half + 0.5 * slope * pre * (1.0 - curve * curve) * (1.0 + 0.134145 * square)
        return carry

    lax.fori_loop(0, 4, widen, 0)
    gather_2.forward_far()

    def column_products(left, right, out):
        def step(t, carry):
            at = pl.ds(pl.multiple_of(t * LANES, LANES), LANES)
            out[at, :] = mm(left[:, at], right[...], TN).astype(BF16)
            return carry

        lax.fori_loop(0, left.shape[1] // LANES, step, 0)

    column_products(gc, act, g2)
    reduce_2.across_y()
    gather_2.finish()

    def hidden_back(j):
        at = token_rows(j)
        low = (mm(gc[at, :], w2[...], NN) * dg[at, :]).astype(BF16)
        gp[at, :] = low
        column = jnp.sum(low.astype(F32), 0, keepdims=True)
        sms[0, pl.ds(8 + s, 1), :] += column
        return mm(low, w1[...], NT)

    sum_two = seq_sum_start(hidden_back, sb_a, cr_a)
    seq_sum_across(sum_two, sb_a, cr_a, xr_a)
    reduce_2.across_last()
    column_products(h2, gp, g1)
    reduce_1.across_y()
    reduce_2.along_z(3)
    reduce_2.along_z(2)
    grad_h = seq_sum_finish(sum_two, sb_a, cr_a, xr_a)
    hat, inverse = normalize(o_mixed[...])
    kept = gc[token_rows(s), :].astype(F32)
    grad_x = kept + norm_back(grad_h, gain_two, hat, inverse)
    o_gtok[...] = grad_x
    low = grad_x.astype(BF16)
    sms[0, 1:2, :] = jnp.sum(grad_h * hat, 0, keepdims=True)
    sms[0, 4:5, :] = jnp.sum(grad_h, 0, keepdims=True)
    sms[0, 5:6, :] = jnp.sum(kept, 0, keepdims=True)
    sms[0, 3:4, :] = jnp.sum(low.astype(F32), 0, keepdims=True)
    gc[token_rows(s), :] = low
    gb_in = TokenGather(gc)
    gb_in.start(gc.at[token_rows(s)])

    sum_three = seq_sum_start(lambda j: mm(act[token_rows(j), :], w2[...], NT), sb_b, cr_b)
    seq_sum_across(sum_three, sb_b, cr_b, xr_b)
    reduce_2.along_z(1)
    reduce_1.across_last()
    gb_in.forward()
    gb_in.finish()

    def attended_back(j, carry):
        wide = mm(gc[token_rows(j), :], wo[...], NT).astype(BF16)
        for head in range(4):
            gatt[head, token_rows(j), :] = wide[:, head * LANES : (head + 1) * LANES]
        return carry

    lax.fori_loop(0, 4, attended_back, 0)

    def out_products(head, carry):
        at = pl.ds(pl.multiple_of(head * LANES, LANES), LANES)
        go[at, :] = mm(att_t[head], gc[...], NN).astype(BF16)
        return carry

    lax.fori_loop(0, 4, out_products, 0)
    ro_across_y()
    reduce_2.relay()
    branch = seq_sum_finish(sum_three, sb_b, cr_b, xr_b)
    o_mixed[...] = jnp.where(real_rows(s, d), o_mixed[...] + branch + bias_two, 0.0)

    wide_lanes = lane_ids(rows)
    chunk_lanes = lane_ids(chunk)

    def attend_back(head, carry):
        grad_k = jnp.zeros((rows, LANES), F32)
        grad_v = jnp.zeros((rows, LANES), F32)
        grad_q = []
        for part in range(rows // chunk):
            at = slice(part * chunk, (part + 1) * chunk)
            query, grad_out = qkv[head, at, :], gatt[head, at, :]
            scores = mm(qkv[4 + head], query, NT)
            probs = jnp.exp(scores * scale - lse[head, :, at])
            grad_p = mm(qkv[8 + head], grad_out, NT)
            delta = jnp.sum(probs * grad_p, 0, keepdims=True)
            grad_s = (probs * (grad_p - delta)).astype(BF16)
            grad_k += mm(grad_s, query, NN)
            grad_v += mm(probs.astype(BF16), grad_out, NN)
            grad_q.append(mm(qkv[4 + head], grad_s, TN))
        for part in range(rows // chunk):
            at = slice(part * chunk, (part + 1) * chunk)
            low = jnp.where(chunk_lanes < hd, grad_q[part].T * scale, 0.0).astype(BF16)
            qkv[head, at, :] = low
            shs[0, pl.ds(4 * head + k, 1), :] += jnp.sum(low.astype(F32), 0, keepdims=True)
        qkv[4 + head] = jnp.where(wide_lanes < hd, grad_k * scale, 0.0).astype(BF16)
        low = grad_v.astype(BF16)
        qkv[8 + head] = low
        shs[0, pl.ds(16 + 4 * head + k, 1), :] = jnp.sum(low.astype(F32), 0, keepdims=True)
        return carry

    reduce_1.along_z(3)
    lax.fori_loop(0, 2, attend_back, 0)
    reduce_1.along_z(2)
    lax.fori_loop(2, 4, attend_back, 0)
    reduce_1.along_z(1)
    reduce_1.relay()

    def pack(j, carry):
        tiles = [None] * (qw // LANES)
        for n in range(12):
            tile, offset = divmod(n * hd, LANES)
            part = qkv[n, token_rows(j), :].astype(F32)
            if offset:
                part = pltpu.roll(part, offset, 1)
            ends = [(tile, lanes >= offset)]
            if offset + hd > LANES:
                ends.append((tile + 1, lanes < offset + hd - LANES))
            for to, where in ends:
                kept = jnp.where(where, part, 0.0)
                tiles[to] = kept if tiles[to] is None else tiles[to] + kept
        for to, tile in enumerate(tiles):
            gpj[token_rows(j), LANES * to : LANES * (to + 1)] = tile.astype(BF16)
        return carry

    lax.fori_loop(0, 4, pack, 0)
    column_products(h1, gpj, gq)
    reduce_q.across_y()
    ro_along_z()
    reduce_2.pieces()

    def tokens_back(j):
        part = mm(gpj[token_rows(j), :], wq[...], NT)
        hat, _ = normalize(xs[token_rows(j), :].astype(F32))
        sms[0, 0:1, :] += jnp.sum(part * hat, 0, keepdims=True)
        sms[0, 2:3, :] += jnp.sum(part, 0, keepdims=True)
        return part

    sum_four = seq_sum_start(tokens_back, sb_a, cr_a)
    sm_at, sh_at = take(7), take(7)

    def vectors(stage, slots, devices):
        for slot, device in zip(slots, devices, strict=True):
            send(sms.at[stage], smr.at[slot], sm_at + slot, device)
            send(shs.at[stage], shr.at[slot], sh_at + slot, device)

    def vectors_sum(stage, slots, devices):
        for slot, device in zip(slots, devices, strict=True):
            copy(smr.at[slot], smr.at[slot], sm_at + slot, device).wait_recv()
            copy(shr.at[slot], shr.at[slot], sh_at + slot, device).wait_recv()
        total, heads = sms[stage], shs[stage]
        for slot in slots:
            total += smr[slot]
            heads += shr[slot]
        return total, heads

    z_to_all, z_from_all = [z_dev(t) for t in (1, 2, 3)], [z_dev(-t) for t in (1, 2, 3)]
    s_to_all, s_from_all = [(i, s_at(t)) for t in (1, 2, 3)], [(i, s_at(-t)) for t in (1, 2, 3)]
    vectors(0, (1, 2, 3), z_to_all)
    seq_sum_across(sum_four, sb_a, cr_a, xr_a)
    reduce_q.along_z(3, 2)
    reduce_q.relay()
    grad_h = seq_sum_finish(sum_four, sb_a, cr_a, xr_a)
    hat, inverse = normalize(xs[token_rows(s), :].astype(F32))
    o_gtok[...] += norm_back(grad_h, gain_one, hat, inverse)
    reduce_q.along_z(1)
    sms[1], shs[1] = vectors_sum(0, (1, 2, 3), z_from_all)
    vectors(1, (4, 5, 6), s_to_all)
    reduce_1.pieces()
    sms[2], shs[2] = vectors_sum(1, (4, 5, 6), s_from_all)
    vectors(2, (0,), (y_peer,))
    ro_pieces()
    reduce_q.pieces()
    o_sm[...], o_sh[...] = vectors_sum(2, (0,), (y_peer,))
    reduce_2.finish()
    reduce_1.finish()
    ro_finish()
    o_sent()
    reduce_q.finish()
    for part in (gather_q, gather_1, gather_2, reduce_q, reduce_1, reduce_2):
        part.sent()
    for made in sends:
        made.wait_send()


def whole_layer(tokens, offsets, w_qkv, w_out, w_fc1, w_fc2, gains, biases, fc1_bias, cotangent):
    _, slice_len, d = tokens.shape
    hd = d // HEADS
    own, wide = w_fc1.shape
    f = wide // 4
    f_pad = -(-f // LANES) * LANES
    packed = 12 * hd
    qw = -(-(packed + 8) // LANES) * LANES
    n_z = lax.axis_size("img") // 2
    rb = own * 4
    rows = 4 * BLOCK
    seq = lax.axis_index("seq")

    def grow(array, *shape):
        return jnp.pad(array, [(0, to - at) for at, to in zip(array.shape, shape, strict=True)])

    heads = w_qkv.reshape(own, 3, n_z, 2, 2, hd).transpose(4, 3, 0, 1, 2, 5).reshape(4, own, packed)
    vectors = jnp.broadcast_to(jnp.concatenate([gains, biases], 1)[None], (4, own, 8))
    pq = grow(jnp.concatenate([heads, vectors], 2), 4, PIECE, qw)
    p1, p2 = (grow(w.reshape(own, 4, f).transpose(1, 0, 2), 4, PIECE, f_pad) for w in (w_fc1, w_fc2))
    po = grow(w_out, PIECE, d)
    tok, cot = grow(tokens[0], BLOCK, d), grow(cotangent[0], BLOCK, d)
    fb = grow(lax.dynamic_slice(fc1_bias.astype(F32), (seq * f,), (f,))[None], 1, f_pad)

    hbm = pl.BlockSpec(memory_space=pl.ANY)
    vmem = pl.BlockSpec(memory_space=pltpu.VMEM)
    outs = [
        ((BLOCK, d), F32, vmem),
        ((BLOCK, d), F32, vmem),
        ((4, PIECE, qw), BF16, hbm),
        ((PIECE, d), BF16, hbm),
        ((4, PIECE, f_pad), BF16, hbm),
        ((4, PIECE, f_pad), BF16, hbm),
        ((16, d), F32, vmem),
        ((32, LANES), F32, vmem),
    ]
    low = [
        (d, qw), (4 * LANES, d), (d, f_pad), (d, f_pad),
        (4, PIECE, qw), (2, PIECE, d), (4, PIECE, f_pad), (4, PIECE, f_pad),
    ]
    scratch = [pltpu.VMEM(shape, BF16) for shape in low]
    scratch += [pltpu.VMEM((160, max(d, f_pad)), F32)]
    scratch += [pltpu.VMEM((rows, w), BF16) for w in (d, d, d, d, f_pad, f_pad)]
    scratch += [pltpu.VMEM((rows, f_pad), F32)]
    scratch += [
        pltpu.VMEM((12, rows, LANES), BF16),
        pltpu.VMEM((rows, 4 * LANES), BF16),
        pltpu.VMEM((4, LANES, rows), BF16),
        pltpu.VMEM((4, rows, LANES), BF16),
        pltpu.VMEM((rows, qw), BF16),
        pltpu.VMEM((4, 1, rows), F32),
    ]
    scratch += [pltpu.VMEM(shape, BF16) for shape in ((d, f_pad), (d, f_pad), (4 * LANES, d), (d, qw))]
    scratch += [pltpu.VMEM((n_z, h, w), BF16) for h, w in ((rb, f_pad), (rb, f_pad), (HEAD_ROWS, d), (rb, qw))]
    scratch += [pltpu.VMEM((n_z, h, w), BF16) for h, w in ((rb, f_pad), (rb, f_pad), (HEAD_ROWS, d), (rb, qw))]
    scratch += [pltpu.VMEM((n_z, SLIVER, w), BF16) for w in (f_pad, f_pad)]
    for _ in range(2):
        scratch += [pltpu.VMEM((n, BLOCK, d), BF16) for n in (3, 2)] + [pltpu.VMEM((BLOCK, d), BF16)]
    scratch += [
        pltpu.VMEM((2, BLOCK, d), F32),
        pltpu.VMEM((8, d), F32),
        pltpu.VMEM((2, 16, LANES), F32),
        pltpu.VMEM((3, 16, d), F32),
        pltpu.VMEM((7, 16, d), F32),
        pltpu.VMEM((3, 32, LANES), F32),
        pltpu.VMEM((7, 32, LANES), F32),
        pltpu.SemaphoreType.DMA((200,)),
        pltpu.SemaphoreType.DMA((200,)),
        pltpu.SemaphoreType.DMA((8,)),
    ]
    mixed, grad_tokens, gq, go, g1, g2, small, by_head = pl.pallas_call(
        partial(layer_kernel, (slice_len, d, hd, f, qw, n_z)),
        out_shape=[jax.ShapeDtypeStruct(shape, kind) for shape, kind, _ in outs],
        in_specs=[pl.BlockSpec(memory_space=pltpu.SMEM)] + [hbm] * 6 + [vmem],
        out_specs=[spec for _, _, spec in outs],
        scratch_shapes=scratch,
        compiler_params=pltpu.CompilerParams(
            collective_id=0, has_side_effects=True, vmem_limit_bytes=VMEM_BYTES
        ),
    )(offsets, pq, po, p1, p2, tok, cot, fb)

    mixed, grad_tokens = mixed[None, :slice_len], grad_tokens[None, :slice_len]
    grad_qkv = (
        gq[:, :own, :packed]
        .reshape(2, 2, own, 3, n_z, hd)
        .transpose(2, 3, 4, 1, 0, 5)
        .reshape(own, 3 * d)
        .astype(F32)
    )
    grad_out = go[:own].astype(F32)
    grad_fc1, grad_fc2 = (g[:, :own, :f].transpose(1, 0, 2).reshape(own, wide).astype(F32) for g in (g1, g2))
    start = (lax.axis_index("img") * 4 + seq) * own
    mine = lax.dynamic_slice(small[:8], (0, start), (8, own))
    query_value = lax.dynamic_slice(by_head[:, :hd].reshape(2, d), (0, start), (2, own))
    grad_gains = mine[:2].T
    grad_biases = jnp.stack([mine[2], query_value[0], query_value[1], mine[3], mine[4], mine[5]], 1)
    grad_fc1_bias = small[8:12, :f].reshape(wide)
    return mixed, grad_tokens, grad_qkv, grad_out, grad_fc1, grad_fc2, grad_gains, grad_biases, grad_fc1_bias


def local(tokens, offsets, w_qkv, w_out, w_fc1, w_fc2, gains, biases, fc1_bias, cotangent):
    images_here, slice_len, model_width = tokens.shape
    head_count = HEADS
    head_dim = model_width // head_count
    length = slice_len * lax.axis_size("seq")
    row_count = images_here * slice_len
    score_scale = head_dim ** (-0.5)
    gathered = (
        lax.all_gather(w_qkv, ("img", "seq"), axis=0, tiled=True),
        lax.all_gather(w_out, ("img", "seq"), axis=0, tiled=True),
        lax.all_gather(w_fc1, ("img", "seq"), axis=0, tiled=True),
        lax.all_gather(w_fc2, ("img", "seq"), axis=0, tiled=True),
        lax.all_gather(gains, ("img", "seq"), axis=0, tiled=True),
        lax.all_gather(biases, ("img", "seq"), axis=0, tiled=True),
    )
    wide_qkv, wide_out, wide_fc1, wide_fc2, gain_all, bias_all = gathered
    gain_cols = gain_all.astype(jnp.float32)
    bias_cols = bias_all.astype(jnp.float32)
    starts = offsets[:, None]
    positions = lax.axis_index("seq") * slice_len + jnp.arange(slice_len, dtype=jnp.int32)
    own_valid = (positions[None, :] >= starts) & (positions[None, :] < starts + VALID)
    row_valid = own_valid.astype(jnp.float32)
    key_pos = jnp.arange(length, dtype=jnp.int32)
    key_valid = (key_pos[None, :] >= starts) & (key_pos[None, :] < starts + VALID)
    inputs = tokens.astype(jnp.float32).reshape(row_count, model_width)
    h_one, norm_one_back = jax.vjp(layer_norm, inputs, gain_cols[:, 0], bias_cols[:, 0])
    h_one_low = h_one.astype(jnp.bfloat16)
    qkv_bias = jnp.concatenate([bias_cols[:, 1], jnp.zeros_like(bias_cols[:, 1]), bias_cols[:, 2]])
    projected = (
        jnp.dot(h_one_low, wide_qkv, preferred_element_type=jnp.float32) + qkv_bias
    ).astype(jnp.bfloat16)
    query_rows = projected[:, :model_width]
    key_rows = projected[:, model_width : 2 * model_width].reshape(
        images_here, slice_len, model_width
    )
    value_rows = projected[:, 2 * model_width :].reshape(images_here, slice_len, model_width)
    keys_all, values_all = (
        lax.all_gather(key_rows, "seq", axis=1, tiled=True),
        lax.all_gather(value_rows, "seq", axis=1, tiled=True),
    )
    query_heads = split_heads(query_rows, images_here, slice_len, head_count, head_dim)
    key_heads = split_heads(keys_all, images_here, length, head_count, head_dim)
    value_heads = split_heads(values_all, images_here, length, head_count, head_dim)

    def head_scores(head_query_rows, head_key_rows, mask):
        scores = (
            jnp.einsum(
                "asl,aul->asu", head_query_rows, head_key_rows, preferred_element_type=jnp.float32
            )
            * score_scale
        )
        return jnp.where(mask[:, None, :], scores, masked_score)

    def forward_head(head_args):
        head_query_rows, head_key_rows, head_value_rows = head_args
        scores = head_scores(head_query_rows, head_key_rows, key_valid)
        maxima = jnp.max(scores, -1, keepdims=True)
        exponent = jnp.exp(scores - maxima)
        totals_row = jnp.sum(exponent, -1, keepdims=True)
        probs = exponent / totals_row
        attended_head = jnp.einsum(
            "owz,ozf->owf",
            probs.astype(jnp.bfloat16),
            head_value_rows,
            preferred_element_type=jnp.float32,
        )
        return (attended_head, maxima[..., 0] + jnp.log(totals_row[..., 0]))

    attended_heads, log_total = lax.map(forward_head, (query_heads, key_heads, value_heads))
    attended = join_heads(attended_heads).reshape(row_count, model_width).astype(jnp.bfloat16)
    middle = (
        inputs + jnp.dot(attended, wide_out, preferred_element_type=jnp.float32) + bias_cols[:, 3]
    )
    h_two, norm_two_back = jax.vjp(layer_norm, middle, gain_cols[:, 1], bias_cols[:, 4])
    h_two_low = h_two.astype(jnp.bfloat16)
    preact = jnp.dot(h_two_low, wide_fc1, preferred_element_type=jnp.float32) + fc1_bias.astype(
        jnp.float32
    )
    activated, gelu_back = jax.vjp(partial(jax.nn.gelu, approximate=True), preact)
    activated_low = activated.astype(jnp.bfloat16)
    branch_two = last_dot(activated_low, wide_fc2) + bias_cols[:, 5]
    valid_rows = row_valid.reshape(row_count, 1)
    mixed = (valid_rows * (middle + branch_two)).reshape(images_here, slice_len, model_width)
    wide_qkv, wide_out, wide_fc1, wide_fc2 = (
        lax.all_gather(w_qkv, ("img", "seq"), axis=0, tiled=True),
        lax.all_gather(w_out, ("img", "seq"), axis=0, tiled=True),
        lax.all_gather(w_fc1, ("img", "seq"), axis=0, tiled=True),
        lax.all_gather(w_fc2, ("img", "seq"), axis=0, tiled=True),
    )
    grad_output = cotangent.astype(jnp.float32).reshape(row_count, model_width) * valid_rows
    grad_branch = grad_output.astype(jnp.bfloat16)
    grad_bias_two = jnp.sum(grad_branch.astype(jnp.float32), 0)
    grad_fc2_local = row_dot(grad_branch, activated_low)
    grad_activated = jnp.dot(grad_branch, wide_fc2, preferred_element_type=jnp.float32)
    (grad_preact,) = gelu_back(grad_activated)
    preact_low = grad_preact.astype(jnp.bfloat16)
    grad_hidden_bias = jnp.sum(preact_low.astype(jnp.float32), 0)
    grad_fc1_local = row_dot(h_two_low, preact_low)
    grad_h_two = last_dot(preact_low, wide_fc1)
    grad_middle_norm, grad_gain_two, grad_shift_two = norm_two_back(grad_h_two)
    grad_middle = grad_output + grad_middle_norm
    grad_branch_one = grad_middle.astype(jnp.bfloat16)
    grad_out_bias = jnp.sum(grad_branch_one.astype(jnp.float32), 0)
    output_gradient_shard = row_dot(attended, grad_branch_one)
    grad_attended = last_dot(grad_branch_one, wide_out).astype(jnp.bfloat16)
    grad_att_heads = split_heads(grad_attended, images_here, slice_len, head_count, head_dim)

    def backward_head(head_args):
        head_query_rows, head_key_rows, head_value_rows, head_gradient, total_head = head_args
        scores = head_scores(head_query_rows, head_key_rows, key_valid)
        probs = jnp.exp(scores - total_head[..., None])
        grad_probs = jnp.einsum(
            "asl,aul->asu", head_gradient, head_value_rows, preferred_element_type=jnp.float32
        )
        grad_scores = probs * (grad_probs - jnp.sum(probs * grad_probs, -1, keepdims=True))
        reduced_scores = grad_scores.astype(jnp.bfloat16)
        grad_query = (
            jnp.einsum(
                "owz,ozf->owf", reduced_scores, head_key_rows, preferred_element_type=jnp.float32
            )
            * score_scale
        )
        grad_key = (
            jnp.einsum(
                "xzl,xzv->xlv", reduced_scores, head_query_rows, preferred_element_type=jnp.float32
            )
            * score_scale
        )
        grad_value = jnp.einsum(
            "xzl,xzv->xlv",
            probs.astype(jnp.bfloat16),
            head_gradient,
            preferred_element_type=jnp.float32,
        )
        return (grad_query, grad_key, grad_value)

    grad_q_heads, grad_k_heads, grad_v_heads = lax.map(
        backward_head, (query_heads, key_heads, value_heads, grad_att_heads, log_total)
    )
    key_gradient_rows, grad_values = (
        lax.psum_scatter(
            join_heads(grad_k_heads).astype(jnp.bfloat16), "seq", scatter_dimension=1, tiled=True
        ).astype(jnp.float32),
        lax.psum_scatter(
            join_heads(grad_v_heads).astype(jnp.bfloat16), "seq", scatter_dimension=1, tiled=True
        ).astype(jnp.float32),
    )
    grad_projected = jnp.concatenate(
        [
            join_heads(grad_q_heads).reshape(row_count, model_width),
            key_gradient_rows.reshape(row_count, model_width),
            grad_values.reshape(row_count, model_width),
        ],
        1,
    ).astype(jnp.bfloat16)
    grad_query_bias = jnp.sum(grad_projected[:, :model_width].astype(jnp.float32), 0)
    grad_value_bias = jnp.sum(grad_projected[:, 2 * model_width :].astype(jnp.float32), 0)
    grad_qkv_local = row_dot(h_one_low, grad_projected)
    grad_h_one = last_dot(grad_projected, wide_qkv)
    grad_input_norm, grad_gain_one, grad_shift_one = norm_one_back(grad_h_one)
    grad_tokens = (grad_middle + grad_input_norm).reshape(images_here, slice_len, model_width)
    grad_gain_local = jnp.stack([grad_gain_one, grad_gain_two], 1)
    grad_bias_local = jnp.stack(
        [
            grad_shift_one,
            grad_query_bias,
            grad_value_bias,
            grad_out_bias,
            grad_shift_two,
            grad_bias_two,
        ],
        1,
    )
    owned = (
        lax.psum_scatter(grad_qkv_local, ("img", "seq"), scatter_dimension=0, tiled=True),
        lax.psum_scatter(output_gradient_shard, ("img", "seq"), scatter_dimension=0, tiled=True),
        lax.psum_scatter(grad_fc1_local, ("img", "seq"), scatter_dimension=0, tiled=True),
        lax.psum_scatter(grad_fc2_local, ("img", "seq"), scatter_dimension=0, tiled=True),
        lax.psum_scatter(grad_gain_local, ("img", "seq"), scatter_dimension=0, tiled=True),
        lax.psum_scatter(grad_bias_local, ("img", "seq"), scatter_dimension=0, tiled=True),
    )
    hidden_bias_total = lax.psum(grad_hidden_bias, ("img", "seq"))
    return (
        mixed,
        grad_tokens,
        owned[0],
        owned[1],
        owned[2],
        owned[3],
        owned[4],
        owned[5],
        hidden_bias_total,
    )


def solution(mesh):
    in_specs = (
        P("img", "seq", None),
        P("img"),
        P(("img", "seq"), None),
        P(("img", "seq"), None),
        P(("img", "seq"), None),
        P(("img", "seq"), None),
        P(("img", "seq"), None),
        P(("img", "seq"), None),
        P(),
        P("img", "seq", None),
    )
    out_specs = (
        P("img", "seq", None),
        P("img", "seq", None),
        P(("img", "seq"), None),
        P(("img", "seq"), None),
        P(("img", "seq"), None),
        P(("img", "seq"), None),
        P(("img", "seq"), None),
        P(("img", "seq"), None),
        P(),
    )
    shards = mesh.shape["img"] * mesh.shape["seq"]
    fits = mesh.shape["seq"] == 4 and shards == 2 * HEADS
    plan = whole_layer if fits else local
    return jax.shard_map(plan, mesh=mesh, in_specs=in_specs, out_specs=out_specs, check_vma=False)
```

```python
from functools import partial

import jax
import jax.numpy as jnp
from jax import lax
from jax.experimental import pallas as pl
from jax.experimental.pallas import tpu as pltpu
from jax.sharding import PartitionSpec as P

HEADS = 16
VALID = 729


masked_score = -1000000000.0
norm_epsilon = 1e-06


def layer_norm(values, gain_col, bias_col):
    average = jnp.mean(values, -1, keepdims=True)
    centered = values - average
    variance = jnp.mean(centered * centered, -1, keepdims=True)
    return centered * lax.rsqrt(variance + norm_epsilon) * gain_col + bias_col


def row_dot(left, right):
    return lax.dot_general(
        left, right, (((0,), (0,)), ((), ())), preferred_element_type=jnp.float32
    )


def last_dot(left, right):
    return lax.dot_general(
        left, right, (((1,), (1,)), ((), ())), preferred_element_type=jnp.float32
    )


def split_heads(tensor, images_here, count, head_count, head_dim):
    return tensor.reshape(images_here, count, head_count, head_dim).transpose(2, 0, 1, 3)


def join_heads(tensor):
    head_count, images_here, count, head_dim = tensor.shape
    return tensor.transpose(1, 2, 0, 3).reshape(images_here, count, head_count * head_dim)


VMEM_BYTES = 63 * 2**20
MESH_IDS = pl.DeviceIdType.MESH
F32 = jnp.float32
BF16 = jnp.bfloat16
LANES = 128
SLIVER = 16
PIECE = 48
BLOCK = 192
HEAD_ROWS = 80
NN = (((1,), (0,)), ((), ()))
NT = (((1,), (1,)), ((), ()))
TN = (((0,), (0,)), ((), ()))


def mm(left, right, dims):
    return lax.dot_general(left, right, dims, preferred_element_type=F32)


def normalize(values):
    average = jnp.mean(values, -1, keepdims=True)
    centered = values - average
    variance = jnp.mean(centered * centered, -1, keepdims=True)
    inverse = lax.rsqrt(variance + norm_epsilon)
    return centered * inverse, inverse


def norm_back(grad, gain, hat, inverse):
    scaled = grad * gain
    first = jnp.mean(scaled, -1, keepdims=True)
    second = jnp.mean(scaled * hat, -1, keepdims=True)
    return inverse * (scaled - first - hat * second)


def lane_ids(rows):
    return lax.broadcasted_iota(jnp.int32, (rows, LANES), 1)


def lane_window(tiles, start, width, lanes):
    tile, offset = divmod(start, LANES)
    if offset == 0:
        return tiles[tile]
    first = pltpu.roll(tiles[tile], LANES - offset, 1)
    if offset + width <= LANES:
        return first
    second = pltpu.roll(tiles[tile + 1], LANES - offset, 1)
    return jnp.where(lanes < LANES - offset, first, second)


def pack_lanes(parts, width, lanes):
    tiles = {}
    for n, part in enumerate(parts):
        tile, offset = divmod(n * width, LANES)
        if offset:
            part = pltpu.roll(part, offset, 1)
        ends = [(tile, lanes >= offset)]
        if offset + width > LANES:
            ends.append((tile + 1, lanes < offset + width - LANES))
        for to, where in ends:
            kept = jnp.where(where, part, 0.0)
            tiles[to] = tiles[to] + kept if to in tiles else kept
    return [tiles[to] for to in sorted(tiles)]


class Tiles:
    def __init__(self, ref, first, step, height):
        self.ref, self.first, self.step, self.height = ref, first, step, height
        self.wide = ref.shape[1] // LANES

    def __getitem__(self, tile):
        part, at = divmod(tile, self.wide)
        row = self.first + part * self.step
        return self.ref[row : row + self.height, at * LANES : (at + 1) * LANES]

    def fill(self, source):
        whole = self.wide * LANES
        rows, wide = source.shape
        for part in range(-(-wide // whole)):
            row = self.first + part * self.step
            width = min(whole, wide - part * whole)
            self.ref[row + rows // 16 * 16 : row + self.height, :] = jnp.zeros(
                (self.height - rows // 16 * 16, whole), F32
            )
            if width < whole:
                last = width // LANES * LANES
                self.ref[row : row + self.height, last : last + LANES] = jnp.zeros((self.height, LANES), F32)
            self.ref[row : row + rows, 0:width] = source[:, part * whole : part * whole + width].astype(F32)


def layer_kernel(
    dims,
    off_ref, w_qkv, w_out, w_fc1, w_fc2, gains, biases, fc1_bias, tok, cot,
    o_mixed, o_gtok, o_q, o_fo, o_1, o_2, o_fb, o_gains, o_biases,
    wq, wo, w1, w2, rq, ro, r1, r2, tmp,
    xs, gc, h1, h2, act, gp, dg, qkv, attm, att_t, lse,
    g1, g2, gq, y1, y2, yo, yq, z1, z2, zo, zq, s1, s2,
    sb_a, cr_a, xr_a, sb_b, cr_b, xr_b, pf, fb, prm, bh, sms, smr, shs, shr,
    ssem, rsem, lsem,
):
    slice_len, d, hd, f, qw, n_z = dims
    scale = hd ** (-0.5)
    mask_low = masked_score / scale
    chunk = 256
    rows = 4 * BLOCK
    i, s = lax.axis_index("img"), lax.axis_index("seq")
    z, y = lax.div(i, 2), lax.rem(i, 2)
    x, c = lax.div(s, 2), lax.rem(s, 2)
    k = 2 * c + x
    cy = c == y
    core_peer = (i, x * 2 + 1 - c)
    x_peer = (i, (1 - x) * 2 + c)
    y_peer = (z * 2 + 1 - y, s)
    rb = wq.shape[0] // (2 * n_z)
    own = rb // 4

    def z_at(t):
        return lax.rem(z + t + n_z, n_z)

    def z_dev(t):
        return (z_at(t) * 2 + y, s)

    def z_to(zt):
        return (zt * 2 + y, s)

    near = (
        z,
        jnp.where(z == 0, 1, z - 1),
        jnp.where(z == 0, 2, jnp.where(z == 3, 1, z + 1)),
        jnp.where(z <= 1, 3, 0),
    )
    middle = (z == 1) | (z == 2)
    end = jnp.where(z == 1, 0, 3)

    def s_at(t):
        return lax.rem(s + t + 4, 4)

    count = [0]

    def take(n=1):
        first = count[0]
        count[0] += n
        return first

    def copy(src, dst, index, device, at=None):
        return pltpu.make_async_remote_copy(
            src, dst, ssem.at[index], rsem.at[index if at is None else at], device_id=device, device_id_type=MESH_IDS
        )

    sends = []

    def send(src, dst, index, device, at=None):
        made = copy(src, dst, index, device, at)
        made.start()
        sends.append(made)

    def token_rows(j):
        return pl.ds(pl.multiple_of(j * BLOCK, BLOCK), BLOCK)

    def img_rows(b):
        return pl.ds(pl.multiple_of(b * rb, 16), rb)

    def most_rows(b, most=rb - SLIVER):
        return pl.ds(pl.multiple_of(b * rb, 16), most)

    def sliver_rows(b):
        return pl.ds(pl.multiple_of(b * rb + rb - SLIVER, 16), SLIVER)

    barrier = pltpu.get_barrier_semaphore()
    partners = [(i, s_at(t)) for t in (1, 2, 3)] + [z_dev(t) for t in range(1, n_z)] + [y_peer]
    for partner in partners:
        pl.semaphore_signal(barrier, inc=1, device_id=partner, device_id_type=MESH_IDS)

    class Gather:
        def __init__(self, piece, recv, full, local_index):
            self.piece, self.recv, self.full = piece, recv, full
            self.width = full.shape[1]
            self.sp, self.sz, self.sy, self.ss = take(4), take(n_z), take(n_z), take(n_z)
            self.local = local_index
            self.started = []

        def pieces(self):
            self.own_piece().start()
            for t in (1, 2, 3):
                self.piece_to(t).start()

        def own_piece(self):
            return pltpu.make_async_copy(self.piece.at[s, 0:PIECE], self.recv.at[s], lsem.at[self.local])

        def piece_to(self, t):
            to = s_at(t)
            return copy(self.piece.at[to, 0:PIECE], self.recv.at[s], self.sp + t, (i, to))

        def assemble(self):
            self.own_piece().wait()
            for t in (1, 2, 3):
                self.piece_to(t).wait_send()
                came = self.recv.at[s_at(-t)]
                copy(came, came, self.sp + t, (i, s_at(-t))).wait_recv()
            part = rb // 4
            for j in range(4):
                tmp[part * j : part * j + PIECE, 0 : self.width] = self.recv[j].astype(F32)
            self.full[img_rows(i), :] = tmp[0:rb, 0 : self.width].astype(BF16)

        def block(self, zb, side):
            return self.full.at[img_rows(zb * 2 + side)]

        def most(self, zb, side):
            return self.full.at[most_rows(zb * 2 + side)]

        def sliver(self, zb, side):
            return self.full.at[sliver_rows(zb * 2 + side)]

        def slivers(self):
            whole, part = self.block(z, 1 - y), self.sliver(z, 1 - y)
            copy(whole, whole, self.sy, y_peer, self.sy + z).wait_recv()
            for u in (1, 2, 3):
                self.send(part, part, self.ss + u, z_to(near[u]), self.ss + z)

        def send(self, src, dst, index, device, at):
            made = copy(src, dst, index, device, at)
            made.start()
            self.started.append(made)

        def along_z(self):
            own = self.block(z, y)
            for u in (1, 2):
                self.send(own, own, self.sz + u, z_to(near[u]), self.sz + z)

            @pl.when(middle)
            def _():
                copy(own, own, self.sz + 3, z_to(near[3]), self.sz + z).start()

        def across_y(self):
            own = self.block(z, y)
            self.send(own, own, self.sy, y_peer, self.sy + z)

        def forward(self, *steps):
            for u in steps:
                zb = near[u]
                came = self.block(zb, y)
                copy(came, came, self.sz, z_to(zb), self.sz + zb).wait_recv()
                came = self.most(zb, y)
                copy(came, came, self.sy + u, y_peer, self.sy + zb).start()

        def relay(self):
            @pl.when(middle)
            def _():
                came = self.block(near[3], y)
                copy(came, came, self.sz, z_to(end), self.sz + near[3]).wait_recv()
                copy(came, came, self.sz, z_to(end), self.sz + near[3]).start()
                came = self.most(near[3], y)
                copy(came, came, self.sy + 3, y_peer, self.sy + near[3]).start()

        def forward_far(self):
            @pl.when(jnp.logical_not(middle))
            def _():
                self.forward(3)

        def finish(self):
            for u in (1, 2, 3):
                zb = near[u]
                came = self.most(zb, 1 - y)
                copy(came, came, self.sy, y_peer, self.sy + zb).wait_recv()
                came = self.sliver(zb, 1 - y)
                copy(came, came, self.ss, z_to(zb), self.ss + zb).wait_recv()

        def sent(self):
            for made in self.started:
                made.wait_send()

            @pl.when(middle)
            def _():
                own, came = self.block(z, y), self.block(near[3], y)
                copy(own, own, self.sz + 3, z_to(near[3]), self.sz + z).wait_send()
                copy(came, came, self.sz, z_to(end), self.sz + near[3]).wait_send()

            for u in (1, 2, 3):
                came = self.most(near[u], y)
                copy(came, came, self.sy + u, y_peer, self.sy + near[u]).wait_send()

    gather_q = Gather(yq, rq, wq, 0)
    gather_1 = Gather(y1, r1, w1, 1)
    gather_2 = Gather(y2, r2, w2, 2)
    o_piece, o_z, o_y = take(), take(n_z), take(n_z)

    def head_block(array, t):
        return array.at[pl.ds(pl.multiple_of(z_at(-t) * LANES, LANES), HEAD_ROWS)]

    po = yo.at[0, 0:PIECE]

    def o_start():
        @pl.when(cy)
        def _():
            pltpu.make_async_copy(po, ro.at[c], lsem.at[3]).start()

        @pl.when(jnp.logical_not(cy))
        def _():
            copy(po, ro.at[c], o_piece, core_peer).start()

    def o_assemble():
        @pl.when(jnp.logical_not(cy))
        def _():
            copy(po, ro.at[c], o_piece, core_peer).wait_send()

        for h in range(4):
            wo[h * LANES + HEAD_ROWS : (h + 1) * LANES, :] = jnp.zeros((LANES - HEAD_ROWS, d), BF16)

        @pl.when(cy)
        def _():
            pltpu.make_async_copy(po, ro.at[c], lsem.at[3]).wait()
            copy(po, ro.at[1 - c], o_piece, core_peer).wait_recv()
            for j in range(2):
                tmp[own * j : own * j + PIECE, :] = ro[j].astype(F32)
            wo[pl.ds(pl.multiple_of(z * LANES, LANES), HEAD_ROWS), :] = tmp[0:HEAD_ROWS, :].astype(BF16)

    def o_along_z():
        @pl.when(cy)
        def _():
            mine = head_block(wo, 0)
            for t in range(1, n_z):
                copy(mine, mine, o_z + t, z_dev(t)).start()
            copy(mine, mine, o_y, y_peer).start()

    def o_forward():
        @pl.when(cy)
        def _():
            for t in range(1, n_z):
                came = head_block(wo, t)
                copy(came, came, o_z + t, z_dev(-t)).wait_recv()
                copy(came, came, o_y + t, y_peer).start()

    def o_finish():
        @pl.when(jnp.logical_not(cy))
        def _():
            for t in range(n_z):
                came = head_block(wo, t)
                copy(came, came, o_y + t, y_peer).wait_recv()

    def o_sent():
        @pl.when(cy)
        def _():
            mine = head_block(wo, 0)
            for t in range(1, n_z):
                copy(mine, mine, o_z + t, z_dev(t)).wait_send()
            for t in range(n_z):
                came = head_block(wo, t)
                copy(came, came, o_y + t, y_peer).wait_send()

    class TokenGather:
        def __init__(self, full):
            self.full = full
            self.sx, self.sc, self.sd = take(), take(), take()

        def at(self, j):
            return self.full.at[token_rows(j)]

        def start(self, own):
            self.own = own
            copy(own, self.at(s), self.sx, x_peer).start()
            copy(own, self.at(s), self.sc, core_peer).start()

        def forward(self):
            across = self.at((1 - x) * 2 + c)
            copy(across, across, self.sx, x_peer).wait_recv()
            copy(across, across, self.sd, core_peer).start()

        def finish(self):
            for index, j in ((self.sc, x * 2 + 1 - c), (self.sd, (1 - x) * 2 + 1 - c)):
                copy(self.at(j), self.at(j), index, core_peer).wait_recv()
            copy(self.own, self.at(s), self.sx, x_peer).wait_send()
            copy(self.own, self.at(s), self.sc, core_peer).wait_send()
            across = self.at((1 - x) * 2 + c)
            copy(across, across, self.sd, core_peer).wait_send()

    def seq_sum_start(partial, sb, cr):
        first = take(2)
        last = take()

        def step(t, carry):
            away = t < 2
            j = jnp.where(away, 2 * t + 1 - c, jnp.where(t == 2, 2 * (1 - x) + c, s))
            part = partial(j)

            @pl.when(away)
            def _():
                sb[t] = part.astype(BF16)
                copy(sb.at[t], cr.at[t], first + t, core_peer).start()

            @pl.when(t >= 2)
            def _():
                pf[t - 2] = part

            return carry

        lax.fori_loop(0, 4, step, 0)
        return first, last

    def seq_sum_across(handle, sb, cr, xr):
        first, last = handle
        there = 1 - x
        copy(cr.at[there], cr.at[there], first + there, core_peer).wait_recv()
        sb[2] = (pf[0] + cr[there].astype(F32)).astype(BF16)
        copy(sb.at[2], xr, last, x_peer).start()

    def seq_sum_finish(handle, sb, cr, xr):
        first, last = handle
        copy(cr.at[x], cr.at[x], first + x, core_peer).wait_recv()
        copy(xr, xr, last, x_peer).wait_recv()
        for t in range(2):
            copy(sb.at[t], cr.at[t], first + t, core_peer).wait_send()
        copy(sb.at[2], xr, last, x_peer).wait_send()
        return pf[1] + cr[x].astype(F32) + xr[...].astype(F32)

    class Reduce:
        def __init__(self, grad, yr, zr, zs, fs, out):
            self.grad, self.yr, self.zr, self.zs, self.fs, self.out = grad, yr, zr, zs, fs, out
            self.most = rb if zs is None else rb - SLIVER
            self.width = grad.shape[1]
            self.sy, self.sz, self.sp, self.ss = take(n_z), take(n_z), take(4), take(n_z)

        def kept(self, j):
            return w1.at[pl.ds(pl.multiple_of(self.out + j * PIECE, 16), PIECE), 0 : self.width]

        def at(self, zb, side):
            return img_rows(zb * 2 + side)

        def across_y(self):
            for u in (3, 2, 1):
                b = near[u] * 2 + 1 - y
                send(self.grad.at[most_rows(b, self.most)], self.yr.at[u, 0 : self.most], self.sy + u, y_peer)
                if self.zs is not None:
                    send(self.grad.at[sliver_rows(b)], self.zs.at[z], self.ss + u, z_to(near[u]), self.ss + z)
            if self.zs is None:
                send(self.grad.at[img_rows(z * 2 + 1 - y)], self.yr.at[0], self.sy, y_peer)

        def across_last(self):
            b = z * 2 + 1 - y
            part = self.grad[sliver_rows(b), :].astype(F32)
            for u in (1, 2, 3):
                zb = near[u]
                copy(self.zs.at[zb], self.zs.at[zb], self.ss, z_to(zb), self.ss + zb).wait_recv()
                part += self.zs[zb].astype(F32)
            self.grad[sliver_rows(b), :] = part.astype(BF16)
            send(self.grad.at[img_rows(b)], self.yr.at[0], self.sy, y_peer)

        def along_z(self, *steps):
            for u in steps:
                came = self.yr.at[u, 0 : self.most]
                copy(came, came, self.sy + u, y_peer).wait_recv()
                mine, most = self.at(near[u], y), most_rows(near[u] * 2 + y, self.most)
                added = self.yr[u, 0 : self.most, :].astype(F32)
                self.grad[most, :] = (self.grad[most, :].astype(F32) + added).astype(BF16)
                if u < 3:
                    send(self.grad.at[mine], self.zr.at[z], self.sz + u, z_to(near[u]), self.sz + z)
                else:

                    @pl.when(jnp.logical_not(middle))
                    def _():
                        self.far().start()

        def far(self):
            rows_far = self.grad.at[self.at(near[3], y)]
            return copy(rows_far, self.zr.at[near[1]], self.sz + 3, z_to(near[1]), self.sz + near[1])

        def onward(self):
            rows_far = self.grad.at[self.at(near[3], y)]
            return copy(rows_far, self.zr.at[z], self.sz + 3, z_to(near[3]), self.sz + z)

        def relay(self):
            @pl.when(middle)
            def _():
                mine = self.at(near[3], y)
                copy(self.zr.at[z], self.zr.at[z], self.sz, z_to(end), self.sz + z).wait_recv()
                self.grad[mine, :] = (self.grad[mine, :].astype(F32) + self.zr[z].astype(F32)).astype(BF16)
                self.onward().start()

        def came_z(self, u):
            zb = near[u]
            copy(self.zr.at[zb], self.zr.at[zb], self.sz, z_to(zb), self.sz + zb).wait_recv()
            tmp[0:rb, 0 : self.width] += self.zr[zb].astype(F32)

        def pieces(self):
            copy(self.yr.at[0], self.yr.at[0], self.sy, y_peer).wait_recv()
            tmp[0:rb, 0 : self.width] = self.grad[self.at(z, y), :].astype(F32) + self.yr[0].astype(F32)
            self.came_z(1)
            self.came_z(2)

            @pl.when(middle)
            def _():
                self.came_z(3)

            part = rb // 4
            for j in range(4):
                self.fs[j] = tmp[part * j : part * j + PIECE, 0 : self.width].astype(BF16)
            pltpu.make_async_copy(self.fs.at[s], self.kept(s), lsem.at[4]).start()
            for t in (1, 2, 3):
                to = s_at(t)
                send(self.fs.at[to], self.kept(s), self.sp + t, (i, to))
            pltpu.make_async_copy(self.fs.at[s], self.kept(s), lsem.at[4]).wait()

        def sent(self):
            @pl.when(middle)
            def _():
                self.onward().wait_send()

            @pl.when(jnp.logical_not(middle))
            def _():
                self.far().wait_send()

        def finish(self):
            for t in (1, 2, 3):
                came = self.kept(s_at(-t))
                copy(came, came, self.sp + t, (i, s_at(-t))).wait_recv()

        def piece_tiles(self, j):
            row = self.out + j * PIECE
            return [
                w1[row : row + PIECE, t * LANES : (t + 1) * LANES].astype(F32) for t in range(self.width // LANES)
            ]

        def publish(self, tiles, out):
            for t, tile in enumerate(tiles):
                width = min(LANES, out.shape[1] - t * LANES)
                out[:, t * LANES : t * LANES + width] = tile[0:own, 0:width]

        def publish_wide(self, out):
            tiles = {}
            for j in range(4):
                tile, offset = divmod(j * f, LANES)
                for t, part in enumerate(self.piece_tiles(j)):
                    if offset:
                        part = pltpu.roll(part, offset, 1)
                    for to, where in ((tile + t, piece_lanes >= offset), (tile + t + 1, piece_lanes < offset)):
                        if to * LANES < 4 * f:
                            kept = jnp.where(where, part, 0.0)
                            tiles[to] = tiles[to] + kept if to in tiles else kept
            self.publish([tiles[to] for to in sorted(tiles)], out)

        def publish_heads(self, out):
            pieces = [self.piece_tiles(j) for j in range(4)]
            tiles = []
            for kind in range(3):
                parts = []
                for head in range(d // hd):
                    which, to = divmod(head, 4)
                    part = lane_window(pieces[2 * (to % 2) + to // 2], (4 * kind + which) * hd, hd, piece_lanes)
                    parts.append(jnp.where(piece_lanes < hd, part, 0.0))
                tiles += pack_lanes(parts, hd, piece_lanes)
            self.publish(tiles, out)

    reduce_2 = Reduce(g2, y2, z2, s2, r2, 0)
    reduce_1 = Reduce(g1, y1, z1, s1, r1, 4 * PIECE)
    reduce_q = Reduce(gq, yq, zq, None, rq, 8 * PIECE)
    go = wo
    ro_y, ro_z, ro_p = take(n_z), take(n_z), take()

    def ro_across_y():
        @pl.when(jnp.logical_not(cy))
        def _():
            for t in (*range(1, n_z), 0):
                copy(head_block(go, -t), yo.at[t], ro_y + t, y_peer).start()

    def ro_along_z():
        @pl.when(cy)
        def _():
            for t in range(1, n_z):
                copy(yo.at[t], yo.at[t], ro_y + t, y_peer).wait_recv()
                mine = pl.ds(pl.multiple_of(z_at(t) * LANES, LANES), HEAD_ROWS)
                go[mine, :] = (go[mine, :].astype(F32) + yo[t].astype(F32)).astype(BF16)
                copy(go.at[mine], zo.at[t - 1], ro_z + t, z_dev(t)).start()

    def ro_pieces():
        @pl.when(cy)
        def _():
            copy(yo.at[0], yo.at[0], ro_y, y_peer).wait_recv()
            mine = pl.ds(pl.multiple_of(z * LANES, LANES), HEAD_ROWS)
            total = go[mine, :].astype(F32) + yo[0].astype(F32)
            for t in range(1, n_z):
                copy(zo.at[t - 1], zo.at[t - 1], ro_z + t, z_dev(-t)).wait_recv()
                total += zo[t - 1].astype(F32)
            tmp[0:HEAD_ROWS, :] = total
            for j in range(2):
                ro[j] = tmp[own * j : own * j + PIECE, :].astype(BF16)
            pltpu.make_async_copy(ro.at[c], o_fo, lsem.at[5]).start()
            copy(ro.at[1 - c], o_fo, ro_p, core_peer).start()
            pltpu.make_async_copy(ro.at[c], o_fo, lsem.at[5]).wait()

    def ro_finish():
        @pl.when(cy)
        def _():
            for t in range(1, n_z):
                copy(head_block(go, -t), zo.at[t - 1], ro_z + t, z_dev(t)).wait_send()
            copy(ro.at[1 - c], o_fo, ro_p, core_peer).wait_send()

        @pl.when(jnp.logical_not(cy))
        def _():
            for t in range(n_z):
                copy(head_block(go, -t), yo.at[t], ro_y + t, y_peer).wait_send()
            copy(o_fo, o_fo, ro_p, core_peer).wait_recv()

    def real_rows(j, width):
        t = lax.broadcasted_iota(jnp.int32, (BLOCK, width), 0)
        position = j * slice_len + t
        return (t < slice_len) & (position >= off_ref[0]) & (position < off_ref[0] + VALID)

    def padded(rows_in):
        pf[0, BLOCK - 16 : BLOCK, :] = jnp.zeros((16, d), F32)
        pf[0, 0:slice_len, :] = rows_in[0]
        return pf[0]

    tokens_in, cot_in = TokenGather(xs), TokenGather(gc)
    piece_lanes = lane_ids(PIECE)
    three = [Tiles(dg, PIECE * n, PIECE, PIECE) for n in range(3)]
    for n in range(3):
        three[n].fill(w_qkv.at[:, n * d : (n + 1) * d])
    small = Tiles(dg, 3 * PIECE, PIECE, PIECE)
    dg[3 * PIECE : 3 * PIECE + LANES, 0:LANES] = jnp.zeros((LANES, LANES), F32)
    dg[3 * PIECE : 3 * PIECE + 2, 0:own] = gains[...].astype(F32)
    dg[3 * PIECE + 2 : 3 * PIECE + 8, 0:own] = biases[...].astype(F32)
    dg[3 * PIECE : 3 * PIECE + LANES, 0:LANES] = dg[3 * PIECE : 3 * PIECE + LANES, 0:LANES].T
    for to in range(4):
        parts = []
        for n in range(12):
            kind, which = divmod(n, 4)
            head = 4 * which + 2 * (to % 2) + to // 2
            part = lane_window(three[kind], head * hd, hd, piece_lanes)
            parts.append(jnp.where(piece_lanes < hd, part, 0.0))
        tiles = pack_lanes(parts, hd, piece_lanes)
        tiles[-1] = tiles[-1] + pltpu.roll(small[0], 12 * hd % LANES, 1)
        for at, tile in enumerate(tiles):
            yq[to, 0:PIECE, at * LANES : (at + 1) * LANES] = tile.astype(BF16)
    pl.semaphore_wait(barrier, len(partners))
    gather_q.pieces()
    pf[0, BLOCK - 16 : BLOCK, :] = jnp.zeros((16, d), F32)
    pf[0, 0:slice_len, :] = tok[0].astype(F32)
    xs[token_rows(s), :] = pf[0].astype(BF16)
    tokens_in.start(xs.at[token_rows(s)])
    out_rows = Tiles(dg, 12 * PIECE, PIECE, PIECE)
    out_rows.fill(w_out)
    for at in range(d // LANES):
        yo[0, 0:PIECE, at * LANES : (at + 1) * LANES] = out_rows[at].astype(BF16)
    o_start()
    for weights, first, pieces in ((w_fc1, 4, y1), (w_fc2, 8, y2)):
        wide = Tiles(dg, first * PIECE, PIECE, PIECE)
        wide.fill(weights)
        for to in range(4):
            for at in range(w1.shape[1] // LANES):
                start = to * f + at * LANES
                width = min(LANES, f - at * LANES)
                part = lane_window(wide, start, width, piece_lanes)
                if width < LANES:
                    part = jnp.where(piece_lanes < width, part, 0.0)
                pieces[to, 0:PIECE, at * LANES : (at + 1) * LANES] = part.astype(BF16)
        (gather_1 if first == 4 else gather_2).pieces()
    pf[1, BLOCK - 16 : BLOCK, :] = jnp.zeros((16, d), F32)
    pf[1, 0:slice_len, :] = cot[0].astype(F32)
    gc[token_rows(s), :] = jnp.where(real_rows(s, d), pf[1], 0.0).astype(BF16)
    cot_in.start(gc.at[token_rows(s)])
    sms[0] = jnp.zeros(sms.shape[1:], F32)
    shs[0] = jnp.zeros(shs.shape[1:], F32)
    tmp[...] = jnp.zeros(tmp.shape, F32)

    gather_q.assemble()
    gather_q.along_z()
    gather_q.across_y()
    o_assemble()
    o_along_z()
    gather_q.forward(1)
    tokens_in.forward()
    gather_1.assemble()
    gather_q.slivers()
    gather_q.forward(2)
    gather_q.relay()
    gather_1.along_z()
    gather_1.across_y()
    gather_2.assemble()
    gather_q.forward_far()
    o_forward()
    gather_2.across_y()
    cot_in.forward()
    tokens_in.finish()
    gather_q.finish()

    packed = 3 * 4 * hd
    base = packed // LANES * LANES
    columns = wq[:, base : base + LANES].astype(F32)
    prm[...] = columns.T[packed - base : packed - base + 8, :]
    one_lane = lane_ids(1)
    for which, row in ((0, 3), (1, 4)):
        tiles = [prm[row : row + 1, LANES * t : LANES * (t + 1)] for t in range(d // LANES)]
        for head in range(d // hd):
            bh[which, head : head + 1, :] = lane_window(tiles, head * hd, hd, one_lane)
    gain_one, gain_two, shift_one = prm[0:1, :], prm[1:2, :], prm[2:3, :]
    bias_out, shift_two, bias_two = prm[5:6, :], prm[6:7, :], prm[7:8, :]

    lanes = lane_ids(BLOCK)

    def project(j, carry):
        hat, _ = normalize(xs[token_rows(j), :].astype(F32))
        low = (hat * gain_one + shift_one).astype(BF16)
        h1[token_rows(j), :] = low
        wide = mm(low, wq[...], NN)
        tiles = [wide[:, LANES * t : LANES * (t + 1)] for t in range(qw // LANES)]
        key_low = jnp.where(real_rows(j, LANES), 0.0, mask_low)
        for n in range(12):
            kind, head = divmod(n, 4)
            part = lane_window(tiles, n * hd, hd, lanes)
            if kind != 1:
                part = part + bh[kind // 2, pl.ds(4 * head + k, 1), :]
            beside = key_low if kind == 1 else jnp.ones_like(part)
            part = jnp.where(lanes < hd, part, jnp.where(lanes == hd, beside, 0.0))
            qkv[n, token_rows(j), :] = part.astype(BF16)
        return carry

    lax.fori_loop(0, 4, project, 0)
    gather_1.slivers()
    gather_2.along_z()
    sublanes = lax.broadcasted_iota(jnp.int32, (LANES, chunk), 0)

    def attend(step, carry):
        head, part = lax.div(step, rows // chunk), lax.rem(step, rows // chunk)
        at = pl.ds(pl.multiple_of(part * chunk, chunk), chunk)
        scores = mm(qkv[4 + head], qkv[head, at, :], NT)
        top = jnp.max(scores, 0, keepdims=True)
        weights = jnp.exp((scores - top) * scale).astype(BF16)
        summed = mm(qkv[8 + head], weights, TN)
        total = summed[hd : hd + 1, :]
        result = jnp.where(sublanes < hd, summed / total, 0.0)
        att_t[head, :, at] = result.astype(BF16)
        attm[at, pl.ds(pl.multiple_of(head * LANES, LANES), LANES)] = result.T.astype(BF16)
        lse[head, :, at] = top * scale + jnp.log(total)
        return carry

    lax.fori_loop(0, 2 * (rows // chunk), attend, 0)
    gather_1.forward(1)
    lax.fori_loop(2 * (rows // chunk), 4 * (rows // chunk), attend, 0)
    gather_1.relay()
    gather_2.slivers()

    cot_in.finish()
    bias_parts = Tiles(dg, 14 * PIECE, 8, 8)
    bias_parts.fill(fc1_bias)
    row_lanes = lane_ids(8)
    for at in range(w1.shape[1] // LANES):
        width = min(LANES, f - at * LANES)
        mine = jnp.zeros((8, LANES), F32)
        for to in range(4):
            part = lane_window(bias_parts, to * f + at * LANES, width, row_lanes)
            mine = jnp.where(s == to, part, mine)
        fb[:, at * LANES : (at + 1) * LANES] = jnp.where(row_lanes < width, mine, 0.0)[0:1]

    gather_1.forward(2)
    o_finish()
    sum_one = seq_sum_start(lambda j: mm(attm[token_rows(j), :], wo[...], NN), sb_a, cr_a)
    seq_sum_across(sum_one, sb_a, cr_a, xr_a)
    gather_1.forward_far()
    branch = seq_sum_finish(sum_one, sb_a, cr_a, xr_a)
    middle_rows = xs[token_rows(s), :].astype(F32) + branch + bias_out
    o_mixed[0] = middle_rows[0:slice_len]
    hat, _ = normalize(middle_rows)
    h2[token_rows(s), :] = (hat * gain_two + shift_two).astype(BF16)
    h2_in = TokenGather(h2)
    h2_in.start(h2.at[token_rows(s)])
    gather_2.forward(1)
    h2_in.forward()
    gather_2.forward(2)
    gather_2.relay()
    h2_in.finish()
    gather_1.finish()

    slope = (2.0 / 3.141592653589793) ** 0.5

    def widen(j, carry):
        pre = mm(h2[token_rows(j), :], w1[...], NN) + fb[...]
        square = pre * pre
        curve = jnp.tanh(slope * pre * (1.0 + 0.044715 * square))
        half = 0.5 + 0.5 * curve
        act[token_rows(j), :] = (pre * half).astype(BF16)
        dg[token_rows(j), :] = half + 0.5 * slope * pre * (1.0 - curve * curve) * (1.0 + 0.134145 * square)
        return carry

    lax.fori_loop(0, 4, widen, 0)
    gather_2.forward_far()

    def column_products(left, right, out):
        def step(t, carry):
            at = pl.ds(pl.multiple_of(t * LANES, LANES), LANES)
            out[at, :] = mm(left[:, at], right[...], TN).astype(BF16)
            return carry

        lax.fori_loop(0, left.shape[1] // LANES, step, 0)

    column_products(gc, act, g2)
    reduce_2.across_y()
    gather_2.finish()

    def hidden_back(j):
        at = token_rows(j)
        low = (mm(gc[at, :], w2[...], NN) * dg[at, :]).astype(BF16)
        gp[at, :] = low
        column = jnp.sum(low.astype(F32), 0, keepdims=True)
        sms[0, pl.ds(8 + s, 1), :] += column
        return mm(low, w1[...], NT)

    gather_1.sent()
    sum_two = seq_sum_start(hidden_back, sb_a, cr_a)
    seq_sum_across(sum_two, sb_a, cr_a, xr_a)
    reduce_2.across_last()
    column_products(h2, gp, g1)
    reduce_1.across_y()
    reduce_2.along_z(3)
    reduce_2.along_z(2)
    grad_h = seq_sum_finish(sum_two, sb_a, cr_a, xr_a)
    hat, inverse = normalize(padded(o_mixed))
    kept = gc[token_rows(s), :].astype(F32)
    grad_x = kept + norm_back(grad_h, gain_two, hat, inverse)
    o_gtok[0] = grad_x[0:slice_len]
    low = grad_x.astype(BF16)
    sms[0, 1:2, :] = jnp.sum(grad_h * hat, 0, keepdims=True)
    sms[0, 4:5, :] = jnp.sum(grad_h, 0, keepdims=True)
    sms[0, 5:6, :] = jnp.sum(kept, 0, keepdims=True)
    sms[0, 3:4, :] = jnp.sum(low.astype(F32), 0, keepdims=True)
    gc[token_rows(s), :] = low
    gb_in = TokenGather(gc)
    gb_in.start(gc.at[token_rows(s)])

    sum_three = seq_sum_start(lambda j: mm(act[token_rows(j), :], w2[...], NT), sb_b, cr_b)
    seq_sum_across(sum_three, sb_b, cr_b, xr_b)
    reduce_2.along_z(1)
    reduce_1.across_last()
    gb_in.forward()
    gb_in.finish()

    def attended_back(j, carry):
        attm[token_rows(j), :] = mm(gc[token_rows(j), :], wo[...], NT).astype(BF16)
        return carry

    lax.fori_loop(0, 4, attended_back, 0)

    o_sent()

    def out_products(head, carry):
        at = pl.ds(pl.multiple_of(head * LANES, LANES), LANES)
        go[at, :] = mm(att_t[head], gc[...], NN).astype(BF16)
        return carry

    lax.fori_loop(0, 4, out_products, 0)
    ro_across_y()
    reduce_2.relay()
    branch = seq_sum_finish(sum_three, sb_b, cr_b, xr_b)
    o_mixed[0] = jnp.where(real_rows(s, d), padded(o_mixed) + branch + bias_two, 0.0)[0:slice_len]

    wide_lanes = lane_ids(rows)
    chunk_lanes = lane_ids(chunk)

    def attend_back(head, carry):
        grad_k = jnp.zeros((rows, LANES), F32)
        grad_v = jnp.zeros((rows, LANES), F32)
        grad_q = []
        for part in range(rows // chunk):
            at = slice(part * chunk, (part + 1) * chunk)
            query, grad_out = qkv[head, at, :], attm[at, pl.ds(pl.multiple_of(head * LANES, LANES), LANES)]
            scores = mm(qkv[4 + head], query, NT)
            probs = jnp.exp(scores * scale - lse[head, :, at])
            grad_p = mm(qkv[8 + head], grad_out, NT)
            delta = jnp.sum(probs * grad_p, 0, keepdims=True)
            grad_s = (probs * (grad_p - delta)).astype(BF16)
            grad_k += mm(grad_s, query, NN)
            grad_v += mm(probs.astype(BF16), grad_out, NN)
            grad_q.append(mm(qkv[4 + head], grad_s, TN))
        for part in range(rows // chunk):
            at = slice(part * chunk, (part + 1) * chunk)
            low = jnp.where(chunk_lanes < hd, grad_q[part].T * scale, 0.0).astype(BF16)
            qkv[head, at, :] = low
            shs[0, pl.ds(4 * head + k, 1), :] += jnp.sum(low.astype(F32), 0, keepdims=True)
        qkv[4 + head] = jnp.where(wide_lanes < hd, grad_k * scale, 0.0).astype(BF16)
        low = grad_v.astype(BF16)
        qkv[8 + head] = low
        shs[0, pl.ds(16 + 4 * head + k, 1), :] = jnp.sum(low.astype(F32), 0, keepdims=True)
        return carry

    reduce_1.along_z(3)
    lax.fori_loop(0, 2, attend_back, 0)
    reduce_1.along_z(2)
    lax.fori_loop(2, 4, attend_back, 0)
    reduce_1.along_z(1)
    reduce_1.relay()

    gpj = h2.at[:, 0:qw]

    def pack(j, carry):
        parts = [qkv[n, token_rows(j), :].astype(F32) for n in range(12)]
        for to, tile in enumerate(pack_lanes(parts, hd, lanes)):
            gpj[token_rows(j), LANES * to : LANES * (to + 1)] = tile.astype(BF16)
        return carry

    lax.fori_loop(0, 4, pack, 0)
    column_products(h1, gpj, gq)
    reduce_q.across_y()
    ro_along_z()
    reduce_2.pieces()

    def tokens_back(j):
        part = mm(gpj[token_rows(j), :], wq[...], NT)
        hat, _ = normalize(xs[token_rows(j), :].astype(F32))
        sms[0, 0:1, :] += jnp.sum(part * hat, 0, keepdims=True)
        sms[0, 2:3, :] += jnp.sum(part, 0, keepdims=True)
        return part

    sum_four = seq_sum_start(tokens_back, sb_a, cr_a)
    sm_at, sh_at = take(7), take(7)

    def vectors(stage, slots, devices):
        for slot, device in zip(slots, devices, strict=True):
            send(sms.at[stage], smr.at[slot], sm_at + slot, device)
            send(shs.at[stage], shr.at[slot], sh_at + slot, device)

    def vectors_sum(stage, slots, devices):
        for slot, device in zip(slots, devices, strict=True):
            copy(smr.at[slot], smr.at[slot], sm_at + slot, device).wait_recv()
            copy(shr.at[slot], shr.at[slot], sh_at + slot, device).wait_recv()
        total, heads = sms[stage], shs[stage]
        for slot in slots:
            total += smr[slot]
            heads += shr[slot]
        return total, heads

    z_to_all, z_from_all = [z_dev(t) for t in (1, 2, 3)], [z_dev(-t) for t in (1, 2, 3)]
    s_to_all, s_from_all = [(i, s_at(t)) for t in (1, 2, 3)], [(i, s_at(-t)) for t in (1, 2, 3)]
    vectors(0, (1, 2, 3), z_to_all)
    seq_sum_across(sum_four, sb_a, cr_a, xr_a)
    reduce_q.along_z(3, 2)
    reduce_q.relay()
    grad_h = seq_sum_finish(sum_four, sb_a, cr_a, xr_a)
    hat, inverse = normalize(xs[token_rows(s), :].astype(F32))
    o_gtok[0] = (padded(o_gtok) + norm_back(grad_h, gain_one, hat, inverse))[0:slice_len]
    reduce_q.along_z(1)
    sms[1], shs[1] = vectors_sum(0, (1, 2, 3), z_from_all)
    vectors(1, (4, 5, 6), s_to_all)
    reduce_1.pieces()
    reduce_2.finish()
    reduce_2.publish_wide(o_2)
    sms[2], shs[2] = vectors_sum(1, (4, 5, 6), s_from_all)
    vectors(2, (0,), (y_peer,))
    ro_pieces()
    reduce_q.pieces()
    reduce_1.finish()
    reduce_1.publish_wide(o_1)
    summed_rows, by_head = vectors_sum(2, (0,), (y_peer,))
    mine = smr.at[1]
    for to, row in enumerate((0, 1, 2, None, None, 3, 4, 5)):
        if row is not None:
            mine[to : to + 1, :] = summed_rows[row : row + 1, :]
    for which in range(2):
        heads = [by_head[16 * which + head : 16 * which + head + 1, :] for head in range(d // hd)]
        for to, tile in enumerate(pack_lanes(heads, hd, one_lane)):
            mine[3 + which : 4 + which, to * LANES : (to + 1) * LANES] = tile
    start = (i * 4 + s) * own
    turned = pltpu.roll(mine[0:8, :], lax.rem(d - start, d), 1)
    o_gains[...] = turned[0:2, 0:own]
    o_biases[...] = turned[2:8, 0:own]
    spread = {}
    for j in range(4):
        tile, offset = divmod(j * f, LANES)
        for t in range(w1.shape[1] // LANES):
            part = summed_rows[8 + j : 9 + j, t * LANES : (t + 1) * LANES]
            if offset:
                part = pltpu.roll(part, offset, 1)
            for to, where in ((tile + t, one_lane >= offset), (tile + t + 1, one_lane < offset)):
                if to * LANES < 4 * f:
                    kept = jnp.where(where, part, 0.0)
                    spread[to] = spread[to] + kept if to in spread else kept
    for to, tile in spread.items():
        width = min(LANES, 4 * f - to * LANES)
        o_fb[:, to * LANES : to * LANES + width] = tile[:, 0:width]
    ro_finish()
    reduce_q.finish()
    reduce_q.publish_heads(o_q)
    for part in (gather_q, gather_2, reduce_q, reduce_1, reduce_2):
        part.sent()
    for made in sends:
        made.wait_send()


def hand_over(mixed, tokens, g_qkv, g_1, g_2, g_out, g_gains, g_biases, *outs):
    o_mixed, o_tokens, o_qkv, o_1, o_2, o_out, o_gains, o_biases = outs
    o_qkv[...] = g_qkv[...]
    o_1[...] = g_1[...]
    o_2[...] = g_2[...]
    o_mixed[:, 0, :] = mixed[0]
    o_tokens[:, 0, :] = tokens[0]
    o_out[...] = g_out[0 : o_out.shape[0], :].astype(F32)
    o_gains[...] = g_gains[...]
    o_biases[...] = g_biases[...]


def whole_layer(tokens, offsets, w_qkv, w_out, w_fc1, w_fc2, gains, biases, fc1_bias, cotangent):
    _, slice_len, d = tokens.shape
    hd = d // HEADS
    own, wide = w_fc1.shape
    f = wide // 4
    f_pad = -(-f // LANES) * LANES
    packed = 12 * hd
    qw = -(-(packed + 8) // LANES) * LANES
    n_z = lax.axis_size("img") // 2
    rb = own * 4
    rows = 4 * BLOCK

    hbm = pl.BlockSpec(memory_space=pl.ANY)
    vmem = pl.BlockSpec(memory_space=pltpu.VMEM)
    outs = [
        ((1, slice_len, d), F32, vmem),
        ((1, slice_len, d), F32, vmem),
        ((own, 3 * d), F32, vmem),
        ((PIECE, d), BF16, hbm),
        ((own, wide), F32, vmem),
        ((own, wide), F32, vmem),
        ((1, wide), F32, vmem),
        ((2, own), F32, vmem),
        ((6, own), F32, vmem),
    ]
    low = [
        (d, qw), (4 * LANES, d), (d, f_pad), (d, f_pad),
        (4, PIECE, qw), (2, PIECE, d), (4, PIECE, f_pad), (4, PIECE, f_pad),
    ]
    scratch = [pltpu.VMEM(shape, BF16) for shape in low]
    scratch += [pltpu.VMEM((160, max(d, f_pad)), F32)]
    scratch += [pltpu.VMEM((rows, w), BF16) for w in (d, d, d, d, f_pad, f_pad)]
    scratch += [pltpu.VMEM((rows, f_pad), F32)]
    scratch += [
        pltpu.VMEM((12, rows, LANES), BF16),
        pltpu.VMEM((rows, 4 * LANES), BF16),
        pltpu.VMEM((4, LANES, rows), BF16),
        pltpu.VMEM((4, 1, rows), F32),
    ]
    scratch += [pltpu.VMEM(shape, BF16) for shape in ((d, f_pad), (d, f_pad), (d, qw))]
    scratch += [pltpu.VMEM((n_z, h, w), BF16) for h, w in ((rb, f_pad), (rb, f_pad), (HEAD_ROWS, d), (rb, qw))]
    scratch += [pltpu.VMEM((n_z, h, w), BF16) for h, w in ((rb, f_pad), (rb, f_pad), (HEAD_ROWS, d), (rb, qw))]
    scratch += [pltpu.VMEM((n_z, SLIVER, w), BF16) for w in (f_pad, f_pad)]
    for _ in range(2):
        scratch += [pltpu.VMEM((n, BLOCK, d), BF16) for n in (3, 2)] + [pltpu.VMEM((BLOCK, d), BF16)]
    scratch += [
        pltpu.VMEM((2, BLOCK, d), F32),
        pltpu.VMEM((1, f_pad), F32),
        pltpu.VMEM((8, d), F32),
        pltpu.VMEM((2, 16, LANES), F32),
        pltpu.VMEM((3, 16, d), F32),
        pltpu.VMEM((7, 16, d), F32),
        pltpu.VMEM((3, 32, LANES), F32),
        pltpu.VMEM((7, 32, LANES), F32),
        pltpu.SemaphoreType.DMA((200,)),
        pltpu.SemaphoreType.DMA((200,)),
        pltpu.SemaphoreType.DMA((8,)),
    ]
    mixed, grad_tokens, gq, go, g1, g2, g_fb, g_gains, g_biases = pl.pallas_call(
        partial(layer_kernel, (slice_len, d, hd, f, qw, n_z)),
        out_shape=[jax.ShapeDtypeStruct(shape, kind) for shape, kind, _ in outs],
        in_specs=[pl.BlockSpec(memory_space=pltpu.SMEM)] + [vmem] * 9,
        out_specs=[spec for _, _, spec in outs],
        scratch_shapes=scratch,
        compiler_params=pltpu.CompilerParams(
            collective_id=0, has_side_effects=True, vmem_limit_bytes=VMEM_BYTES
        ),
    )(offsets, w_qkv, w_out, w_fc1, w_fc2, gains.T, biases.T, fc1_bias[None], tokens, cotangent)

    rows_out = jax.ShapeDtypeStruct((slice_len, 1, d), F32)
    same = [jax.ShapeDtypeStruct(made.shape, F32) for made in (gq, g1, g2)]
    rest = [jax.ShapeDtypeStruct(shape, F32) for shape in ((own, d), (2, own), (6, own))]
    mixed, grad_tokens, gq, g1, g2, go, g_gains, g_biases = pl.pallas_call(
        hand_over,
        out_shape=[rows_out, rows_out, *same, *rest],
        in_specs=[vmem] * 8,
        out_specs=[vmem] * 8,
    )(mixed, grad_tokens, gq, g1, g2, go, g_gains, g_biases)
    mixed, grad_tokens = mixed.reshape(tokens.shape), grad_tokens.reshape(tokens.shape)
    return mixed, grad_tokens, gq, go, g1, g2, g_gains.T, g_biases.T, g_fb.reshape(wide)


def local(tokens, offsets, w_qkv, w_out, w_fc1, w_fc2, gains, biases, fc1_bias, cotangent):
    images_here, slice_len, model_width = tokens.shape
    head_count = HEADS
    head_dim = model_width // head_count
    length = slice_len * lax.axis_size("seq")
    row_count = images_here * slice_len
    score_scale = head_dim ** (-0.5)
    gathered = (
        lax.all_gather(w_qkv, ("img", "seq"), axis=0, tiled=True),
        lax.all_gather(w_out, ("img", "seq"), axis=0, tiled=True),
        lax.all_gather(w_fc1, ("img", "seq"), axis=0, tiled=True),
        lax.all_gather(w_fc2, ("img", "seq"), axis=0, tiled=True),
        lax.all_gather(gains, ("img", "seq"), axis=0, tiled=True),
        lax.all_gather(biases, ("img", "seq"), axis=0, tiled=True),
    )
    wide_qkv, wide_out, wide_fc1, wide_fc2, gain_all, bias_all = gathered
    gain_cols = gain_all.astype(jnp.float32)
    bias_cols = bias_all.astype(jnp.float32)
    starts = offsets[:, None]
    positions = lax.axis_index("seq") * slice_len + jnp.arange(slice_len, dtype=jnp.int32)
    own_valid = (positions[None, :] >= starts) & (positions[None, :] < starts + VALID)
    row_valid = own_valid.astype(jnp.float32)
    key_pos = jnp.arange(length, dtype=jnp.int32)
    key_valid = (key_pos[None, :] >= starts) & (key_pos[None, :] < starts + VALID)
    inputs = tokens.astype(jnp.float32).reshape(row_count, model_width)
    h_one, norm_one_back = jax.vjp(layer_norm, inputs, gain_cols[:, 0], bias_cols[:, 0])
    h_one_low = h_one.astype(jnp.bfloat16)
    qkv_bias = jnp.concatenate([bias_cols[:, 1], jnp.zeros_like(bias_cols[:, 1]), bias_cols[:, 2]])
    projected = (
        jnp.dot(h_one_low, wide_qkv, preferred_element_type=jnp.float32) + qkv_bias
    ).astype(jnp.bfloat16)
    query_rows = projected[:, :model_width]
    key_rows = projected[:, model_width : 2 * model_width].reshape(
        images_here, slice_len, model_width
    )
    value_rows = projected[:, 2 * model_width :].reshape(images_here, slice_len, model_width)
    keys_all, values_all = (
        lax.all_gather(key_rows, "seq", axis=1, tiled=True),
        lax.all_gather(value_rows, "seq", axis=1, tiled=True),
    )
    query_heads = split_heads(query_rows, images_here, slice_len, head_count, head_dim)
    key_heads = split_heads(keys_all, images_here, length, head_count, head_dim)
    value_heads = split_heads(values_all, images_here, length, head_count, head_dim)

    def head_scores(head_query_rows, head_key_rows, mask):
        scores = (
            jnp.einsum(
                "asl,aul->asu", head_query_rows, head_key_rows, preferred_element_type=jnp.float32
            )
            * score_scale
        )
        return jnp.where(mask[:, None, :], scores, masked_score)

    def forward_head(head_args):
        head_query_rows, head_key_rows, head_value_rows = head_args
        scores = head_scores(head_query_rows, head_key_rows, key_valid)
        maxima = jnp.max(scores, -1, keepdims=True)
        exponent = jnp.exp(scores - maxima)
        totals_row = jnp.sum(exponent, -1, keepdims=True)
        probs = exponent / totals_row
        attended_head = jnp.einsum(
            "owz,ozf->owf",
            probs.astype(jnp.bfloat16),
            head_value_rows,
            preferred_element_type=jnp.float32,
        )
        return (attended_head, maxima[..., 0] + jnp.log(totals_row[..., 0]))

    attended_heads, log_total = lax.map(forward_head, (query_heads, key_heads, value_heads))
    attended = join_heads(attended_heads).reshape(row_count, model_width).astype(jnp.bfloat16)
    middle = (
        inputs + jnp.dot(attended, wide_out, preferred_element_type=jnp.float32) + bias_cols[:, 3]
    )
    h_two, norm_two_back = jax.vjp(layer_norm, middle, gain_cols[:, 1], bias_cols[:, 4])
    h_two_low = h_two.astype(jnp.bfloat16)
    preact = jnp.dot(h_two_low, wide_fc1, preferred_element_type=jnp.float32) + fc1_bias.astype(
        jnp.float32
    )
    activated, gelu_back = jax.vjp(partial(jax.nn.gelu, approximate=True), preact)
    activated_low = activated.astype(jnp.bfloat16)
    branch_two = last_dot(activated_low, wide_fc2) + bias_cols[:, 5]
    valid_rows = row_valid.reshape(row_count, 1)
    mixed = (valid_rows * (middle + branch_two)).reshape(images_here, slice_len, model_width)
    wide_qkv, wide_out, wide_fc1, wide_fc2 = (
        lax.all_gather(w_qkv, ("img", "seq"), axis=0, tiled=True),
        lax.all_gather(w_out, ("img", "seq"), axis=0, tiled=True),
        lax.all_gather(w_fc1, ("img", "seq"), axis=0, tiled=True),
        lax.all_gather(w_fc2, ("img", "seq"), axis=0, tiled=True),
    )
    grad_output = cotangent.astype(jnp.float32).reshape(row_count, model_width) * valid_rows
    grad_branch = grad_output.astype(jnp.bfloat16)
    grad_bias_two = jnp.sum(grad_branch.astype(jnp.float32), 0)
    grad_fc2_local = row_dot(grad_branch, activated_low)
    grad_activated = jnp.dot(grad_branch, wide_fc2, preferred_element_type=jnp.float32)
    (grad_preact,) = gelu_back(grad_activated)
    preact_low = grad_preact.astype(jnp.bfloat16)
    grad_hidden_bias = jnp.sum(preact_low.astype(jnp.float32), 0)
    grad_fc1_local = row_dot(h_two_low, preact_low)
    grad_h_two = last_dot(preact_low, wide_fc1)
    grad_middle_norm, grad_gain_two, grad_shift_two = norm_two_back(grad_h_two)
    grad_middle = grad_output + grad_middle_norm
    grad_branch_one = grad_middle.astype(jnp.bfloat16)
    grad_out_bias = jnp.sum(grad_branch_one.astype(jnp.float32), 0)
    output_gradient_shard = row_dot(attended, grad_branch_one)
    grad_attended = last_dot(grad_branch_one, wide_out).astype(jnp.bfloat16)
    grad_att_heads = split_heads(grad_attended, images_here, slice_len, head_count, head_dim)

    def backward_head(head_args):
        head_query_rows, head_key_rows, head_value_rows, head_gradient, total_head = head_args
        scores = head_scores(head_query_rows, head_key_rows, key_valid)
        probs = jnp.exp(scores - total_head[..., None])
        grad_probs = jnp.einsum(
            "asl,aul->asu", head_gradient, head_value_rows, preferred_element_type=jnp.float32
        )
        grad_scores = probs * (grad_probs - jnp.sum(probs * grad_probs, -1, keepdims=True))
        reduced_scores = grad_scores.astype(jnp.bfloat16)
        grad_query = (
            jnp.einsum(
                "owz,ozf->owf", reduced_scores, head_key_rows, preferred_element_type=jnp.float32
            )
            * score_scale
        )
        grad_key = (
            jnp.einsum(
                "xzl,xzv->xlv", reduced_scores, head_query_rows, preferred_element_type=jnp.float32
            )
            * score_scale
        )
        grad_value = jnp.einsum(
            "xzl,xzv->xlv",
            probs.astype(jnp.bfloat16),
            head_gradient,
            preferred_element_type=jnp.float32,
        )
        return (grad_query, grad_key, grad_value)

    grad_q_heads, grad_k_heads, grad_v_heads = lax.map(
        backward_head, (query_heads, key_heads, value_heads, grad_att_heads, log_total)
    )
    key_gradient_rows, grad_values = (
        lax.psum_scatter(
            join_heads(grad_k_heads).astype(jnp.bfloat16), "seq", scatter_dimension=1, tiled=True
        ).astype(jnp.float32),
        lax.psum_scatter(
            join_heads(grad_v_heads).astype(jnp.bfloat16), "seq", scatter_dimension=1, tiled=True
        ).astype(jnp.float32),
    )
    grad_projected = jnp.concatenate(
        [
            join_heads(grad_q_heads).reshape(row_count, model_width),
            key_gradient_rows.reshape(row_count, model_width),
            grad_values.reshape(row_count, model_width),
        ],
        1,
    ).astype(jnp.bfloat16)
    grad_query_bias = jnp.sum(grad_projected[:, :model_width].astype(jnp.float32), 0)
    grad_value_bias = jnp.sum(grad_projected[:, 2 * model_width :].astype(jnp.float32), 0)
    grad_qkv_local = row_dot(h_one_low, grad_projected)
    grad_h_one = last_dot(grad_projected, wide_qkv)
    grad_input_norm, grad_gain_one, grad_shift_one = norm_one_back(grad_h_one)
    grad_tokens = (grad_middle + grad_input_norm).reshape(images_here, slice_len, model_width)
    grad_gain_local = jnp.stack([grad_gain_one, grad_gain_two], 1)
    grad_bias_local = jnp.stack(
        [
            grad_shift_one,
            grad_query_bias,
            grad_value_bias,
            grad_out_bias,
            grad_shift_two,
            grad_bias_two,
        ],
        1,
    )
    owned = (
        lax.psum_scatter(grad_qkv_local, ("img", "seq"), scatter_dimension=0, tiled=True),
        lax.psum_scatter(output_gradient_shard, ("img", "seq"), scatter_dimension=0, tiled=True),
        lax.psum_scatter(grad_fc1_local, ("img", "seq"), scatter_dimension=0, tiled=True),
        lax.psum_scatter(grad_fc2_local, ("img", "seq"), scatter_dimension=0, tiled=True),
        lax.psum_scatter(grad_gain_local, ("img", "seq"), scatter_dimension=0, tiled=True),
        lax.psum_scatter(grad_bias_local, ("img", "seq"), scatter_dimension=0, tiled=True),
    )
    hidden_bias_total = lax.psum(grad_hidden_bias, ("img", "seq"))
    return (
        mixed,
        grad_tokens,
        owned[0],
        owned[1],
        owned[2],
        owned[3],
        owned[4],
        owned[5],
        hidden_bias_total,
    )


def solution(mesh):
    in_specs = (
        P("img", "seq", None),
        P("img"),
        P(("img", "seq"), None),
        P(("img", "seq"), None),
        P(("img", "seq"), None),
        P(("img", "seq"), None),
        P(("img", "seq"), None),
        P(("img", "seq"), None),
        P(),
        P("img", "seq", None),
    )
    out_specs = (
        P("img", "seq", None),
        P("img", "seq", None),
        P(("img", "seq"), None),
        P(("img", "seq"), None),
        P(("img", "seq"), None),
        P(("img", "seq"), None),
        P(("img", "seq"), None),
        P(("img", "seq"), None),
        P(),
    )
    shards = mesh.shape["img"] * mesh.shape["seq"]
    fits = mesh.shape["seq"] == 4 and shards == 2 * HEADS
    plan = whole_layer if fits else local
    return jax.shard_map(plan, mesh=mesh, in_specs=in_specs, out_specs=out_specs, check_vma=False)
```

```python
from functools import partial

import jax
import jax.numpy as jnp
from jax import lax
from jax.experimental import pallas as pl
from jax.experimental.pallas import tpu as pltpu
from jax.sharding import PartitionSpec as P

HEADS = 16
VALID = 729


masked_score = -1000000000.0
norm_epsilon = 1e-06


def layer_norm(values, gain_col, bias_col):
    average = jnp.mean(values, -1, keepdims=True)
    centered = values - average
    variance = jnp.mean(centered * centered, -1, keepdims=True)
    return centered * lax.rsqrt(variance + norm_epsilon) * gain_col + bias_col


def row_dot(left, right):
    return lax.dot_general(
        left, right, (((0,), (0,)), ((), ())), preferred_element_type=jnp.float32
    )


def last_dot(left, right):
    return lax.dot_general(
        left, right, (((1,), (1,)), ((), ())), preferred_element_type=jnp.float32
    )


def split_heads(tensor, images_here, count, head_count, head_dim):
    return tensor.reshape(images_here, count, head_count, head_dim).transpose(2, 0, 1, 3)


def join_heads(tensor):
    head_count, images_here, count, head_dim = tensor.shape
    return tensor.transpose(1, 2, 0, 3).reshape(images_here, count, head_count * head_dim)


VMEM_BYTES = 63 * 2**20
MESH_IDS = pl.DeviceIdType.MESH
F32 = jnp.float32
BF16 = jnp.bfloat16
LANES = 128
SLIVER = 16
PIECE = 48
BLOCK = 192
HEAD_ROWS = 80
NN = (((1,), (0,)), ((), ()))
NT = (((1,), (1,)), ((), ()))
TN = (((0,), (0,)), ((), ()))


def mm(left, right, dims):
    return lax.dot_general(left, right, dims, preferred_element_type=F32)


def normalize(values):
    average = jnp.mean(values, -1, keepdims=True)
    centered = values - average
    variance = jnp.mean(centered * centered, -1, keepdims=True)
    inverse = lax.rsqrt(variance + norm_epsilon)
    return centered * inverse, inverse


def norm_back(grad, gain, hat, inverse):
    scaled = grad * gain
    first = jnp.mean(scaled, -1, keepdims=True)
    second = jnp.mean(scaled * hat, -1, keepdims=True)
    return inverse * (scaled - first - hat * second)


def lane_ids(rows):
    return lax.broadcasted_iota(jnp.int32, (rows, LANES), 1)


def lane_window(tiles, start, width, lanes):
    tile, offset = divmod(start, LANES)
    if offset == 0:
        return tiles[tile]
    first = pltpu.roll(tiles[tile], LANES - offset, 1)
    if offset + width <= LANES:
        return first
    second = pltpu.roll(tiles[tile + 1], LANES - offset, 1)
    return jnp.where(lanes < LANES - offset, first, second)


def pack_lanes(parts, width, lanes):
    tiles = {}
    for n, part in enumerate(parts):
        tile, offset = divmod(n * width, LANES)
        if offset:
            part = pltpu.roll(part, offset, 1)
        ends = [(tile, lanes >= offset)]
        if offset + width > LANES:
            ends.append((tile + 1, lanes < offset + width - LANES))
        for to, where in ends:
            kept = jnp.where(where, part, 0.0)
            tiles[to] = tiles[to] + kept if to in tiles else kept
    return [tiles[to] for to in sorted(tiles)]


class Tiles:
    def __init__(self, ref, first, step, height):
        self.ref, self.first, self.step, self.height = ref, first, step, height
        self.wide = ref.shape[1] // LANES

    def __getitem__(self, tile):
        part, at = divmod(tile, self.wide)
        row = self.first + part * self.step
        return self.ref[row : row + self.height, at * LANES : (at + 1) * LANES]

    def fill(self, source):
        whole = self.wide * LANES
        rows, wide = source.shape
        for part in range(-(-wide // whole)):
            row = self.first + part * self.step
            width = min(whole, wide - part * whole)
            self.ref[row + rows // 16 * 16 : row + self.height, :] = jnp.zeros(
                (self.height - rows // 16 * 16, whole), F32
            )
            if width < whole:
                last = width // LANES * LANES
                self.ref[row : row + self.height, last : last + LANES] = jnp.zeros((self.height, LANES), F32)
            self.ref[row : row + rows, 0:width] = source[:, part * whole : part * whole + width].astype(F32)


def layer_kernel(
    dims,
    off_ref, w_qkv, w_out, w_fc1, w_fc2, gains, biases, fc1_bias, tok, cot,
    o_mixed, o_gtok, o_q, o_fo, o_1, o_2, o_fb, o_gains, o_biases,
    wq, wo, w1, w2, rq, ro, r1, r2, tmp,
    xs, gc, h1, h2, act, gp, dg, qkv, attm, att_t, lse,
    g1, g2, gq, y1, y2, yo, yq, z1, z2, zo, zq, s1, s2,
    sb_a, cr_a, xr_a, sb_b, cr_b, xr_b, pf, fb, prm, bh, sms, smr, shs, shr,
    ssem, rsem, lsem,
):
    slice_len, d, hd, f, qw, n_z = dims
    scale = hd ** (-0.5)
    mask_low = masked_score / scale
    chunk = 256
    rows = 4 * BLOCK
    i, s = lax.axis_index("img"), lax.axis_index("seq")
    z, y = lax.div(i, 2), lax.rem(i, 2)
    x, c = lax.div(s, 2), lax.rem(s, 2)
    k = 2 * c + x
    cy = c == y
    core_peer = (i, x * 2 + 1 - c)
    x_peer = (i, (1 - x) * 2 + c)
    y_peer = (z * 2 + 1 - y, s)
    rb = wq.shape[0] // (2 * n_z)
    own = rb // 4

    def z_at(t):
        return lax.rem(z + t + n_z, n_z)

    def z_dev(t):
        return (z_at(t) * 2 + y, s)

    def z_to(zt):
        return (zt * 2 + y, s)

    near = (
        z,
        jnp.where(z == 0, 1, z - 1),
        jnp.where(z == 0, 2, jnp.where(z == 3, 1, z + 1)),
        jnp.where(z <= 1, 3, 0),
    )
    middle = (z == 1) | (z == 2)
    end = jnp.where(z == 1, 0, 3)

    def s_at(t):
        return lax.rem(s + t + 4, 4)

    count = [0]

    def take(n=1):
        first = count[0]
        count[0] += n
        return first

    def copy(src, dst, index, device, at=None):
        return pltpu.make_async_remote_copy(
            src, dst, ssem.at[index], rsem.at[index if at is None else at], device_id=device, device_id_type=MESH_IDS
        )

    sends = []

    def send(src, dst, index, device, at=None):
        made = copy(src, dst, index, device, at)
        made.start()
        sends.append(made)

    def token_rows(j):
        return pl.ds(pl.multiple_of(j * BLOCK, BLOCK), BLOCK)

    def img_rows(b):
        return pl.ds(pl.multiple_of(b * rb, 16), rb)

    def most_rows(b, most=rb - SLIVER):
        return pl.ds(pl.multiple_of(b * rb, 16), most)

    def sliver_rows(b):
        return pl.ds(pl.multiple_of(b * rb + rb - SLIVER, 16), SLIVER)

    barrier = pltpu.get_barrier_semaphore()
    partners = [(i, s_at(t)) for t in (1, 2, 3)] + [z_dev(t) for t in range(1, n_z)] + [y_peer]
    for partner in partners:
        pl.semaphore_signal(barrier, inc=1, device_id=partner, device_id_type=MESH_IDS)

    class Gather:
        def __init__(self, piece, recv, full, local_index):
            self.piece, self.recv, self.full = piece, recv, full
            self.width = full.shape[1]
            self.sp, self.sz, self.sy, self.ss = take(4), take(n_z), take(n_z), take(n_z)
            self.local = local_index
            self.started = []

        def pieces(self):
            self.own_piece().start()
            for t in (1, 2, 3):
                self.piece_to(t).start()

        def own_piece(self):
            return pltpu.make_async_copy(self.piece.at[s, 0:PIECE], self.recv.at[s], lsem.at[self.local])

        def piece_to(self, t):
            to = s_at(t)
            return copy(self.piece.at[to, 0:PIECE], self.recv.at[s], self.sp + t, (i, to))

        def assemble(self):
            self.own_piece().wait()
            for t in (1, 2, 3):
                self.piece_to(t).wait_send()
                came = self.recv.at[s_at(-t)]
                copy(came, came, self.sp + t, (i, s_at(-t))).wait_recv()
            part = rb // 4
            for j in range(4):
                tmp[part * j : part * j + PIECE, 0 : self.width] = self.recv[j].astype(F32)
            self.full[img_rows(i), :] = tmp[0:rb, 0 : self.width].astype(BF16)

        def block(self, zb, side):
            return self.full.at[img_rows(zb * 2 + side)]

        def most(self, zb, side):
            return self.full.at[most_rows(zb * 2 + side)]

        def sliver(self, zb, side):
            return self.full.at[sliver_rows(zb * 2 + side)]

        def slivers(self):
            whole, part = self.block(z, 1 - y), self.sliver(z, 1 - y)
            copy(whole, whole, self.sy, y_peer, self.sy + z).wait_recv()
            for u in (1, 2, 3):
                self.send(part, part, self.ss + u, z_to(near[u]), self.ss + z)

        def send(self, src, dst, index, device, at):
            made = copy(src, dst, index, device, at)
            made.start()
            self.started.append(made)

        def along_z(self):
            own = self.block(z, y)
            for u in (1, 2):
                self.send(own, own, self.sz + u, z_to(near[u]), self.sz + z)

            @pl.when(middle)
            def _():
                copy(own, own, self.sz + 3, z_to(near[3]), self.sz + z).start()

        def across_y(self):
            own = self.block(z, y)
            self.send(own, own, self.sy, y_peer, self.sy + z)

        def forward(self, *steps):
            for u in steps:
                zb = near[u]
                came = self.block(zb, y)
                copy(came, came, self.sz, z_to(zb), self.sz + zb).wait_recv()
                came = self.most(zb, y)
                copy(came, came, self.sy + u, y_peer, self.sy + zb).start()

        def relay(self):
            @pl.when(middle)
            def _():
                came = self.block(near[3], y)
                copy(came, came, self.sz, z_to(end), self.sz + near[3]).wait_recv()
                copy(came, came, self.sz, z_to(end), self.sz + near[3]).start()
                came = self.most(near[3], y)
                copy(came, came, self.sy + 3, y_peer, self.sy + near[3]).start()

        def forward_far(self):
            @pl.when(jnp.logical_not(middle))
            def _():
                self.forward(3)

        def finish(self):
            for u in (1, 2, 3):
                zb = near[u]
                came = self.most(zb, 1 - y)
                copy(came, came, self.sy, y_peer, self.sy + zb).wait_recv()
                came = self.sliver(zb, 1 - y)
                copy(came, came, self.ss, z_to(zb), self.ss + zb).wait_recv()

        def sent(self):
            for made in self.started:
                made.wait_send()

            @pl.when(middle)
            def _():
                own, came = self.block(z, y), self.block(near[3], y)
                copy(own, own, self.sz + 3, z_to(near[3]), self.sz + z).wait_send()
                copy(came, came, self.sz, z_to(end), self.sz + near[3]).wait_send()

            for u in (1, 2, 3):
                came = self.most(near[u], y)
                copy(came, came, self.sy + u, y_peer, self.sy + near[u]).wait_send()

    gather_q = Gather(yq, rq, wq, 0)
    gather_1 = Gather(y1, r1, w1, 1)
    gather_2 = Gather(y2, r2, w2, 2)
    o_piece, o_z, o_y = take(), take(n_z), take(n_z)

    def head_block(array, t):
        return array.at[pl.ds(pl.multiple_of(z_at(-t) * LANES, LANES), HEAD_ROWS)]

    po = yo.at[0, 0:PIECE]

    def o_start():
        @pl.when(cy)
        def _():
            pltpu.make_async_copy(po, ro.at[c], lsem.at[3]).start()

        @pl.when(jnp.logical_not(cy))
        def _():
            copy(po, ro.at[c], o_piece, core_peer).start()

    def o_assemble():
        @pl.when(jnp.logical_not(cy))
        def _():
            copy(po, ro.at[c], o_piece, core_peer).wait_send()

        for h in range(4):
            wo[h * LANES + HEAD_ROWS : (h + 1) * LANES, :] = jnp.zeros((LANES - HEAD_ROWS, d), BF16)

        @pl.when(cy)
        def _():
            pltpu.make_async_copy(po, ro.at[c], lsem.at[3]).wait()
            copy(po, ro.at[1 - c], o_piece, core_peer).wait_recv()
            for j in range(2):
                tmp[own * j : own * j + PIECE, :] = ro[j].astype(F32)
            wo[pl.ds(pl.multiple_of(z * LANES, LANES), HEAD_ROWS), :] = tmp[0:HEAD_ROWS, :].astype(BF16)

    def o_along_z():
        @pl.when(cy)
        def _():
            mine = head_block(wo, 0)
            for t in range(1, n_z):
                copy(mine, mine, o_z + t, z_dev(t)).start()
            copy(mine, mine, o_y, y_peer).start()

    def o_forward():
        @pl.when(cy)
        def _():
            for t in range(1, n_z):
                came = head_block(wo, t)
                copy(came, came, o_z + t, z_dev(-t)).wait_recv()
                copy(came, came, o_y + t, y_peer).start()

    def o_finish():
        @pl.when(jnp.logical_not(cy))
        def _():
            for t in range(n_z):
                came = head_block(wo, t)
                copy(came, came, o_y + t, y_peer).wait_recv()

    def o_sent():
        @pl.when(cy)
        def _():
            mine = head_block(wo, 0)
            for t in range(1, n_z):
                copy(mine, mine, o_z + t, z_dev(t)).wait_send()
            for t in range(n_z):
                came = head_block(wo, t)
                copy(came, came, o_y + t, y_peer).wait_send()

    class TokenGather:
        def __init__(self, full):
            self.full = full
            self.sx, self.sc, self.sd = take(), take(), take()

        def at(self, j):
            return self.full.at[token_rows(j)]

        def start(self, own):
            self.own = own
            copy(own, self.at(s), self.sx, x_peer).start()
            copy(own, self.at(s), self.sc, core_peer).start()

        def forward(self):
            across = self.at((1 - x) * 2 + c)
            copy(across, across, self.sx, x_peer).wait_recv()
            copy(across, across, self.sd, core_peer).start()

        def take_step(self, t):
            @pl.when(t == 1)
            def _():
                came = self.at(x * 2 + 1 - c)
                copy(came, came, self.sc, core_peer).wait_recv()

            pl.when(t == 2)(self.forward)

            @pl.when(t == 3)
            def _():
                came = self.at((1 - x) * 2 + 1 - c)
                copy(came, came, self.sd, core_peer).wait_recv()

        def sent(self):
            copy(self.own, self.at(s), self.sx, x_peer).wait_send()
            copy(self.own, self.at(s), self.sc, core_peer).wait_send()
            across = self.at((1 - x) * 2 + c)
            copy(across, across, self.sd, core_peer).wait_send()

        def finish(self):
            for index, j in ((self.sc, x * 2 + 1 - c), (self.sd, (1 - x) * 2 + 1 - c)):
                copy(self.at(j), self.at(j), index, core_peer).wait_recv()
            self.sent()

    class SeqSum:
        def __init__(self, partial, sb, cr, xr):
            self.partial, self.sb, self.cr, self.xr = partial, sb, cr, xr
            self.first, self.last = take(2), take()

        def to_core(self, slot):
            return copy(self.sb.at[slot], self.cr.at[slot], self.first + slot, core_peer)

        def to_chip(self):
            return copy(self.sb.at[2], self.xr, self.last, x_peer)

        def run(self, low=0, high=4):
            partial = self.partial

            def step(t, carry):
                away, slot = lax.rem(t, 2) == 0, lax.div(t, 2)
                if low < 2 < high:
                    pl.when(t == 2)(self.across)
                part = partial(jnp.where(t < 2, 1 - x, x) * 2 + jnp.where(away, 1 - c, c))

                @pl.when(away)
                def _():
                    self.sb[slot] = part.astype(BF16)
                    self.to_core(slot).start()

                @pl.when(jnp.logical_not(away))
                def _():
                    pf[slot] = part

                return carry

            lax.fori_loop(low, high, step, 0)

        def across(self):
            copy(self.cr.at[0], self.cr.at[0], self.first, core_peer).wait_recv()
            self.sb[2] = (pf[0] + self.cr[0].astype(F32)).astype(BF16)
            self.to_chip().start()

        def finish(self):
            copy(self.cr.at[1], self.cr.at[1], self.first + 1, core_peer).wait_recv()
            copy(self.xr, self.xr, self.last, x_peer).wait_recv()
            for slot in range(2):
                self.to_core(slot).wait_send()
            self.to_chip().wait_send()
            return pf[1] + self.cr[1].astype(F32) + self.xr[...].astype(F32)

    class Reduce:
        def __init__(self, grad, yr, zr, zs, fs, out):
            self.grad, self.yr, self.zr, self.zs, self.fs, self.out = grad, yr, zr, zs, fs, out
            self.most = rb if zs is None else rb - SLIVER
            self.width = grad.shape[1]
            self.sy, self.sz, self.sp, self.ss = take(n_z), take(n_z), take(4), take(n_z)

        def kept(self, j):
            return w1.at[pl.ds(pl.multiple_of(self.out + j * PIECE, 16), PIECE), 0 : self.width]

        def at(self, zb, side):
            return img_rows(zb * 2 + side)

        def across_y(self):
            for u in (3, 2, 1):
                b = near[u] * 2 + 1 - y
                send(self.grad.at[most_rows(b, self.most)], self.yr.at[u, 0 : self.most], self.sy + u, y_peer)
                if self.zs is not None:
                    send(self.grad.at[sliver_rows(b)], self.zs.at[z], self.ss + u, z_to(near[u]), self.ss + z)
            if self.zs is None:
                send(self.grad.at[img_rows(z * 2 + 1 - y)], self.yr.at[0], self.sy, y_peer)

        def across_last(self):
            b = z * 2 + 1 - y
            part = self.grad[sliver_rows(b), :].astype(F32)
            for u in (1, 2, 3):
                zb = near[u]
                copy(self.zs.at[zb], self.zs.at[zb], self.ss, z_to(zb), self.ss + zb).wait_recv()
                part += self.zs[zb].astype(F32)
            self.grad[sliver_rows(b), :] = part.astype(BF16)
            send(self.grad.at[img_rows(b)], self.yr.at[0], self.sy, y_peer)

        def along_z(self, *steps):
            for u in steps:
                came = self.yr.at[u, 0 : self.most]
                copy(came, came, self.sy + u, y_peer).wait_recv()
                mine, most = self.at(near[u], y), most_rows(near[u] * 2 + y, self.most)
                added = self.yr[u, 0 : self.most, :].astype(F32)
                self.grad[most, :] = (self.grad[most, :].astype(F32) + added).astype(BF16)
                if u < 3:
                    send(self.grad.at[mine], self.zr.at[z], self.sz + u, z_to(near[u]), self.sz + z)
                else:

                    @pl.when(jnp.logical_not(middle))
                    def _():
                        self.far().start()

        def far(self):
            rows_far = self.grad.at[self.at(near[3], y)]
            return copy(rows_far, self.zr.at[near[1]], self.sz + 3, z_to(near[1]), self.sz + near[1])

        def onward(self):
            rows_far = self.grad.at[self.at(near[3], y)]
            return copy(rows_far, self.zr.at[z], self.sz + 3, z_to(near[3]), self.sz + z)

        def relay(self):
            @pl.when(middle)
            def _():
                mine = self.at(near[3], y)
                copy(self.zr.at[z], self.zr.at[z], self.sz, z_to(end), self.sz + z).wait_recv()
                self.grad[mine, :] = (self.grad[mine, :].astype(F32) + self.zr[z].astype(F32)).astype(BF16)
                self.onward().start()

        def came_z(self, u):
            zb = near[u]
            copy(self.zr.at[zb], self.zr.at[zb], self.sz, z_to(zb), self.sz + zb).wait_recv()
            tmp[0:rb, 0 : self.width] += self.zr[zb].astype(F32)

        def pieces(self):
            copy(self.yr.at[0], self.yr.at[0], self.sy, y_peer).wait_recv()
            tmp[0:rb, 0 : self.width] = self.grad[self.at(z, y), :].astype(F32) + self.yr[0].astype(F32)
            self.came_z(1)
            self.came_z(2)

            @pl.when(middle)
            def _():
                self.came_z(3)

            part = rb // 4
            for j in range(4):
                self.fs[j] = tmp[part * j : part * j + PIECE, 0 : self.width].astype(BF16)
            pltpu.make_async_copy(self.fs.at[s], self.kept(s), lsem.at[4]).start()
            for t in (1, 2, 3):
                to = s_at(t)
                send(self.fs.at[to], self.kept(s), self.sp + t, (i, to))
            pltpu.make_async_copy(self.fs.at[s], self.kept(s), lsem.at[4]).wait()

        def sent(self):
            @pl.when(middle)
            def _():
                self.onward().wait_send()

            @pl.when(jnp.logical_not(middle))
            def _():
                self.far().wait_send()

        def finish(self):
            for t in (1, 2, 3):
                came = self.kept(s_at(-t))
                copy(came, came, self.sp + t, (i, s_at(-t))).wait_recv()

        def piece_tiles(self, j):
            row = self.out + j * PIECE
            return [
                w1[row : row + PIECE, t * LANES : (t + 1) * LANES].astype(F32) for t in range(self.width // LANES)
            ]

        def publish(self, tiles, out):
            for t, tile in enumerate(tiles):
                width = min(LANES, out.shape[1] - t * LANES)
                out[:, t * LANES : t * LANES + width] = tile[0:own, 0:width]

        def publish_wide(self, out):
            tiles = {}
            for j in range(4):
                tile, offset = divmod(j * f, LANES)
                for t, part in enumerate(self.piece_tiles(j)):
                    if offset:
                        part = pltpu.roll(part, offset, 1)
                    for to, where in ((tile + t, piece_lanes >= offset), (tile + t + 1, piece_lanes < offset)):
                        if to * LANES < 4 * f:
                            kept = jnp.where(where, part, 0.0)
                            tiles[to] = tiles[to] + kept if to in tiles else kept
            self.publish([tiles[to] for to in sorted(tiles)], out)

        def publish_heads(self, out):
            pieces = [self.piece_tiles(j) for j in range(4)]
            tiles = []
            for kind in range(3):
                parts = []
                for head in range(d // hd):
                    which, to = divmod(head, 4)
                    part = lane_window(pieces[2 * (to % 2) + to // 2], (4 * kind + which) * hd, hd, piece_lanes)
                    parts.append(jnp.where(piece_lanes < hd, part, 0.0))
                tiles += pack_lanes(parts, hd, piece_lanes)
            self.publish(tiles, out)

    reduce_2 = Reduce(g2, y2, z2, s2, r2, 0)
    reduce_1 = Reduce(g1, y1, z1, s1, r1, 4 * PIECE)
    reduce_q = Reduce(gq, yq, zq, None, rq, 8 * PIECE)
    go = wo
    ro_y, ro_z, ro_p = take(n_z), take(n_z), take()

    def ro_across_y():
        @pl.when(jnp.logical_not(cy))
        def _():
            for t in (*range(1, n_z), 0):
                copy(head_block(go, -t), yo.at[t], ro_y + t, y_peer).start()

    def ro_along_z():
        @pl.when(cy)
        def _():
            for t in range(1, n_z):
                copy(yo.at[t], yo.at[t], ro_y + t, y_peer).wait_recv()
                mine = pl.ds(pl.multiple_of(z_at(t) * LANES, LANES), HEAD_ROWS)
                go[mine, :] = (go[mine, :].astype(F32) + yo[t].astype(F32)).astype(BF16)
                copy(go.at[mine], zo.at[t - 1], ro_z + t, z_dev(t)).start()

    def ro_pieces():
        @pl.when(cy)
        def _():
            copy(yo.at[0], yo.at[0], ro_y, y_peer).wait_recv()
            mine = pl.ds(pl.multiple_of(z * LANES, LANES), HEAD_ROWS)
            total = go[mine, :].astype(F32) + yo[0].astype(F32)
            for t in range(1, n_z):
                copy(zo.at[t - 1], zo.at[t - 1], ro_z + t, z_dev(-t)).wait_recv()
                total += zo[t - 1].astype(F32)
            tmp[0:HEAD_ROWS, :] = total
            for j in range(2):
                ro[j] = tmp[own * j : own * j + PIECE, :].astype(BF16)
            pltpu.make_async_copy(ro.at[c], o_fo, lsem.at[5]).start()
            copy(ro.at[1 - c], o_fo, ro_p, core_peer).start()
            pltpu.make_async_copy(ro.at[c], o_fo, lsem.at[5]).wait()

    def ro_finish():
        @pl.when(cy)
        def _():
            for t in range(1, n_z):
                copy(head_block(go, -t), zo.at[t - 1], ro_z + t, z_dev(t)).wait_send()
            copy(ro.at[1 - c], o_fo, ro_p, core_peer).wait_send()

        @pl.when(jnp.logical_not(cy))
        def _():
            for t in range(n_z):
                copy(head_block(go, -t), yo.at[t], ro_y + t, y_peer).wait_send()
            copy(o_fo, o_fo, ro_p, core_peer).wait_recv()

    def arriving(t):
        return jnp.where(t < 2, x, 1 - x) * 2 + jnp.where(lax.rem(t, 2) == 0, c, 1 - c)

    def real_rows(j, width):
        t = lax.broadcasted_iota(jnp.int32, (BLOCK, width), 0)
        position = j * slice_len + t
        return (t < slice_len) & (position >= off_ref[0]) & (position < off_ref[0] + VALID)

    def padded(rows_in):
        pf[0, BLOCK - 16 : BLOCK, :] = jnp.zeros((16, d), F32)
        pf[0, 0:slice_len, :] = rows_in[0]
        return pf[0]

    tokens_in, cot_in = TokenGather(xs), TokenGather(gc)
    piece_lanes = lane_ids(PIECE)
    three = [Tiles(dg, PIECE * n, PIECE, PIECE) for n in range(3)]
    for n in range(3):
        three[n].fill(w_qkv.at[:, n * d : (n + 1) * d])
    small = Tiles(dg, 3 * PIECE, PIECE, PIECE)
    dg[3 * PIECE : 3 * PIECE + LANES, 0:LANES] = jnp.zeros((LANES, LANES), F32)
    dg[3 * PIECE : 3 * PIECE + 2, 0:own] = gains[...].astype(F32)
    dg[3 * PIECE + 2 : 3 * PIECE + 8, 0:own] = biases[...].astype(F32)
    dg[3 * PIECE : 3 * PIECE + LANES, 0:LANES] = dg[3 * PIECE : 3 * PIECE + LANES, 0:LANES].T
    for to in range(4):
        parts = []
        for n in range(12):
            kind, which = divmod(n, 4)
            head = 4 * which + 2 * (to % 2) + to // 2
            part = lane_window(three[kind], head * hd, hd, piece_lanes)
            parts.append(jnp.where(piece_lanes < hd, part, 0.0))
        tiles = pack_lanes(parts, hd, piece_lanes)
        tiles[-1] = tiles[-1] + pltpu.roll(small[0], 12 * hd % LANES, 1)
        for at, tile in enumerate(tiles):
            yq[to, 0:PIECE, at * LANES : (at + 1) * LANES] = tile.astype(BF16)
    pl.semaphore_wait(barrier, len(partners))
    gather_q.pieces()
    pf[0, BLOCK - 16 : BLOCK, :] = jnp.zeros((16, d), F32)
    pf[0, 0:slice_len, :] = tok[0].astype(F32)
    xs[token_rows(s), :] = pf[0].astype(BF16)
    tokens_in.start(xs.at[token_rows(s)])
    out_rows = Tiles(dg, 12 * PIECE, PIECE, PIECE)
    out_rows.fill(w_out)
    for at in range(d // LANES):
        yo[0, 0:PIECE, at * LANES : (at + 1) * LANES] = out_rows[at].astype(BF16)
    o_start()
    for weights, first, pieces in ((w_fc1, 4, y1), (w_fc2, 8, y2)):
        wide = Tiles(dg, first * PIECE, PIECE, PIECE)
        wide.fill(weights)
        for to in range(4):
            for at in range(w1.shape[1] // LANES):
                start = to * f + at * LANES
                width = min(LANES, f - at * LANES)
                part = lane_window(wide, start, width, piece_lanes)
                if width < LANES:
                    part = jnp.where(piece_lanes < width, part, 0.0)
                pieces[to, 0:PIECE, at * LANES : (at + 1) * LANES] = part.astype(BF16)
        (gather_1 if first == 4 else gather_2).pieces()
    pf[1, BLOCK - 16 : BLOCK, :] = jnp.zeros((16, d), F32)
    pf[1, 0:slice_len, :] = cot[0].astype(F32)
    gc[token_rows(s), :] = jnp.where(real_rows(s, d), pf[1], 0.0).astype(BF16)
    cot_in.start(gc.at[token_rows(s)])
    sms[0] = jnp.zeros(sms.shape[1:], F32)
    shs[0] = jnp.zeros(shs.shape[1:], F32)
    tmp[...] = jnp.zeros(tmp.shape, F32)

    gather_q.assemble()
    gather_q.along_z()
    gather_q.across_y()
    o_assemble()
    o_along_z()
    gather_q.forward(1)
    tokens_in.forward()
    gather_1.assemble()
    gather_q.slivers()
    gather_q.forward(2)
    gather_q.relay()
    gather_1.along_z()
    gather_1.across_y()
    gather_2.assemble()
    gather_q.forward_far()
    o_forward()
    gather_2.across_y()
    cot_in.forward()
    tokens_in.finish()
    gather_q.finish()

    packed = 3 * 4 * hd
    base = packed // LANES * LANES
    columns = wq[:, base : base + LANES].astype(F32)
    prm[...] = columns.T[packed - base : packed - base + 8, :]
    one_lane = lane_ids(1)
    for which, row in ((0, 3), (1, 4)):
        tiles = [prm[row : row + 1, LANES * t : LANES * (t + 1)] for t in range(d // LANES)]
        for head in range(d // hd):
            bh[which, head : head + 1, :] = lane_window(tiles, head * hd, hd, one_lane)
    gain_one, gain_two, shift_one = prm[0:1, :], prm[1:2, :], prm[2:3, :]
    bias_out, shift_two, bias_two = prm[5:6, :], prm[6:7, :], prm[7:8, :]

    lanes = lane_ids(BLOCK)

    def project(j, carry):
        hat, _ = normalize(xs[token_rows(j), :].astype(F32))
        low = (hat * gain_one + shift_one).astype(BF16)
        h1[token_rows(j), :] = low
        wide = mm(low, wq[...], NN)
        tiles = [wide[:, LANES * t : LANES * (t + 1)] for t in range(qw // LANES)]
        key_low = jnp.where(real_rows(j, LANES), 0.0, mask_low)
        for n in range(12):
            kind, head = divmod(n, 4)
            part = lane_window(tiles, n * hd, hd, lanes)
            if kind != 1:
                part = part + bh[kind // 2, pl.ds(4 * head + k, 1), :]
            beside = key_low if kind == 1 else jnp.ones_like(part)
            part = jnp.where(lanes < hd, part, jnp.where(lanes == hd, beside, 0.0))
            qkv[n, token_rows(j), :] = part.astype(BF16)
        return carry

    lax.fori_loop(0, 4, project, 0)
    gather_1.slivers()
    gather_2.along_z()
    half = rows // 2
    sublanes = lax.broadcasted_iota(jnp.int32, (LANES, half), 0)

    def attend(step, carry):
        head, part = lax.rem(step, 4), jnp.where(step < 4, 1 - x, x)
        at = pl.ds(pl.multiple_of(part * half, LANES), half)
        scores = mm(qkv[4 + head], qkv[head, at, :], NT)
        top = jnp.max(scores, 0, keepdims=True)
        weights = jnp.exp((scores - top) * scale).astype(BF16)
        summed = mm(qkv[8 + head], weights, TN)
        total = summed[hd : hd + 1, :]
        result = jnp.where(sublanes < hd, summed / total, 0.0)
        att_t[head, :, at] = result.astype(BF16)
        attm[at, pl.ds(pl.multiple_of(head * LANES, LANES), LANES)] = result.T.astype(BF16)
        lse[head, :, at] = top * scale + jnp.log(total)
        return carry

    lax.fori_loop(0, 4, attend, 0)
    gather_1.forward(1)
    o_finish()
    sum_one = SeqSum(lambda j: mm(attm[token_rows(j), :], wo[...], NN), sb_a, cr_a, xr_a)
    sum_one.run(0, 2)
    sum_one.across()
    lax.fori_loop(4, 8, attend, 0)
    sum_one.run(2, 4)
    gather_1.relay()
    gather_2.slivers()
    gather_1.forward(2)
    cot_in.finish()
    bias_parts = Tiles(dg, 14 * PIECE, 8, 8)
    bias_parts.fill(fc1_bias)
    row_lanes = lane_ids(8)
    for at in range(w1.shape[1] // LANES):
        width = min(LANES, f - at * LANES)
        mine = jnp.zeros((8, LANES), F32)
        for to in range(4):
            part = lane_window(bias_parts, to * f + at * LANES, width, row_lanes)
            mine = jnp.where(s == to, part, mine)
        fb[:, at * LANES : (at + 1) * LANES] = jnp.where(row_lanes < width, mine, 0.0)[0:1]

    gather_1.forward_far()
    branch = sum_one.finish()
    middle_rows = xs[token_rows(s), :].astype(F32) + branch + bias_out
    o_mixed[0] = middle_rows[0:slice_len]
    hat, _ = normalize(middle_rows)
    h2[token_rows(s), :] = (hat * gain_two + shift_two).astype(BF16)
    h2_in = TokenGather(h2)
    h2_in.start(h2.at[token_rows(s)])
    gather_2.forward(1)
    gather_1.finish()

    slope = (2.0 / 3.141592653589793) ** 0.5

    def widen(t, carry):
        h2_in.take_step(t)
        j = arriving(t)
        pre = mm(h2[token_rows(j), :], w1[...], NN) + fb[...]
        square = pre * pre
        curve = jnp.tanh(slope * pre * (1.0 + 0.044715 * square))
        half = 0.5 + 0.5 * curve
        act[token_rows(j), :] = (pre * half).astype(BF16)
        dg[token_rows(j), :] = half + 0.5 * slope * pre * (1.0 - curve * curve) * (1.0 + 0.134145 * square)
        return carry

    lax.fori_loop(0, 2, widen, 0)
    gather_2.forward(2)
    gather_2.relay()
    lax.fori_loop(2, 4, widen, 0)
    h2_in.sent()
    gather_2.forward_far()

    def column_products(left, right, out):
        def step(t, carry):
            at = pl.ds(pl.multiple_of(t * LANES, LANES), LANES)
            out[at, :] = mm(left[:, at], right[...], TN).astype(BF16)
            return carry

        lax.fori_loop(0, left.shape[1] // LANES, step, 0)

    column_products(gc, act, g2)
    reduce_2.across_y()
    gather_2.finish()

    def hidden_back(j):
        at = token_rows(j)
        low = (mm(gc[at, :], w2[...], NN) * dg[at, :]).astype(BF16)
        gp[at, :] = low
        column = jnp.sum(low.astype(F32), 0, keepdims=True)
        sms[0, 6:7, :] += column
        return mm(low, w1[...], NT)

    gather_1.sent()
    sum_two = SeqSum(hidden_back, sb_a, cr_a, xr_a)
    sum_two.run()
    reduce_2.across_last()
    column_products(h2, gp, g1)
    reduce_1.across_y()
    reduce_2.along_z(3)
    reduce_2.along_z(2)
    grad_h = sum_two.finish()
    hat, inverse = normalize(padded(o_mixed))
    kept = gc[token_rows(s), :].astype(F32)
    grad_x = kept + norm_back(grad_h, gain_two, hat, inverse)
    o_gtok[0] = grad_x[0:slice_len]
    low = grad_x.astype(BF16)
    sms[0, 1:2, :] = jnp.sum(grad_h * hat, 0, keepdims=True)
    sms[0, 4:5, :] = jnp.sum(grad_h, 0, keepdims=True)
    sms[0, 5:6, :] = jnp.sum(kept, 0, keepdims=True)
    sms[0, 3:4, :] = jnp.sum(low.astype(F32), 0, keepdims=True)
    gc[token_rows(s), :] = low
    gb_in = TokenGather(gc)
    gb_in.start(gc.at[token_rows(s)])

    sum_three = SeqSum(lambda j: mm(act[token_rows(j), :], w2[...], NT), sb_b, cr_b, xr_b)
    sum_three.run()
    reduce_2.along_z(1)
    reduce_1.across_last()

    def attended_back(t, carry):
        gb_in.take_step(t)
        j = arriving(t)
        attm[token_rows(j), :] = mm(gc[token_rows(j), :], wo[...], NT).astype(BF16)
        return carry

    lax.fori_loop(0, 4, attended_back, 0)
    gb_in.sent()

    o_sent()

    def out_products(head, carry):
        at = pl.ds(pl.multiple_of(head * LANES, LANES), LANES)
        go[at, :] = mm(att_t[head], gc[...], NN).astype(BF16)
        return carry

    lax.fori_loop(0, 4, out_products, 0)
    ro_across_y()
    reduce_2.relay()

    wide_lanes = lane_ids(rows)
    chunk_lanes = lane_ids(chunk)

    def attend_back(head, carry):
        grad_k = jnp.zeros((rows, LANES), F32)
        grad_v = jnp.zeros((rows, LANES), F32)
        grad_q = []
        for part in range(rows // chunk):
            at = slice(part * chunk, (part + 1) * chunk)
            query, grad_out = qkv[head, at, :], attm[at, pl.ds(pl.multiple_of(head * LANES, LANES), LANES)]
            scores = mm(qkv[4 + head], query, NT)
            probs = jnp.exp(scores * scale - lse[head, :, at])
            grad_p = mm(qkv[8 + head], grad_out, NT)
            delta = jnp.sum(probs * grad_p, 0, keepdims=True)
            grad_s = (probs * (grad_p - delta)).astype(BF16)
            grad_k += mm(grad_s, query, NN)
            grad_v += mm(probs.astype(BF16), grad_out, NN)
            grad_q.append(mm(qkv[4 + head], grad_s, TN))
        for part in range(rows // chunk):
            at = slice(part * chunk, (part + 1) * chunk)
            low = jnp.where(chunk_lanes < hd, grad_q[part].T * scale, 0.0).astype(BF16)
            qkv[head, at, :] = low
            shs[0, pl.ds(4 * head + k, 1), :] += jnp.sum(low.astype(F32), 0, keepdims=True)
        qkv[4 + head] = jnp.where(wide_lanes < hd, grad_k * scale, 0.0).astype(BF16)
        low = grad_v.astype(BF16)
        qkv[8 + head] = low
        shs[0, pl.ds(16 + 4 * head + k, 1), :] = jnp.sum(low.astype(F32), 0, keepdims=True)
        return carry

    reduce_1.along_z(3)
    lax.fori_loop(0, 2, attend_back, 0)
    reduce_1.along_z(2)
    lax.fori_loop(2, 4, attend_back, 0)
    reduce_1.along_z(1)
    reduce_1.relay()

    branch = sum_three.finish()
    o_mixed[0] = jnp.where(real_rows(s, d), padded(o_mixed) + branch + bias_two, 0.0)[0:slice_len]
    gpj = h2.at[:, 0:qw]

    def pack(j, carry):
        parts = [qkv[n, token_rows(j), :].astype(F32) for n in range(12)]
        for to, tile in enumerate(pack_lanes(parts, hd, lanes)):
            gpj[token_rows(j), LANES * to : LANES * (to + 1)] = tile.astype(BF16)
        return carry

    lax.fori_loop(0, 4, pack, 0)

    def tokens_back(j):
        part = mm(gpj[token_rows(j), :], wq[...], NT)
        hat, _ = normalize(xs[token_rows(j), :].astype(F32))
        sms[0, 0:1, :] += jnp.sum(part * hat, 0, keepdims=True)
        sms[0, 2:3, :] += jnp.sum(part, 0, keepdims=True)
        return part

    sum_four = SeqSum(tokens_back, sb_a, cr_a, xr_a)
    sum_four.run()
    sm_at, sh_at = take(7), take(7)

    def vectors(stage, slots, devices):
        for slot, device in zip(slots, devices, strict=True):
            send(sms.at[stage], smr.at[slot], sm_at + slot, device)
            send(shs.at[stage], shr.at[slot], sh_at + slot, device)

    def vectors_sum(stage, slots, devices):
        for slot, device in zip(slots, devices, strict=True):
            copy(smr.at[slot], smr.at[slot], sm_at + slot, device).wait_recv()
            copy(shr.at[slot], shr.at[slot], sh_at + slot, device).wait_recv()
        total, heads = sms[stage], shs[stage]
        for slot in slots:
            total += smr[slot]
            heads += shr[slot]
        return total, heads

    z_to_all, z_from_all = [z_dev(t) for t in (1, 2, 3)], [z_dev(-t) for t in (1, 2, 3)]
    s_to_all, s_from_all = [(i, s_at(t)) for t in (1, 2, 3)], [(i, s_at(-t)) for t in (1, 2, 3)]
    vectors(0, (0,), (y_peer,))
    column_products(h1, gpj, gq)
    reduce_q.across_y()
    sms[1], shs[1] = vectors_sum(0, (0,), (y_peer,))
    vectors(1, (1, 2, 3), z_to_all)
    ro_along_z()
    reduce_2.pieces()
    reduce_q.along_z(3, 2)
    reduce_q.relay()
    grad_h = sum_four.finish()
    hat, inverse = normalize(xs[token_rows(s), :].astype(F32))
    o_gtok[0] = (padded(o_gtok) + norm_back(grad_h, gain_one, hat, inverse))[0:slice_len]
    reduce_q.along_z(1)
    sms[2], shs[2] = vectors_sum(1, (1, 2, 3), z_from_all)
    vectors(2, (4, 5, 6), s_to_all)
    reduce_1.pieces()
    reduce_2.finish()
    reduce_2.publish_wide(o_2)
    ro_pieces()
    reduce_q.pieces()
    reduce_1.finish()
    reduce_1.publish_wide(o_1)
    summed_rows, by_head = vectors_sum(2, (4, 5, 6), s_from_all)
    prm[pl.ds(s, 1), :] = sms[2, 6:7, :]
    for t in (1, 2, 3):
        prm[pl.ds(s_at(-t), 1), :] = smr[3 + t, 6:7, :]
    mine = smr.at[1]
    for to, row in enumerate((0, 1, 2, None, None, 3, 4, 5)):
        if row is not None:
            mine[to : to + 1, :] = summed_rows[row : row + 1, :]
    for which in range(2):
        heads = [by_head[16 * which + head : 16 * which + head + 1, :] for head in range(d // hd)]
        for to, tile in enumerate(pack_lanes(heads, hd, one_lane)):
            mine[3 + which : 4 + which, to * LANES : (to + 1) * LANES] = tile
    start = (i * 4 + s) * own
    turned = pltpu.roll(mine[0:8, :], lax.rem(d - start, d), 1)
    o_gains[...] = turned[0:2, 0:own]
    o_biases[...] = turned[2:8, 0:own]
    spread = {}
    for j in range(4):
        tile, offset = divmod(j * f, LANES)
        for t in range(w1.shape[1] // LANES):
            part = prm[j : j + 1, t * LANES : (t + 1) * LANES]
            if offset:
                part = pltpu.roll(part, offset, 1)
            for to, where in ((tile + t, one_lane >= offset), (tile + t + 1, one_lane < offset)):
                if to * LANES < 4 * f:
                    kept = jnp.where(where, part, 0.0)
                    spread[to] = spread[to] + kept if to in spread else kept
    for to, tile in spread.items():
        width = min(LANES, 4 * f - to * LANES)
        o_fb[:, to * LANES : to * LANES + width] = tile[:, 0:width]
    ro_finish()
    reduce_q.finish()
    reduce_q.publish_heads(o_q)
    for part in (gather_q, gather_2, reduce_q, reduce_1, reduce_2):
        part.sent()
    for made in sends:
        made.wait_send()


def hand_over(mixed, tokens, g_qkv, g_1, g_2, g_out, g_gains, g_biases, *outs):
    o_mixed, o_tokens, o_qkv, o_1, o_2, o_out, o_gains, o_biases = outs
    o_qkv[...] = g_qkv[...]
    o_1[...] = g_1[...]
    o_2[...] = g_2[...]
    o_mixed[:, 0, :] = mixed[0]
    o_tokens[:, 0, :] = tokens[0]
    o_out[...] = g_out[0 : o_out.shape[0], :].astype(F32)
    o_gains[...] = g_gains[...]
    o_biases[...] = g_biases[...]


def whole_layer(tokens, offsets, w_qkv, w_out, w_fc1, w_fc2, gains, biases, fc1_bias, cotangent):
    _, slice_len, d = tokens.shape
    hd = d // HEADS
    own, wide = w_fc1.shape
    f = wide // 4
    f_pad = -(-f // LANES) * LANES
    packed = 12 * hd
    qw = -(-(packed + 8) // LANES) * LANES
    n_z = lax.axis_size("img") // 2
    rb = own * 4
    rows = 4 * BLOCK

    hbm = pl.BlockSpec(memory_space=pl.ANY)
    vmem = pl.BlockSpec(memory_space=pltpu.VMEM)
    outs = [
        ((1, slice_len, d), F32, vmem),
        ((1, slice_len, d), F32, vmem),
        ((own, 3 * d), F32, vmem),
        ((PIECE, d), BF16, hbm),
        ((own, wide), F32, vmem),
        ((own, wide), F32, vmem),
        ((1, wide), F32, vmem),
        ((2, own), F32, vmem),
        ((6, own), F32, vmem),
    ]
    low = [
        (d, qw), (4 * LANES, d), (d, f_pad), (d, f_pad),
        (4, PIECE, qw), (2, PIECE, d), (4, PIECE, f_pad), (4, PIECE, f_pad),
    ]
    scratch = [pltpu.VMEM(shape, BF16) for shape in low]
    scratch += [pltpu.VMEM((160, max(d, f_pad)), F32)]
    scratch += [pltpu.VMEM((rows, w), BF16) for w in (d, d, d, d, f_pad, f_pad)]
    scratch += [pltpu.VMEM((rows, f_pad), F32)]
    scratch += [
        pltpu.VMEM((12, rows, LANES), BF16),
        pltpu.VMEM((rows, 4 * LANES), BF16),
        pltpu.VMEM((4, LANES, rows), BF16),
        pltpu.VMEM((4, 1, rows), F32),
    ]
    scratch += [pltpu.VMEM(shape, BF16) for shape in ((d, f_pad), (d, f_pad), (d, qw))]
    scratch += [pltpu.VMEM((n_z, h, w), BF16) for h, w in ((rb, f_pad), (rb, f_pad), (HEAD_ROWS, d), (rb, qw))]
    scratch += [pltpu.VMEM((n_z, h, w), BF16) for h, w in ((rb, f_pad), (rb, f_pad), (HEAD_ROWS, d), (rb, qw))]
    scratch += [pltpu.VMEM((n_z, SLIVER, w), BF16) for w in (f_pad, f_pad)]
    for _ in range(2):
        scratch += [pltpu.VMEM((n, BLOCK, d), BF16) for n in (3, 2)] + [pltpu.VMEM((BLOCK, d), BF16)]
    scratch += [
        pltpu.VMEM((2, BLOCK, d), F32),
        pltpu.VMEM((1, f_pad), F32),
        pltpu.VMEM((8, d), F32),
        pltpu.VMEM((2, 16, LANES), F32),
        pltpu.VMEM((3, 8, d), F32),
        pltpu.VMEM((7, 8, d), F32),
        pltpu.VMEM((3, 32, LANES), F32),
        pltpu.VMEM((7, 32, LANES), F32),
        pltpu.SemaphoreType.DMA((200,)),
        pltpu.SemaphoreType.DMA((200,)),
        pltpu.SemaphoreType.DMA((8,)),
    ]
    mixed, grad_tokens, gq, go, g1, g2, g_fb, g_gains, g_biases = pl.pallas_call(
        partial(layer_kernel, (slice_len, d, hd, f, qw, n_z)),
        out_shape=[jax.ShapeDtypeStruct(shape, kind) for shape, kind, _ in outs],
        in_specs=[pl.BlockSpec(memory_space=pltpu.SMEM)] + [vmem] * 9,
        out_specs=[spec for _, _, spec in outs],
        scratch_shapes=scratch,
        compiler_params=pltpu.CompilerParams(
            collective_id=0, has_side_effects=True, vmem_limit_bytes=VMEM_BYTES
        ),
    )(offsets, w_qkv, w_out, w_fc1, w_fc2, gains.T, biases.T, fc1_bias[None], tokens, cotangent)

    rows_out = jax.ShapeDtypeStruct((slice_len, 1, d), F32)
    same = [jax.ShapeDtypeStruct(made.shape, F32) for made in (gq, g1, g2)]
    rest = [jax.ShapeDtypeStruct(shape, F32) for shape in ((own, d), (2, own), (6, own))]
    mixed, grad_tokens, gq, g1, g2, go, g_gains, g_biases = pl.pallas_call(
        hand_over,
        out_shape=[rows_out, rows_out, *same, *rest],
        in_specs=[vmem] * 8,
        out_specs=[vmem] * 8,
    )(mixed, grad_tokens, gq, g1, g2, go, g_gains, g_biases)
    mixed, grad_tokens = mixed.reshape(tokens.shape), grad_tokens.reshape(tokens.shape)
    return mixed, grad_tokens, gq, go, g1, g2, g_gains.T, g_biases.T, g_fb.reshape(wide)


def local(tokens, offsets, w_qkv, w_out, w_fc1, w_fc2, gains, biases, fc1_bias, cotangent):
    images_here, slice_len, model_width = tokens.shape
    head_count = HEADS
    head_dim = model_width // head_count
    length = slice_len * lax.axis_size("seq")
    row_count = images_here * slice_len
    score_scale = head_dim ** (-0.5)
    gathered = (
        lax.all_gather(w_qkv, ("img", "seq"), axis=0, tiled=True),
        lax.all_gather(w_out, ("img", "seq"), axis=0, tiled=True),
        lax.all_gather(w_fc1, ("img", "seq"), axis=0, tiled=True),
        lax.all_gather(w_fc2, ("img", "seq"), axis=0, tiled=True),
        lax.all_gather(gains, ("img", "seq"), axis=0, tiled=True),
        lax.all_gather(biases, ("img", "seq"), axis=0, tiled=True),
    )
    wide_qkv, wide_out, wide_fc1, wide_fc2, gain_all, bias_all = gathered
    gain_cols = gain_all.astype(jnp.float32)
    bias_cols = bias_all.astype(jnp.float32)
    starts = offsets[:, None]
    positions = lax.axis_index("seq") * slice_len + jnp.arange(slice_len, dtype=jnp.int32)
    own_valid = (positions[None, :] >= starts) & (positions[None, :] < starts + VALID)
    row_valid = own_valid.astype(jnp.float32)
    key_pos = jnp.arange(length, dtype=jnp.int32)
    key_valid = (key_pos[None, :] >= starts) & (key_pos[None, :] < starts + VALID)
    inputs = tokens.astype(jnp.float32).reshape(row_count, model_width)
    h_one, norm_one_back = jax.vjp(layer_norm, inputs, gain_cols[:, 0], bias_cols[:, 0])
    h_one_low = h_one.astype(jnp.bfloat16)
    qkv_bias = jnp.concatenate([bias_cols[:, 1], jnp.zeros_like(bias_cols[:, 1]), bias_cols[:, 2]])
    projected = (
        jnp.dot(h_one_low, wide_qkv, preferred_element_type=jnp.float32) + qkv_bias
    ).astype(jnp.bfloat16)
    query_rows = projected[:, :model_width]
    key_rows = projected[:, model_width : 2 * model_width].reshape(
        images_here, slice_len, model_width
    )
    value_rows = projected[:, 2 * model_width :].reshape(images_here, slice_len, model_width)
    keys_all, values_all = (
        lax.all_gather(key_rows, "seq", axis=1, tiled=True),
        lax.all_gather(value_rows, "seq", axis=1, tiled=True),
    )
    query_heads = split_heads(query_rows, images_here, slice_len, head_count, head_dim)
    key_heads = split_heads(keys_all, images_here, length, head_count, head_dim)
    value_heads = split_heads(values_all, images_here, length, head_count, head_dim)

    def head_scores(head_query_rows, head_key_rows, mask):
        scores = (
            jnp.einsum(
                "asl,aul->asu", head_query_rows, head_key_rows, preferred_element_type=jnp.float32
            )
            * score_scale
        )
        return jnp.where(mask[:, None, :], scores, masked_score)

    def forward_head(head_args):
        head_query_rows, head_key_rows, head_value_rows = head_args
        scores = head_scores(head_query_rows, head_key_rows, key_valid)
        maxima = jnp.max(scores, -1, keepdims=True)
        exponent = jnp.exp(scores - maxima)
        totals_row = jnp.sum(exponent, -1, keepdims=True)
        probs = exponent / totals_row
        attended_head = jnp.einsum(
            "owz,ozf->owf",
            probs.astype(jnp.bfloat16),
            head_value_rows,
            preferred_element_type=jnp.float32,
        )
        return (attended_head, maxima[..., 0] + jnp.log(totals_row[..., 0]))

    attended_heads, log_total = lax.map(forward_head, (query_heads, key_heads, value_heads))
    attended = join_heads(attended_heads).reshape(row_count, model_width).astype(jnp.bfloat16)
    middle = (
        inputs + jnp.dot(attended, wide_out, preferred_element_type=jnp.float32) + bias_cols[:, 3]
    )
    h_two, norm_two_back = jax.vjp(layer_norm, middle, gain_cols[:, 1], bias_cols[:, 4])
    h_two_low = h_two.astype(jnp.bfloat16)
    preact = jnp.dot(h_two_low, wide_fc1, preferred_element_type=jnp.float32) + fc1_bias.astype(
        jnp.float32
    )
    activated, gelu_back = jax.vjp(partial(jax.nn.gelu, approximate=True), preact)
    activated_low = activated.astype(jnp.bfloat16)
    branch_two = last_dot(activated_low, wide_fc2) + bias_cols[:, 5]
    valid_rows = row_valid.reshape(row_count, 1)
    mixed = (valid_rows * (middle + branch_two)).reshape(images_here, slice_len, model_width)
    wide_qkv, wide_out, wide_fc1, wide_fc2 = (
        lax.all_gather(w_qkv, ("img", "seq"), axis=0, tiled=True),
        lax.all_gather(w_out, ("img", "seq"), axis=0, tiled=True),
        lax.all_gather(w_fc1, ("img", "seq"), axis=0, tiled=True),
        lax.all_gather(w_fc2, ("img", "seq"), axis=0, tiled=True),
    )
    grad_output = cotangent.astype(jnp.float32).reshape(row_count, model_width) * valid_rows
    grad_branch = grad_output.astype(jnp.bfloat16)
    grad_bias_two = jnp.sum(grad_branch.astype(jnp.float32), 0)
    grad_fc2_local = row_dot(grad_branch, activated_low)
    grad_activated = jnp.dot(grad_branch, wide_fc2, preferred_element_type=jnp.float32)
    (grad_preact,) = gelu_back(grad_activated)
    preact_low = grad_preact.astype(jnp.bfloat16)
    grad_hidden_bias = jnp.sum(preact_low.astype(jnp.float32), 0)
    grad_fc1_local = row_dot(h_two_low, preact_low)
    grad_h_two = last_dot(preact_low, wide_fc1)
    grad_middle_norm, grad_gain_two, grad_shift_two = norm_two_back(grad_h_two)
    grad_middle = grad_output + grad_middle_norm
    grad_branch_one = grad_middle.astype(jnp.bfloat16)
    grad_out_bias = jnp.sum(grad_branch_one.astype(jnp.float32), 0)
    output_gradient_shard = row_dot(attended, grad_branch_one)
    grad_attended = last_dot(grad_branch_one, wide_out).astype(jnp.bfloat16)
    grad_att_heads = split_heads(grad_attended, images_here, slice_len, head_count, head_dim)

    def backward_head(head_args):
        head_query_rows, head_key_rows, head_value_rows, head_gradient, total_head = head_args
        scores = head_scores(head_query_rows, head_key_rows, key_valid)
        probs = jnp.exp(scores - total_head[..., None])
        grad_probs = jnp.einsum(
            "asl,aul->asu", head_gradient, head_value_rows, preferred_element_type=jnp.float32
        )
        grad_scores = probs * (grad_probs - jnp.sum(probs * grad_probs, -1, keepdims=True))
        reduced_scores = grad_scores.astype(jnp.bfloat16)
        grad_query = (
            jnp.einsum(
                "owz,ozf->owf", reduced_scores, head_key_rows, preferred_element_type=jnp.float32
            )
            * score_scale
        )
        grad_key = (
            jnp.einsum(
                "xzl,xzv->xlv", reduced_scores, head_query_rows, preferred_element_type=jnp.float32
            )
            * score_scale
        )
        grad_value = jnp.einsum(
            "xzl,xzv->xlv",
            probs.astype(jnp.bfloat16),
            head_gradient,
            preferred_element_type=jnp.float32,
        )
        return (grad_query, grad_key, grad_value)

    grad_q_heads, grad_k_heads, grad_v_heads = lax.map(
        backward_head, (query_heads, key_heads, value_heads, grad_att_heads, log_total)
    )
    key_gradient_rows, grad_values = (
        lax.psum_scatter(
            join_heads(grad_k_heads).astype(jnp.bfloat16), "seq", scatter_dimension=1, tiled=True
        ).astype(jnp.float32),
        lax.psum_scatter(
            join_heads(grad_v_heads).astype(jnp.bfloat16), "seq", scatter_dimension=1, tiled=True
        ).astype(jnp.float32),
    )
    grad_projected = jnp.concatenate(
        [
            join_heads(grad_q_heads).reshape(row_count, model_width),
            key_gradient_rows.reshape(row_count, model_width),
            grad_values.reshape(row_count, model_width),
        ],
        1,
    ).astype(jnp.bfloat16)
    grad_query_bias = jnp.sum(grad_projected[:, :model_width].astype(jnp.float32), 0)
    grad_value_bias = jnp.sum(grad_projected[:, 2 * model_width :].astype(jnp.float32), 0)
    grad_qkv_local = row_dot(h_one_low, grad_projected)
    grad_h_one = last_dot(grad_projected, wide_qkv)
    grad_input_norm, grad_gain_one, grad_shift_one = norm_one_back(grad_h_one)
    grad_tokens = (grad_middle + grad_input_norm).reshape(images_here, slice_len, model_width)
    grad_gain_local = jnp.stack([grad_gain_one, grad_gain_two], 1)
    grad_bias_local = jnp.stack(
        [
            grad_shift_one,
            grad_query_bias,
            grad_value_bias,
            grad_out_bias,
            grad_shift_two,
            grad_bias_two,
        ],
        1,
    )
    owned = (
        lax.psum_scatter(grad_qkv_local, ("img", "seq"), scatter_dimension=0, tiled=True),
        lax.psum_scatter(output_gradient_shard, ("img", "seq"), scatter_dimension=0, tiled=True),
        lax.psum_scatter(grad_fc1_local, ("img", "seq"), scatter_dimension=0, tiled=True),
        lax.psum_scatter(grad_fc2_local, ("img", "seq"), scatter_dimension=0, tiled=True),
        lax.psum_scatter(grad_gain_local, ("img", "seq"), scatter_dimension=0, tiled=True),
        lax.psum_scatter(grad_bias_local, ("img", "seq"), scatter_dimension=0, tiled=True),
    )
    hidden_bias_total = lax.psum(grad_hidden_bias, ("img", "seq"))
    return (
        mixed,
        grad_tokens,
        owned[0],
        owned[1],
        owned[2],
        owned[3],
        owned[4],
        owned[5],
        hidden_bias_total,
    )


def solution(mesh):
    in_specs = (
        P("img", "seq", None),
        P("img"),
        P(("img", "seq"), None),
        P(("img", "seq"), None),
        P(("img", "seq"), None),
        P(("img", "seq"), None),
        P(("img", "seq"), None),
        P(("img", "seq"), None),
        P(),
        P("img", "seq", None),
    )
    out_specs = (
        P("img", "seq", None),
        P("img", "seq", None),
        P(("img", "seq"), None),
        P(("img", "seq"), None),
        P(("img", "seq"), None),
        P(("img", "seq"), None),
        P(("img", "seq"), None),
        P(("img", "seq"), None),
        P(),
    )
    shards = mesh.shape["img"] * mesh.shape["seq"]
    fits = mesh.shape["seq"] == 4 and shards == 2 * HEADS
    plan = whole_layer if fits else local
    return jax.shard_map(plan, mesh=mesh, in_specs=in_specs, out_specs=out_specs, check_vma=False)
```

```python
from functools import partial

import jax
import jax.numpy as jnp
from jax import lax
from jax.experimental import pallas as pl
from jax.experimental.pallas import tpu as pltpu
from jax.sharding import PartitionSpec as P

HEADS = 16
VALID = 729


masked_score = -1000000000.0
norm_epsilon = 1e-06


def layer_norm(values, gain_col, bias_col):
    average = jnp.mean(values, -1, keepdims=True)
    centered = values - average
    variance = jnp.mean(centered * centered, -1, keepdims=True)
    return centered * lax.rsqrt(variance + norm_epsilon) * gain_col + bias_col


def row_dot(left, right):
    return lax.dot_general(
        left, right, (((0,), (0,)), ((), ())), preferred_element_type=jnp.float32
    )


def last_dot(left, right):
    return lax.dot_general(
        left, right, (((1,), (1,)), ((), ())), preferred_element_type=jnp.float32
    )


def split_heads(tensor, images_here, count, head_count, head_dim):
    return tensor.reshape(images_here, count, head_count, head_dim).transpose(2, 0, 1, 3)


def join_heads(tensor):
    head_count, images_here, count, head_dim = tensor.shape
    return tensor.transpose(1, 2, 0, 3).reshape(images_here, count, head_count * head_dim)


VMEM_BYTES = 63 * 2**20
MESH_IDS = pl.DeviceIdType.MESH
F32 = jnp.float32
BF16 = jnp.bfloat16
LANES = 128
SLIVER = 16
PIECE = 48
BLOCK = 192
HEAD_ROWS = 80
NN = (((1,), (0,)), ((), ()))
NT = (((1,), (1,)), ((), ()))
TN = (((0,), (0,)), ((), ()))


def mm(left, right, dims):
    return lax.dot_general(left, right, dims, preferred_element_type=F32)


def normalize(values):
    average = jnp.mean(values, -1, keepdims=True)
    centered = values - average
    variance = jnp.mean(centered * centered, -1, keepdims=True)
    inverse = lax.rsqrt(variance + norm_epsilon)
    return centered * inverse, inverse


def norm_back(grad, gain, hat, inverse):
    scaled = grad * gain
    first = jnp.mean(scaled, -1, keepdims=True)
    second = jnp.mean(scaled * hat, -1, keepdims=True)
    return inverse * (scaled - first - hat * second)


def lane_ids(rows):
    return lax.broadcasted_iota(jnp.int32, (rows, LANES), 1)


def lane_window(tiles, start, width, lanes):
    tile, offset = divmod(start, LANES)
    if offset == 0:
        return tiles[tile]
    first = pltpu.roll(tiles[tile], LANES - offset, 1)
    if offset + width <= LANES:
        return first
    second = pltpu.roll(tiles[tile + 1], LANES - offset, 1)
    return jnp.where(lanes < LANES - offset, first, second)


def pack_lanes(parts, width, lanes):
    tiles = {}
    for n, part in enumerate(parts):
        tile, offset = divmod(n * width, LANES)
        if offset:
            part = pltpu.roll(part, offset, 1)
        ends = [(tile, lanes >= offset)]
        if offset + width > LANES:
            ends.append((tile + 1, lanes < offset + width - LANES))
        for to, where in ends:
            kept = jnp.where(where, part, 0.0)
            tiles[to] = tiles[to] + kept if to in tiles else kept
    return [tiles[to] for to in sorted(tiles)]


class Tiles:
    def __init__(self, ref, first, step, height):
        self.ref, self.first, self.step, self.height = ref, first, step, height
        self.wide = ref.shape[1] // LANES

    def __getitem__(self, tile):
        part, at = divmod(tile, self.wide)
        row = self.first + part * self.step
        return self.ref[row : row + self.height, at * LANES : (at + 1) * LANES]

    def fill(self, source):
        whole = self.wide * LANES
        rows, wide = source.shape
        for part in range(-(-wide // whole)):
            row = self.first + part * self.step
            width = min(whole, wide - part * whole)
            self.ref[row + rows // 16 * 16 : row + self.height, :] = jnp.zeros(
                (self.height - rows // 16 * 16, whole), F32
            )
            if width < whole:
                last = width // LANES * LANES
                self.ref[row : row + self.height, last : last + LANES] = jnp.zeros((self.height, LANES), F32)
            self.ref[row : row + rows, 0:width] = source[:, part * whole : part * whole + width].astype(F32)


def layer_kernel(
    dims,
    off_ref, w_qkv, w_out, w_fc1, w_fc2, gains, biases, fc1_bias, tok, cot,
    o_mixed, o_gtok, o_q, o_fo, o_1, o_2, o_fb, o_gains, o_biases,
    wq, wo, w1, w2, rq, ro, r1, r2, tmp,
    xs, gc, h1, h2, act, gp, dg, qkv, attm, att_t, lse,
    g1, g2, gq, y1, y2, yo, yq, z1, z2, zo, zq, s1, s2,
    sb_a, cr_a, xr_a, sb_b, cr_b, xr_b, pf, fb, prm, bh, sms, smr, shs, shr,
    ssem, rsem, lsem,
):
    slice_len, d, hd, f, qw, n_z = dims
    scale = hd ** (-0.5)
    mask_low = masked_score / scale
    chunk = 256
    rows = 4 * BLOCK
    i, s = lax.axis_index("img"), lax.axis_index("seq")
    z, y = lax.div(i, 2), lax.rem(i, 2)
    x, c = lax.div(s, 2), lax.rem(s, 2)
    k = 2 * c + x
    cy = c == y
    core_peer = (i, x * 2 + 1 - c)
    x_peer = (i, (1 - x) * 2 + c)
    y_peer = (z * 2 + 1 - y, s)
    rb = wq.shape[0] // (2 * n_z)
    own = rb // 4

    def z_at(t):
        return lax.rem(z + t + n_z, n_z)

    def z_dev(t):
        return (z_at(t) * 2 + y, s)

    def z_to(zt):
        return (zt * 2 + y, s)

    near = (
        z,
        jnp.where(z == 0, 1, z - 1),
        jnp.where(z == 0, 2, jnp.where(z == 3, 1, z + 1)),
        jnp.where(z <= 1, 3, 0),
    )
    middle = (z == 1) | (z == 2)
    end = jnp.where(z == 1, 0, 3)

    def s_at(t):
        return lax.rem(s + t + 4, 4)

    count = [0]

    def take(n=1):
        first = count[0]
        count[0] += n
        return first

    def copy(src, dst, index, device, at=None):
        return pltpu.make_async_remote_copy(
            src, dst, ssem.at[index], rsem.at[index if at is None else at], device_id=device, device_id_type=MESH_IDS
        )

    sends = []

    def send(src, dst, index, device, at=None):
        made = copy(src, dst, index, device, at)
        made.start()
        sends.append(made)

    def token_rows(j):
        return pl.ds(pl.multiple_of(j * BLOCK, BLOCK), BLOCK)

    half_block = BLOCK // 2
    halves = (slice(0, half_block), slice(half_block, BLOCK))

    def half_rows(j, p):
        return pl.ds(pl.multiple_of(j * BLOCK + p * half_block, 32), half_block)

    def img_rows(b):
        return pl.ds(pl.multiple_of(b * rb, 16), rb)

    def most_rows(b, most=rb - SLIVER):
        return pl.ds(pl.multiple_of(b * rb, 16), most)

    def sliver_rows(b):
        return pl.ds(pl.multiple_of(b * rb + rb - SLIVER, 16), SLIVER)

    barrier = pltpu.get_barrier_semaphore()
    partners = [(i, s_at(t)) for t in (1, 2, 3)] + [z_dev(t) for t in range(1, n_z)] + [y_peer]
    for partner in partners:
        pl.semaphore_signal(barrier, inc=1, device_id=partner, device_id_type=MESH_IDS)

    class Gather:
        def __init__(self, piece, recv, full, local_index):
            self.piece, self.recv, self.full = piece, recv, full
            self.width = full.shape[1]
            self.sp, self.sz, self.sy, self.ss = take(4), take(n_z), take(n_z), take(n_z)
            self.local = local_index
            self.started = []

        def pieces(self):
            self.own_piece().start()
            for t in (1, 2, 3):
                self.piece_to(t).start()

        def own_piece(self):
            return pltpu.make_async_copy(self.piece.at[s, 0:PIECE], self.recv.at[s], lsem.at[self.local])

        def piece_to(self, t):
            to = s_at(t)
            return copy(self.piece.at[to, 0:PIECE], self.recv.at[s], self.sp + t, (i, to))

        def assemble(self):
            self.own_piece().wait()
            for t in (1, 2, 3):
                self.piece_to(t).wait_send()
                came = self.recv.at[s_at(-t)]
                copy(came, came, self.sp + t, (i, s_at(-t))).wait_recv()
            part = rb // 4
            for j in range(4):
                tmp[part * j : part * j + PIECE, 0 : self.width] = self.recv[j].astype(F32)
            self.full[img_rows(i), :] = tmp[0:rb, 0 : self.width].astype(BF16)

        def block(self, zb, side):
            return self.full.at[img_rows(zb * 2 + side)]

        def most(self, zb, side):
            return self.full.at[most_rows(zb * 2 + side)]

        def sliver(self, zb, side):
            return self.full.at[sliver_rows(zb * 2 + side)]

        def slivers(self):
            whole, part = self.block(z, 1 - y), self.sliver(z, 1 - y)
            copy(whole, whole, self.sy, y_peer, self.sy + z).wait_recv()
            for u in (1, 2, 3):
                self.send(part, part, self.ss + u, z_to(near[u]), self.ss + z)

        def send(self, src, dst, index, device, at):
            made = copy(src, dst, index, device, at)
            made.start()
            self.started.append(made)

        def along_z(self):
            own = self.block(z, y)
            for u in (1, 2):
                self.send(own, own, self.sz + u, z_to(near[u]), self.sz + z)

            @pl.when(middle)
            def _():
                copy(own, own, self.sz + 3, z_to(near[3]), self.sz + z).start()

        def across_y(self):
            own = self.block(z, y)
            self.send(own, own, self.sy, y_peer, self.sy + z)

        def forward(self, *steps):
            for u in steps:
                zb = near[u]
                came = self.block(zb, y)
                copy(came, came, self.sz, z_to(zb), self.sz + zb).wait_recv()
                came = self.most(zb, y)
                copy(came, came, self.sy + u, y_peer, self.sy + zb).start()

        def relay(self):
            @pl.when(middle)
            def _():
                came = self.block(near[3], y)
                copy(came, came, self.sz, z_to(end), self.sz + near[3]).wait_recv()
                copy(came, came, self.sz, z_to(end), self.sz + near[3]).start()
                came = self.most(near[3], y)
                copy(came, came, self.sy + 3, y_peer, self.sy + near[3]).start()

        def forward_far(self):
            @pl.when(jnp.logical_not(middle))
            def _():
                self.forward(3)

        def finish(self):
            for u in (1, 2, 3):
                zb = near[u]
                came = self.most(zb, 1 - y)
                copy(came, came, self.sy, y_peer, self.sy + zb).wait_recv()
                came = self.sliver(zb, 1 - y)
                copy(came, came, self.ss, z_to(zb), self.ss + zb).wait_recv()

        def sent(self):
            for made in self.started:
                made.wait_send()

            @pl.when(middle)
            def _():
                own, came = self.block(z, y), self.block(near[3], y)
                copy(own, own, self.sz + 3, z_to(near[3]), self.sz + z).wait_send()
                copy(came, came, self.sz, z_to(end), self.sz + near[3]).wait_send()

            for u in (1, 2, 3):
                came = self.most(near[u], y)
                copy(came, came, self.sy + u, y_peer, self.sy + near[u]).wait_send()

    gather_q = Gather(yq, rq, wq, 0)
    gather_1 = Gather(y1, r1, w1, 1)
    gather_2 = Gather(y2, r2, w2, 2)
    o_piece, o_z, o_y = take(), take(n_z), take(n_z)

    def head_block(array, t):
        return array.at[pl.ds(pl.multiple_of(z_at(-t) * LANES, LANES), HEAD_ROWS)]

    po = yo.at[0, 0:PIECE]

    def o_start():
        @pl.when(cy)
        def _():
            pltpu.make_async_copy(po, ro.at[c], lsem.at[3]).start()

        @pl.when(jnp.logical_not(cy))
        def _():
            copy(po, ro.at[c], o_piece, core_peer).start()

    def o_assemble():
        @pl.when(jnp.logical_not(cy))
        def _():
            copy(po, ro.at[c], o_piece, core_peer).wait_send()

        for h in range(4):
            wo[h * LANES + HEAD_ROWS : (h + 1) * LANES, :] = jnp.zeros((LANES - HEAD_ROWS, d), BF16)

        @pl.when(cy)
        def _():
            pltpu.make_async_copy(po, ro.at[c], lsem.at[3]).wait()
            copy(po, ro.at[1 - c], o_piece, core_peer).wait_recv()
            for j in range(2):
                tmp[own * j : own * j + PIECE, :] = ro[j].astype(F32)
            wo[pl.ds(pl.multiple_of(z * LANES, LANES), HEAD_ROWS), :] = tmp[0:HEAD_ROWS, :].astype(BF16)

    def o_along_z():
        @pl.when(cy)
        def _():
            mine = head_block(wo, 0)
            for t in range(1, n_z):
                copy(mine, mine, o_z + t, z_dev(t)).start()
            copy(mine, mine, o_y, y_peer).start()

    def o_forward():
        @pl.when(cy)
        def _():
            for t in range(1, n_z):
                came = head_block(wo, t)
                copy(came, came, o_z + t, z_dev(-t)).wait_recv()
                copy(came, came, o_y + t, y_peer).start()

    def o_finish():
        @pl.when(jnp.logical_not(cy))
        def _():
            for t in range(n_z):
                came = head_block(wo, t)
                copy(came, came, o_y + t, y_peer).wait_recv()

    def o_sent():
        @pl.when(cy)
        def _():
            mine = head_block(wo, 0)
            for t in range(1, n_z):
                copy(mine, mine, o_z + t, z_dev(t)).wait_send()
            for t in range(n_z):
                came = head_block(wo, t)
                copy(came, came, o_y + t, y_peer).wait_send()

    class TokenGather:
        def __init__(self, full):
            self.full = full
            self.sx, self.sc, self.sd = take(2), take(2), take(2)

        def hop(self, j, p, index, device):
            rows_p = self.full.at[half_rows(j, p)]
            return copy(rows_p, rows_p, index + p, device)

        def start(self, *halves):
            for p in halves:
                self.hop(s, p, self.sx, x_peer).start()
                self.hop(s, p, self.sc, core_peer).start()

        def forward(self):
            for p in (0, 1):
                made = self.hop((1 - x) * 2 + c, p, self.sx, x_peer)
                made.wait_recv()
                self.hop((1 - x) * 2 + c, p, self.sd, core_peer).start()

        def wait_core(self):
            for p in (0, 1):
                self.hop(x * 2 + 1 - c, p, self.sc, core_peer).wait_recv()

        def wait_last(self):
            for p in (0, 1):
                self.hop((1 - x) * 2 + 1 - c, p, self.sd, core_peer).wait_recv()

        def take_step(self, t):
            pl.when(t == 1)(self.wait_core)
            pl.when(t == 2)(self.forward)
            pl.when(t == 3)(self.wait_last)

        def sent(self):
            for p in (0, 1):
                self.hop(s, p, self.sx, x_peer).wait_send()
                self.hop(s, p, self.sc, core_peer).wait_send()
                self.hop((1 - x) * 2 + c, p, self.sd, core_peer).wait_send()

        def finish(self):
            self.wait_core()
            self.wait_last()
            self.sent()

    class SeqSum:
        def __init__(self, partial, sb, cr, xr):
            self.partial, self.sb, self.cr, self.xr = partial, sb, cr, xr
            self.first, self.last = take(2), take(2)

        def to_core(self, slot):
            return copy(self.sb.at[slot], self.cr.at[slot], self.first + slot, core_peer)

        def to_chip(self, p):
            own_half = pl.ds(p * half_block, half_block)
            return copy(self.sb.at[2, own_half], self.xr.at[own_half], self.last + p, x_peer)

        def run(self, low=0, high=4):
            partial = self.partial

            def step(t, carry):
                away, slot = lax.rem(t, 2) == 0, lax.div(t, 2)
                if low < 2 < high:
                    pl.when(t == 2)(self.across)
                part = partial(jnp.where(t < 2, 1 - x, x) * 2 + jnp.where(away, 1 - c, c))

                @pl.when(away)
                def _():
                    self.sb[slot] = part.astype(BF16)
                    self.to_core(slot).start()

                @pl.when(jnp.logical_not(away))
                def _():
                    pf[slot] = part

                return carry

            lax.fori_loop(low, high, step, 0)

        def across(self):
            copy(self.cr.at[0], self.cr.at[0], self.first, core_peer).wait_recv()
            for p, at in enumerate(halves):
                self.sb[2, at, :] = (pf[0, at, :] + self.cr[0, at, :].astype(F32)).astype(BF16)
                self.to_chip(p).start()

        def finish(self, p):
            at = halves[p]
            if p == 0:
                copy(self.cr.at[1], self.cr.at[1], self.first + 1, core_peer).wait_recv()
            self.to_chip(p).wait_recv()
            self.to_chip(p).wait_send()
            self.to_core(p).wait_send()
            return pf[1, at, :] + self.cr[1, at, :].astype(F32) + self.xr[at, :].astype(F32)

    class Reduce:
        def __init__(self, grad, yr, zr, zs, fs, out):
            self.grad, self.yr, self.zr, self.zs, self.fs, self.out = grad, yr, zr, zs, fs, out
            self.most = rb if zs is None else rb - SLIVER
            self.width = grad.shape[1]
            self.sy, self.sz, self.sp, self.ss = take(n_z), take(n_z), take(4), take(n_z)

        def kept(self, j):
            return w1.at[pl.ds(pl.multiple_of(self.out + j * PIECE, 16), PIECE), 0 : self.width]

        def at(self, zb, side):
            return img_rows(zb * 2 + side)

        def across_y(self):
            for u in (3, 2, 1):
                b = near[u] * 2 + 1 - y
                send(self.grad.at[most_rows(b, self.most)], self.yr.at[u, 0 : self.most], self.sy + u, y_peer)
                if self.zs is not None:
                    send(self.grad.at[sliver_rows(b)], self.zs.at[z], self.ss + u, z_to(near[u]), self.ss + z)
            if self.zs is None:
                send(self.grad.at[img_rows(z * 2 + 1 - y)], self.yr.at[0], self.sy, y_peer)

        def across_last(self):
            b = z * 2 + 1 - y
            part = self.grad[sliver_rows(b), :].astype(F32)
            for u in (1, 2, 3):
                zb = near[u]
                copy(self.zs.at[zb], self.zs.at[zb], self.ss, z_to(zb), self.ss + zb).wait_recv()
                part += self.zs[zb].astype(F32)
            self.grad[sliver_rows(b), :] = part.astype(BF16)
            send(self.grad.at[img_rows(b)], self.yr.at[0], self.sy, y_peer)

        def along_z(self, *steps):
            for u in steps:
                came = self.yr.at[u, 0 : self.most]
                copy(came, came, self.sy + u, y_peer).wait_recv()
                mine, most = self.at(near[u], y), most_rows(near[u] * 2 + y, self.most)
                added = self.yr[u, 0 : self.most, :].astype(F32)
                self.grad[most, :] = (self.grad[most, :].astype(F32) + added).astype(BF16)
                if u < 3:
                    send(self.grad.at[mine], self.zr.at[z], self.sz + u, z_to(near[u]), self.sz + z)
                else:

                    @pl.when(jnp.logical_not(middle))
                    def _():
                        self.far().start()

        def far(self):
            rows_far = self.grad.at[self.at(near[3], y)]
            return copy(rows_far, self.zr.at[near[1]], self.sz + 3, z_to(near[1]), self.sz + near[1])

        def onward(self):
            rows_far = self.grad.at[self.at(near[3], y)]
            return copy(rows_far, self.zr.at[z], self.sz + 3, z_to(near[3]), self.sz + z)

        def relay(self):
            @pl.when(middle)
            def _():
                mine = self.at(near[3], y)
                copy(self.zr.at[z], self.zr.at[z], self.sz, z_to(end), self.sz + z).wait_recv()
                self.grad[mine, :] = (self.grad[mine, :].astype(F32) + self.zr[z].astype(F32)).astype(BF16)
                self.onward().start()

        def came_z(self, u):
            zb = near[u]
            copy(self.zr.at[zb], self.zr.at[zb], self.sz, z_to(zb), self.sz + zb).wait_recv()
            tmp[0:rb, 0 : self.width] += self.zr[zb].astype(F32)

        def pieces(self):
            copy(self.yr.at[0], self.yr.at[0], self.sy, y_peer).wait_recv()
            tmp[0:rb, 0 : self.width] = self.grad[self.at(z, y), :].astype(F32) + self.yr[0].astype(F32)
            self.came_z(1)
            self.came_z(2)

            @pl.when(middle)
            def _():
                self.came_z(3)

            part = rb // 4
            for j in range(4):
                self.fs[j] = tmp[part * j : part * j + PIECE, 0 : self.width].astype(BF16)
            pltpu.make_async_copy(self.fs.at[s], self.kept(s), lsem.at[4]).start()
            for t in (1, 2, 3):
                to = s_at(t)
                send(self.fs.at[to], self.kept(s), self.sp + t, (i, to))
            pltpu.make_async_copy(self.fs.at[s], self.kept(s), lsem.at[4]).wait()

        def sent(self):
            @pl.when(middle)
            def _():
                self.onward().wait_send()

            @pl.when(jnp.logical_not(middle))
            def _():
                self.far().wait_send()

        def finish(self):
            for t in (1, 2, 3):
                came = self.kept(s_at(-t))
                copy(came, came, self.sp + t, (i, s_at(-t))).wait_recv()

        def piece_tiles(self, j):
            row = self.out + j * PIECE
            return [
                w1[row : row + PIECE, t * LANES : (t + 1) * LANES].astype(F32) for t in range(self.width // LANES)
            ]

        def publish(self, tiles, out):
            for t, tile in enumerate(tiles):
                width = min(LANES, out.shape[1] - t * LANES)
                out[:, t * LANES : t * LANES + width] = tile[0:own, 0:width]

        def publish_wide(self, out):
            tiles = {}
            for j in range(4):
                tile, offset = divmod(j * f, LANES)
                for t, part in enumerate(self.piece_tiles(j)):
                    if offset:
                        part = pltpu.roll(part, offset, 1)
                    for to, where in ((tile + t, piece_lanes >= offset), (tile + t + 1, piece_lanes < offset)):
                        if to * LANES < 4 * f:
                            kept = jnp.where(where, part, 0.0)
                            tiles[to] = tiles[to] + kept if to in tiles else kept
            self.publish([tiles[to] for to in sorted(tiles)], out)

        def publish_heads(self, out):
            pieces = [self.piece_tiles(j) for j in range(4)]
            tiles = []
            for kind in range(3):
                parts = []
                for head in range(d // hd):
                    which, to = divmod(head, 4)
                    part = lane_window(pieces[2 * (to % 2) + to // 2], (4 * kind + which) * hd, hd, piece_lanes)
                    parts.append(jnp.where(piece_lanes < hd, part, 0.0))
                tiles += pack_lanes(parts, hd, piece_lanes)
            self.publish(tiles, out)

    reduce_2 = Reduce(g2, y2, z2, s2, r2, 0)
    reduce_1 = Reduce(g1, y1, z1, s1, r1, 4 * PIECE)
    reduce_q = Reduce(gq, yq, zq, None, rq, 8 * PIECE)
    go = wo
    ro_y, ro_z, ro_p = take(n_z), take(n_z), take()

    def ro_across_y():
        @pl.when(jnp.logical_not(cy))
        def _():
            for t in (*range(1, n_z), 0):
                copy(head_block(go, -t), yo.at[t], ro_y + t, y_peer).start()

    def ro_along_z():
        @pl.when(cy)
        def _():
            for t in range(1, n_z):
                copy(yo.at[t], yo.at[t], ro_y + t, y_peer).wait_recv()
                mine = pl.ds(pl.multiple_of(z_at(t) * LANES, LANES), HEAD_ROWS)
                go[mine, :] = (go[mine, :].astype(F32) + yo[t].astype(F32)).astype(BF16)
                copy(go.at[mine], zo.at[t - 1], ro_z + t, z_dev(t)).start()

    def ro_pieces():
        @pl.when(cy)
        def _():
            copy(yo.at[0], yo.at[0], ro_y, y_peer).wait_recv()
            mine = pl.ds(pl.multiple_of(z * LANES, LANES), HEAD_ROWS)
            total = go[mine, :].astype(F32) + yo[0].astype(F32)
            for t in range(1, n_z):
                copy(zo.at[t - 1], zo.at[t - 1], ro_z + t, z_dev(-t)).wait_recv()
                total += zo[t - 1].astype(F32)
            tmp[0:HEAD_ROWS, :] = total
            for j in range(2):
                ro[j] = tmp[own * j : own * j + PIECE, :].astype(BF16)
            pltpu.make_async_copy(ro.at[c], o_fo, lsem.at[5]).start()
            copy(ro.at[1 - c], o_fo, ro_p, core_peer).start()
            pltpu.make_async_copy(ro.at[c], o_fo, lsem.at[5]).wait()

    def ro_finish():
        @pl.when(cy)
        def _():
            for t in range(1, n_z):
                copy(head_block(go, -t), zo.at[t - 1], ro_z + t, z_dev(t)).wait_send()
            copy(ro.at[1 - c], o_fo, ro_p, core_peer).wait_send()

        @pl.when(jnp.logical_not(cy))
        def _():
            for t in range(n_z):
                copy(head_block(go, -t), yo.at[t], ro_y + t, y_peer).wait_send()
            copy(o_fo, o_fo, ro_p, core_peer).wait_recv()

    def arriving(t):
        return jnp.where(t < 2, x, 1 - x) * 2 + jnp.where(lax.rem(t, 2) == 0, c, 1 - c)

    def real_rows(j, width):
        t = lax.broadcasted_iota(jnp.int32, (BLOCK, width), 0)
        position = j * slice_len + t
        return (t < slice_len) & (position >= off_ref[0]) & (position < off_ref[0] + VALID)

    def half_of(rows_in, p):
        if p == 0:
            return rows_in[0, halves[0], :]
        pf[0, BLOCK - 16 : BLOCK, :] = jnp.zeros((16, d), F32)
        pf[0, half_block:slice_len, :] = rows_in[0, half_block:slice_len, :]
        return pf[0, halves[1], :]

    def put_half(rows_out, p, value):
        if p == 0:
            rows_out[0, halves[0], :] = value
        else:
            rows_out[0, half_block:slice_len, :] = value[0 : slice_len - half_block]

    tokens_in, cot_in = TokenGather(xs), TokenGather(gc)
    piece_lanes = lane_ids(PIECE)
    three = [Tiles(dg, PIECE * n, PIECE, PIECE) for n in range(3)]
    for n in range(3):
        three[n].fill(w_qkv.at[:, n * d : (n + 1) * d])
    small = Tiles(dg, 3 * PIECE, PIECE, PIECE)
    dg[3 * PIECE : 3 * PIECE + LANES, 0:LANES] = jnp.zeros((LANES, LANES), F32)
    dg[3 * PIECE : 3 * PIECE + 2, 0:own] = gains[...].astype(F32)
    dg[3 * PIECE + 2 : 3 * PIECE + 8, 0:own] = biases[...].astype(F32)
    dg[3 * PIECE : 3 * PIECE + LANES, 0:LANES] = dg[3 * PIECE : 3 * PIECE + LANES, 0:LANES].T
    for to in range(4):
        parts = []
        for n in range(12):
            kind, which = divmod(n, 4)
            head = 4 * which + 2 * (to % 2) + to // 2
            part = lane_window(three[kind], head * hd, hd, piece_lanes)
            parts.append(jnp.where(piece_lanes < hd, part, 0.0))
        tiles = pack_lanes(parts, hd, piece_lanes)
        tiles[-1] = tiles[-1] + pltpu.roll(small[0], 12 * hd % LANES, 1)
        for at, tile in enumerate(tiles):
            yq[to, 0:PIECE, at * LANES : (at + 1) * LANES] = tile.astype(BF16)
    pl.semaphore_wait(barrier, len(partners))
    gather_q.pieces()
    pf[0, BLOCK - 16 : BLOCK, :] = jnp.zeros((16, d), F32)
    pf[0, 0:slice_len, :] = tok[0].astype(F32)
    xs[token_rows(s), :] = pf[0].astype(BF16)
    tokens_in.start(0, 1)
    out_rows = Tiles(dg, 12 * PIECE, PIECE, PIECE)
    out_rows.fill(w_out)
    for at in range(d // LANES):
        yo[0, 0:PIECE, at * LANES : (at + 1) * LANES] = out_rows[at].astype(BF16)
    o_start()
    for weights, first, pieces in ((w_fc1, 4, y1), (w_fc2, 8, y2)):
        wide = Tiles(dg, first * PIECE, PIECE, PIECE)
        wide.fill(weights)
        for to in range(4):
            for at in range(w1.shape[1] // LANES):
                start = to * f + at * LANES
                width = min(LANES, f - at * LANES)
                part = lane_window(wide, start, width, piece_lanes)
                if width < LANES:
                    part = jnp.where(piece_lanes < width, part, 0.0)
                pieces[to, 0:PIECE, at * LANES : (at + 1) * LANES] = part.astype(BF16)
        (gather_1 if first == 4 else gather_2).pieces()
    pf[1, BLOCK - 16 : BLOCK, :] = jnp.zeros((16, d), F32)
    pf[1, 0:slice_len, :] = cot[0].astype(F32)
    gc[token_rows(s), :] = jnp.where(real_rows(s, d), pf[1], 0.0).astype(BF16)
    cot_in.start(0, 1)
    sms[0] = jnp.zeros(sms.shape[1:], F32)
    shs[0] = jnp.zeros(shs.shape[1:], F32)
    tmp[...] = jnp.zeros(tmp.shape, F32)

    gather_q.assemble()
    gather_q.along_z()
    gather_q.across_y()
    o_assemble()
    o_along_z()
    gather_q.forward(1)
    tokens_in.forward()
    gather_1.assemble()
    gather_q.slivers()
    gather_q.forward(2)
    gather_q.relay()
    gather_1.along_z()
    gather_1.across_y()
    gather_2.assemble()
    gather_q.forward_far()
    o_forward()
    gather_2.across_y()
    cot_in.forward()
    tokens_in.finish()
    gather_q.finish()

    packed = 3 * 4 * hd
    base = packed // LANES * LANES
    columns = wq[:, base : base + LANES].astype(F32)
    prm[...] = columns.T[packed - base : packed - base + 8, :]
    one_lane = lane_ids(1)
    for which, row in ((0, 3), (1, 4)):
        tiles = [prm[row : row + 1, LANES * t : LANES * (t + 1)] for t in range(d // LANES)]
        for head in range(d // hd):
            bh[which, head : head + 1, :] = lane_window(tiles, head * hd, hd, one_lane)
    gain_one, gain_two, shift_one = prm[0:1, :], prm[1:2, :], prm[2:3, :]
    bias_out, shift_two, bias_two = prm[5:6, :], prm[6:7, :], prm[7:8, :]

    lanes = lane_ids(BLOCK)

    def project(j, carry):
        hat, _ = normalize(xs[token_rows(j), :].astype(F32))
        low = (hat * gain_one + shift_one).astype(BF16)
        h1[token_rows(j), :] = low
        wide = mm(low, wq[...], NN)
        tiles = [wide[:, LANES * t : LANES * (t + 1)] for t in range(qw // LANES)]
        key_low = jnp.where(real_rows(j, LANES), 0.0, mask_low)
        for n in range(12):
            kind, head = divmod(n, 4)
            part = lane_window(tiles, n * hd, hd, lanes)
            if kind != 1:
                part = part + bh[kind // 2, pl.ds(4 * head + k, 1), :]
            beside = key_low if kind == 1 else jnp.ones_like(part)
            part = jnp.where(lanes < hd, part, jnp.where(lanes == hd, beside, 0.0))
            qkv[n, token_rows(j), :] = part.astype(BF16)
        return carry

    lax.fori_loop(0, 4, project, 0)
    gather_1.slivers()
    gather_2.along_z()
    half = rows // 2
    sublanes = lax.broadcasted_iota(jnp.int32, (LANES, half), 0)

    def attend(step, carry):
        head, part = lax.rem(step, 4), jnp.where(step < 4, 1 - x, x)
        at = pl.ds(pl.multiple_of(part * half, LANES), half)
        scores = mm(qkv[4 + head], qkv[head, at, :], NT)
        top = jnp.max(scores, 0, keepdims=True)
        weights = jnp.exp((scores - top) * scale).astype(BF16)
        summed = mm(qkv[8 + head], weights, TN)
        total = summed[hd : hd + 1, :]
        result = jnp.where(sublanes < hd, summed / total, 0.0)
        att_t[head, :, at] = result.astype(BF16)
        attm[at, pl.ds(pl.multiple_of(head * LANES, LANES), LANES)] = result.T.astype(BF16)
        lse[head, :, at] = top * scale + jnp.log(total)
        return carry

    lax.fori_loop(0, 4, attend, 0)
    gather_1.forward(1)
    o_finish()
    sum_one = SeqSum(lambda j: mm(attm[token_rows(j), :], wo[...], NN), sb_a, cr_a, xr_a)
    sum_one.run(0, 2)
    sum_one.across()
    lax.fori_loop(4, 8, attend, 0)
    sum_one.run(2, 4)
    gather_1.relay()
    gather_2.slivers()
    gather_1.forward(2)
    cot_in.finish()
    bias_parts = Tiles(dg, 14 * PIECE, 8, 8)
    bias_parts.fill(fc1_bias[...].astype(F32)[None])
    row_lanes = lane_ids(8)
    for at in range(w1.shape[1] // LANES):
        width = min(LANES, f - at * LANES)
        mine = jnp.zeros((8, LANES), F32)
        for to in range(4):
            part = lane_window(bias_parts, to * f + at * LANES, width, row_lanes)
            mine = jnp.where(s == to, part, mine)
        fb[:, at * LANES : (at + 1) * LANES] = jnp.where(row_lanes < width, mine, 0.0)[0:1]

    gather_1.forward_far()
    h2_in = TokenGather(h2)
    for p in (0, 1):
        middle_rows = xs[half_rows(s, p), :].astype(F32) + sum_one.finish(p) + bias_out
        put_half(o_mixed, p, middle_rows)
        hat, _ = normalize(middle_rows)
        h2[half_rows(s, p), :] = (hat * gain_two + shift_two).astype(BF16)
        h2_in.start(p)
    gather_2.forward(1)
    gather_1.finish()

    slope = (2.0 / 3.141592653589793) ** 0.5

    def widen(t, carry):
        h2_in.take_step(t)
        j = arriving(t)
        pre = mm(h2[token_rows(j), :], w1[...], NN) + fb[...]
        square = pre * pre
        curve = jnp.tanh(slope * pre * (1.0 + 0.044715 * square))
        half = 0.5 + 0.5 * curve
        act[token_rows(j), :] = (pre * half).astype(BF16)
        dg[token_rows(j), :] = half + 0.5 * slope * pre * (1.0 - curve * curve) * (1.0 + 0.134145 * square)
        return carry

    lax.fori_loop(0, 2, widen, 0)
    gather_2.forward(2)
    gather_2.relay()
    lax.fori_loop(2, 4, widen, 0)
    h2_in.sent()
    gather_2.forward_far()

    def column_products(left, right, out):
        def step(t, carry):
            at = pl.ds(pl.multiple_of(t * LANES, LANES), LANES)
            out[at, :] = mm(left[:, at], right[...], TN).astype(BF16)
            return carry

        lax.fori_loop(0, left.shape[1] // LANES, step, 0)

    column_products(gc, act, g2)
    reduce_2.across_y()
    gather_2.finish()

    def hidden_back(j):
        at = token_rows(j)
        low = (mm(gc[at, :], w2[...], NN) * dg[at, :]).astype(BF16)
        gp[at, :] = low
        column = jnp.sum(low.astype(F32), 0, keepdims=True)
        sms[0, 6:7, :] += column
        return mm(low, w1[...], NT)

    gather_1.sent()
    sum_two = SeqSum(hidden_back, sb_a, cr_a, xr_a)
    sum_two.run()
    reduce_2.across_last()
    column_products(h2, gp, g1)
    reduce_1.across_y()
    reduce_2.along_z(3)
    reduce_2.along_z(2)
    gb_in = TokenGather(gc)
    for p in (0, 1):
        grad_h = sum_two.finish(p)
        hat, inverse = normalize(half_of(o_mixed, p))
        kept = gc[half_rows(s, p), :].astype(F32)
        grad_x = kept + norm_back(grad_h, gain_two, hat, inverse)
        put_half(o_gtok, p, grad_x)
        low = grad_x.astype(BF16)
        gc[half_rows(s, p), :] = low
        gb_in.start(p)
        for row, column in ((1, grad_h * hat), (4, grad_h), (5, kept), (3, low.astype(F32))):
            sms[0, row : row + 1, :] += jnp.sum(column, 0, keepdims=True)

    sum_three = SeqSum(lambda j: mm(act[token_rows(j), :], w2[...], NT), sb_b, cr_b, xr_b)
    sum_three.run()
    reduce_2.along_z(1)
    reduce_1.across_last()

    def attended_back(t, carry):
        gb_in.take_step(t)
        j = arriving(t)
        attm[token_rows(j), :] = mm(gc[token_rows(j), :], wo[...], NT).astype(BF16)
        return carry

    lax.fori_loop(0, 4, attended_back, 0)
    gb_in.sent()

    o_sent()

    def out_products(head, carry):
        at = pl.ds(pl.multiple_of(head * LANES, LANES), LANES)
        go[at, :] = mm(att_t[head], gc[...], NN).astype(BF16)
        return carry

    lax.fori_loop(0, 4, out_products, 0)
    ro_across_y()
    reduce_2.relay()

    wide_lanes = lane_ids(rows)
    chunk_lanes = lane_ids(chunk)

    def attend_back(head, carry):
        grad_k = jnp.zeros((rows, LANES), F32)
        grad_v = jnp.zeros((rows, LANES), F32)
        grad_q = []
        for part in range(rows // chunk):
            at = slice(part * chunk, (part + 1) * chunk)
            query, grad_out = qkv[head, at, :], attm[at, pl.ds(pl.multiple_of(head * LANES, LANES), LANES)]
            scores = mm(qkv[4 + head], query, NT)
            probs = jnp.exp(scores * scale - lse[head, :, at])
            grad_p = mm(qkv[8 + head], grad_out, NT)
            delta = jnp.sum(probs * grad_p, 0, keepdims=True)
            grad_s = (probs * (grad_p - delta)).astype(BF16)
            grad_k += mm(grad_s, query, NN)
            grad_v += mm(probs.astype(BF16), grad_out, NN)
            grad_q.append(mm(qkv[4 + head], grad_s, TN))
        for part in range(rows // chunk):
            at = slice(part * chunk, (part + 1) * chunk)
            low = jnp.where(chunk_lanes < hd, grad_q[part].T * scale, 0.0).astype(BF16)
            qkv[head, at, :] = low
            shs[0, pl.ds(4 * head + k, 1), :] += jnp.sum(low.astype(F32), 0, keepdims=True)
        qkv[4 + head] = jnp.where(wide_lanes < hd, grad_k * scale, 0.0).astype(BF16)
        low = grad_v.astype(BF16)
        qkv[8 + head] = low
        shs[0, pl.ds(16 + 4 * head + k, 1), :] = jnp.sum(low.astype(F32), 0, keepdims=True)
        return carry

    reduce_1.along_z(3)
    lax.fori_loop(0, 2, attend_back, 0)
    reduce_1.along_z(2)
    lax.fori_loop(2, 4, attend_back, 0)
    reduce_1.along_z(1)
    reduce_1.relay()

    for p, at in enumerate(halves):
        total = half_of(o_mixed, p) + sum_three.finish(p) + bias_two
        put_half(o_mixed, p, jnp.where(real_rows(s, d)[at], total, 0.0))
    gpj = h2.at[:, 0:qw]

    def pack(j, carry):
        parts = [qkv[n, token_rows(j), :].astype(F32) for n in range(12)]
        for to, tile in enumerate(pack_lanes(parts, hd, lanes)):
            gpj[token_rows(j), LANES * to : LANES * (to + 1)] = tile.astype(BF16)
        return carry

    lax.fori_loop(0, 4, pack, 0)

    def tokens_back(j):
        part = mm(gpj[token_rows(j), :], wq[...], NT)
        hat, _ = normalize(xs[token_rows(j), :].astype(F32))
        sms[0, 0:1, :] += jnp.sum(part * hat, 0, keepdims=True)
        sms[0, 2:3, :] += jnp.sum(part, 0, keepdims=True)
        return part

    sum_four = SeqSum(tokens_back, sb_a, cr_a, xr_a)
    sum_four.run()
    sm_at, sh_at = take(7), take(7)

    def vectors(stage, slots, devices):
        for slot, device in zip(slots, devices, strict=True):
            send(sms.at[stage], smr.at[slot], sm_at + slot, device)
            send(shs.at[stage], shr.at[slot], sh_at + slot, device)

    def vectors_sum(stage, slots, devices):
        for slot, device in zip(slots, devices, strict=True):
            copy(smr.at[slot], smr.at[slot], sm_at + slot, device).wait_recv()
            copy(shr.at[slot], shr.at[slot], sh_at + slot, device).wait_recv()
        total, heads = sms[stage], shs[stage]
        for slot in slots:
            total += smr[slot]
            heads += shr[slot]
        return total, heads

    z_to_all, z_from_all = [z_dev(t) for t in (1, 2, 3)], [z_dev(-t) for t in (1, 2, 3)]
    s_to_all, s_from_all = [(i, s_at(t)) for t in (1, 2, 3)], [(i, s_at(-t)) for t in (1, 2, 3)]
    vectors(0, (0,), (y_peer,))
    column_products(h1, gpj, gq)
    reduce_q.across_y()
    sms[1], shs[1] = vectors_sum(0, (0,), (y_peer,))
    vectors(1, (1, 2, 3), z_to_all)
    ro_along_z()
    reduce_2.pieces()
    reduce_q.along_z(3, 2)
    reduce_q.relay()
    for p in (0, 1):
        grad_h = sum_four.finish(p)
        hat, inverse = normalize(xs[half_rows(s, p), :].astype(F32))
        put_half(o_gtok, p, half_of(o_gtok, p) + norm_back(grad_h, gain_one, hat, inverse))
    reduce_q.along_z(1)
    sms[2], shs[2] = vectors_sum(1, (1, 2, 3), z_from_all)
    vectors(2, (4, 5, 6), s_to_all)
    reduce_1.pieces()
    reduce_2.finish()
    reduce_2.publish_wide(o_2)
    ro_pieces()
    reduce_q.pieces()
    reduce_1.finish()
    reduce_1.publish_wide(o_1)
    summed_rows, by_head = vectors_sum(2, (4, 5, 6), s_from_all)
    prm[pl.ds(s, 1), :] = sms[2, 6:7, :]
    for t in (1, 2, 3):
        prm[pl.ds(s_at(-t), 1), :] = smr[3 + t, 6:7, :]
    mine = smr.at[1]
    for to, row in enumerate((0, 1, 2, None, None, 3, 4, 5)):
        if row is not None:
            mine[to : to + 1, :] = summed_rows[row : row + 1, :]
    for which in range(2):
        heads = [by_head[16 * which + head : 16 * which + head + 1, :] for head in range(d // hd)]
        for to, tile in enumerate(pack_lanes(heads, hd, one_lane)):
            mine[3 + which : 4 + which, to * LANES : (to + 1) * LANES] = tile
    start = (i * 4 + s) * own
    turned = pltpu.roll(mine[0:8, :], lax.rem(d - start, d), 1)
    o_gains[...] = turned[0:2, 0:own]
    o_biases[...] = turned[2:8, 0:own]
    spread = {}
    for j in range(4):
        tile, offset = divmod(j * f, LANES)
        for t in range(w1.shape[1] // LANES):
            part = prm[j : j + 1, t * LANES : (t + 1) * LANES]
            if offset:
                part = pltpu.roll(part, offset, 1)
            for to, where in ((tile + t, one_lane >= offset), (tile + t + 1, one_lane < offset)):
                if to * LANES < 4 * f:
                    kept = jnp.where(where, part, 0.0)
                    spread[to] = spread[to] + kept if to in spread else kept
    for to, tile in spread.items():
        width = min(LANES, 4 * f - to * LANES)
        o_fb[:, to * LANES : to * LANES + width] = tile[:, 0:width]
    ro_finish()
    reduce_q.finish()
    reduce_q.publish_heads(o_q)
    for part in (gather_q, gather_2, reduce_q, reduce_1, reduce_2):
        part.sent()
    for made in sends:
        made.wait_send()


def hand_over(mixed, tokens, g_qkv, g_1, g_2, g_out, g_gains, g_biases, g_fb, *outs):
    o_mixed, o_tokens, o_qkv, o_1, o_2, o_out, o_gains, o_biases, o_fb = outs
    o_qkv[...] = g_qkv[...]
    o_1[...] = g_1[...]
    o_2[...] = g_2[...]
    o_mixed[:, 0, :] = mixed[0]
    o_tokens[:, 0, :] = tokens[0]
    o_out[...] = g_out[0 : o_out.shape[0], :].astype(F32)
    o_gains[...] = g_gains[...]
    o_biases[...] = g_biases[...]
    o_fb[...] = g_fb[0]


def whole_layer(tokens, offsets, w_qkv, w_out, w_fc1, w_fc2, gains, biases, fc1_bias, cotangent):
    _, slice_len, d = tokens.shape
    hd = d // HEADS
    own, wide = w_fc1.shape
    f = wide // 4
    f_pad = -(-f // LANES) * LANES
    packed = 12 * hd
    qw = -(-(packed + 8) // LANES) * LANES
    n_z = lax.axis_size("img") // 2
    rb = own * 4
    rows = 4 * BLOCK

    hbm = pl.BlockSpec(memory_space=pl.ANY)
    vmem = pl.BlockSpec(memory_space=pltpu.VMEM)
    outs = [
        ((1, slice_len, d), F32, vmem),
        ((1, slice_len, d), F32, vmem),
        ((own, 3 * d), F32, vmem),
        ((PIECE, d), BF16, hbm),
        ((own, wide), F32, vmem),
        ((own, wide), F32, vmem),
        ((1, wide), F32, vmem),
        ((2, own), F32, vmem),
        ((6, own), F32, vmem),
    ]
    low = [
        (d, qw), (4 * LANES, d), (d, f_pad), (d, f_pad),
        (4, PIECE, qw), (2, PIECE, d), (4, PIECE, f_pad), (4, PIECE, f_pad),
    ]
    scratch = [pltpu.VMEM(shape, BF16) for shape in low]
    scratch += [pltpu.VMEM((160, max(d, f_pad)), F32)]
    scratch += [pltpu.VMEM((rows, w), BF16) for w in (d, d, d, d, f_pad, f_pad)]
    scratch += [pltpu.VMEM((rows, f_pad), F32)]
    scratch += [
        pltpu.VMEM((12, rows, LANES), BF16),
        pltpu.VMEM((rows, 4 * LANES), BF16),
        pltpu.VMEM((4, LANES, rows), BF16),
        pltpu.VMEM((4, 1, rows), F32),
    ]
    scratch += [pltpu.VMEM(shape, BF16) for shape in ((d, f_pad), (d, f_pad), (d, qw))]
    scratch += [pltpu.VMEM((n_z, h, w), BF16) for h, w in ((rb, f_pad), (rb, f_pad), (HEAD_ROWS, d), (rb, qw))]
    scratch += [pltpu.VMEM((n_z, h, w), BF16) for h, w in ((rb, f_pad), (rb, f_pad), (HEAD_ROWS, d), (rb, qw))]
    scratch += [pltpu.VMEM((n_z, SLIVER, w), BF16) for w in (f_pad, f_pad)]
    for _ in range(2):
        scratch += [pltpu.VMEM((n, BLOCK, d), BF16) for n in (3, 2)] + [pltpu.VMEM((BLOCK, d), BF16)]
    scratch += [
        pltpu.VMEM((2, BLOCK, d), F32),
        pltpu.VMEM((1, f_pad), F32),
        pltpu.VMEM((8, d), F32),
        pltpu.VMEM((2, 16, LANES), F32),
        pltpu.VMEM((3, 8, d), F32),
        pltpu.VMEM((7, 8, d), F32),
        pltpu.VMEM((3, 32, LANES), F32),
        pltpu.VMEM((7, 32, LANES), F32),
        pltpu.SemaphoreType.DMA((200,)),
        pltpu.SemaphoreType.DMA((200,)),
        pltpu.SemaphoreType.DMA((8,)),
    ]
    mixed, grad_tokens, gq, go, g1, g2, g_fb, g_gains, g_biases = pl.pallas_call(
        partial(layer_kernel, (slice_len, d, hd, f, qw, n_z)),
        out_shape=[jax.ShapeDtypeStruct(shape, kind) for shape, kind, _ in outs],
        in_specs=[pl.BlockSpec(memory_space=pltpu.SMEM)] + [vmem] * 9,
        out_specs=[spec for _, _, spec in outs],
        scratch_shapes=scratch,
        compiler_params=pltpu.CompilerParams(
            collective_id=0, has_side_effects=True, vmem_limit_bytes=VMEM_BYTES
        ),
    )(offsets, w_qkv, w_out, w_fc1, w_fc2, gains.T, biases.T, fc1_bias, tokens, cotangent)

    rows_out = jax.ShapeDtypeStruct((slice_len, 1, d), F32)
    same = [jax.ShapeDtypeStruct(made.shape, F32) for made in (gq, g1, g2)]
    rest = [jax.ShapeDtypeStruct(shape, F32) for shape in ((own, d), (2, own), (6, own), (wide,))]
    mixed, grad_tokens, gq, g1, g2, go, g_gains, g_biases, g_fb = pl.pallas_call(
        hand_over,
        out_shape=[rows_out, rows_out, *same, *rest],
        in_specs=[vmem] * 9,
        out_specs=[vmem] * 9,
    )(mixed, grad_tokens, gq, g1, g2, go, g_gains, g_biases, g_fb)
    mixed, grad_tokens = mixed.reshape(tokens.shape), grad_tokens.reshape(tokens.shape)
    return mixed, grad_tokens, gq, go, g1, g2, g_gains.T, g_biases.T, g_fb


def local(tokens, offsets, w_qkv, w_out, w_fc1, w_fc2, gains, biases, fc1_bias, cotangent):
    images_here, slice_len, model_width = tokens.shape
    head_count = HEADS
    head_dim = model_width // head_count
    length = slice_len * lax.axis_size("seq")
    row_count = images_here * slice_len
    score_scale = head_dim ** (-0.5)
    gathered = (
        lax.all_gather(w_qkv, ("img", "seq"), axis=0, tiled=True),
        lax.all_gather(w_out, ("img", "seq"), axis=0, tiled=True),
        lax.all_gather(w_fc1, ("img", "seq"), axis=0, tiled=True),
        lax.all_gather(w_fc2, ("img", "seq"), axis=0, tiled=True),
        lax.all_gather(gains, ("img", "seq"), axis=0, tiled=True),
        lax.all_gather(biases, ("img", "seq"), axis=0, tiled=True),
    )
    wide_qkv, wide_out, wide_fc1, wide_fc2, gain_all, bias_all = gathered
    gain_cols = gain_all.astype(jnp.float32)
    bias_cols = bias_all.astype(jnp.float32)
    starts = offsets[:, None]
    positions = lax.axis_index("seq") * slice_len + jnp.arange(slice_len, dtype=jnp.int32)
    own_valid = (positions[None, :] >= starts) & (positions[None, :] < starts + VALID)
    row_valid = own_valid.astype(jnp.float32)
    key_pos = jnp.arange(length, dtype=jnp.int32)
    key_valid = (key_pos[None, :] >= starts) & (key_pos[None, :] < starts + VALID)
    inputs = tokens.astype(jnp.float32).reshape(row_count, model_width)
    h_one, norm_one_back = jax.vjp(layer_norm, inputs, gain_cols[:, 0], bias_cols[:, 0])
    h_one_low = h_one.astype(jnp.bfloat16)
    qkv_bias = jnp.concatenate([bias_cols[:, 1], jnp.zeros_like(bias_cols[:, 1]), bias_cols[:, 2]])
    projected = (
        jnp.dot(h_one_low, wide_qkv, preferred_element_type=jnp.float32) + qkv_bias
    ).astype(jnp.bfloat16)
    query_rows = projected[:, :model_width]
    key_rows = projected[:, model_width : 2 * model_width].reshape(
        images_here, slice_len, model_width
    )
    value_rows = projected[:, 2 * model_width :].reshape(images_here, slice_len, model_width)
    keys_all, values_all = (
        lax.all_gather(key_rows, "seq", axis=1, tiled=True),
        lax.all_gather(value_rows, "seq", axis=1, tiled=True),
    )
    query_heads = split_heads(query_rows, images_here, slice_len, head_count, head_dim)
    key_heads = split_heads(keys_all, images_here, length, head_count, head_dim)
    value_heads = split_heads(values_all, images_here, length, head_count, head_dim)

    def head_scores(head_query_rows, head_key_rows, mask):
        scores = (
            jnp.einsum(
                "asl,aul->asu", head_query_rows, head_key_rows, preferred_element_type=jnp.float32
            )
            * score_scale
        )
        return jnp.where(mask[:, None, :], scores, masked_score)

    def forward_head(head_args):
        head_query_rows, head_key_rows, head_value_rows = head_args
        scores = head_scores(head_query_rows, head_key_rows, key_valid)
        maxima = jnp.max(scores, -1, keepdims=True)
        exponent = jnp.exp(scores - maxima)
        totals_row = jnp.sum(exponent, -1, keepdims=True)
        probs = exponent / totals_row
        attended_head = jnp.einsum(
            "owz,ozf->owf",
            probs.astype(jnp.bfloat16),
            head_value_rows,
            preferred_element_type=jnp.float32,
        )
        return (attended_head, maxima[..., 0] + jnp.log(totals_row[..., 0]))

    attended_heads, log_total = lax.map(forward_head, (query_heads, key_heads, value_heads))
    attended = join_heads(attended_heads).reshape(row_count, model_width).astype(jnp.bfloat16)
    middle = (
        inputs + jnp.dot(attended, wide_out, preferred_element_type=jnp.float32) + bias_cols[:, 3]
    )
    h_two, norm_two_back = jax.vjp(layer_norm, middle, gain_cols[:, 1], bias_cols[:, 4])
    h_two_low = h_two.astype(jnp.bfloat16)
    preact = jnp.dot(h_two_low, wide_fc1, preferred_element_type=jnp.float32) + fc1_bias.astype(
        jnp.float32
    )
    activated, gelu_back = jax.vjp(partial(jax.nn.gelu, approximate=True), preact)
    activated_low = activated.astype(jnp.bfloat16)
    branch_two = last_dot(activated_low, wide_fc2) + bias_cols[:, 5]
    valid_rows = row_valid.reshape(row_count, 1)
    mixed = (valid_rows * (middle + branch_two)).reshape(images_here, slice_len, model_width)
    wide_qkv, wide_out, wide_fc1, wide_fc2 = (
        lax.all_gather(w_qkv, ("img", "seq"), axis=0, tiled=True),
        lax.all_gather(w_out, ("img", "seq"), axis=0, tiled=True),
        lax.all_gather(w_fc1, ("img", "seq"), axis=0, tiled=True),
        lax.all_gather(w_fc2, ("img", "seq"), axis=0, tiled=True),
    )
    grad_output = cotangent.astype(jnp.float32).reshape(row_count, model_width) * valid_rows
    grad_branch = grad_output.astype(jnp.bfloat16)
    grad_bias_two = jnp.sum(grad_branch.astype(jnp.float32), 0)
    grad_fc2_local = row_dot(grad_branch, activated_low)
    grad_activated = jnp.dot(grad_branch, wide_fc2, preferred_element_type=jnp.float32)
    (grad_preact,) = gelu_back(grad_activated)
    preact_low = grad_preact.astype(jnp.bfloat16)
    grad_hidden_bias = jnp.sum(preact_low.astype(jnp.float32), 0)
    grad_fc1_local = row_dot(h_two_low, preact_low)
    grad_h_two = last_dot(preact_low, wide_fc1)
    grad_middle_norm, grad_gain_two, grad_shift_two = norm_two_back(grad_h_two)
    grad_middle = grad_output + grad_middle_norm
    grad_branch_one = grad_middle.astype(jnp.bfloat16)
    grad_out_bias = jnp.sum(grad_branch_one.astype(jnp.float32), 0)
    output_gradient_shard = row_dot(attended, grad_branch_one)
    grad_attended = last_dot(grad_branch_one, wide_out).astype(jnp.bfloat16)
    grad_att_heads = split_heads(grad_attended, images_here, slice_len, head_count, head_dim)

    def backward_head(head_args):
        head_query_rows, head_key_rows, head_value_rows, head_gradient, total_head = head_args
        scores = head_scores(head_query_rows, head_key_rows, key_valid)
        probs = jnp.exp(scores - total_head[..., None])
        grad_probs = jnp.einsum(
            "asl,aul->asu", head_gradient, head_value_rows, preferred_element_type=jnp.float32
        )
        grad_scores = probs * (grad_probs - jnp.sum(probs * grad_probs, -1, keepdims=True))
        reduced_scores = grad_scores.astype(jnp.bfloat16)
        grad_query = (
            jnp.einsum(
                "owz,ozf->owf", reduced_scores, head_key_rows, preferred_element_type=jnp.float32
            )
            * score_scale
        )
        grad_key = (
            jnp.einsum(
                "xzl,xzv->xlv", reduced_scores, head_query_rows, preferred_element_type=jnp.float32
            )
            * score_scale
        )
        grad_value = jnp.einsum(
            "xzl,xzv->xlv",
            probs.astype(jnp.bfloat16),
            head_gradient,
            preferred_element_type=jnp.float32,
        )
        return (grad_query, grad_key, grad_value)

    grad_q_heads, grad_k_heads, grad_v_heads = lax.map(
        backward_head, (query_heads, key_heads, value_heads, grad_att_heads, log_total)
    )
    key_gradient_rows, grad_values = (
        lax.psum_scatter(
            join_heads(grad_k_heads).astype(jnp.bfloat16), "seq", scatter_dimension=1, tiled=True
        ).astype(jnp.float32),
        lax.psum_scatter(
            join_heads(grad_v_heads).astype(jnp.bfloat16), "seq", scatter_dimension=1, tiled=True
        ).astype(jnp.float32),
    )
    grad_projected = jnp.concatenate(
        [
            join_heads(grad_q_heads).reshape(row_count, model_width),
            key_gradient_rows.reshape(row_count, model_width),
            grad_values.reshape(row_count, model_width),
        ],
        1,
    ).astype(jnp.bfloat16)
    grad_query_bias = jnp.sum(grad_projected[:, :model_width].astype(jnp.float32), 0)
    grad_value_bias = jnp.sum(grad_projected[:, 2 * model_width :].astype(jnp.float32), 0)
    grad_qkv_local = row_dot(h_one_low, grad_projected)
    grad_h_one = last_dot(grad_projected, wide_qkv)
    grad_input_norm, grad_gain_one, grad_shift_one = norm_one_back(grad_h_one)
    grad_tokens = (grad_middle + grad_input_norm).reshape(images_here, slice_len, model_width)
    grad_gain_local = jnp.stack([grad_gain_one, grad_gain_two], 1)
    grad_bias_local = jnp.stack(
        [
            grad_shift_one,
            grad_query_bias,
            grad_value_bias,
            grad_out_bias,
            grad_shift_two,
            grad_bias_two,
        ],
        1,
    )
    owned = (
        lax.psum_scatter(grad_qkv_local, ("img", "seq"), scatter_dimension=0, tiled=True),
        lax.psum_scatter(output_gradient_shard, ("img", "seq"), scatter_dimension=0, tiled=True),
        lax.psum_scatter(grad_fc1_local, ("img", "seq"), scatter_dimension=0, tiled=True),
        lax.psum_scatter(grad_fc2_local, ("img", "seq"), scatter_dimension=0, tiled=True),
        lax.psum_scatter(grad_gain_local, ("img", "seq"), scatter_dimension=0, tiled=True),
        lax.psum_scatter(grad_bias_local, ("img", "seq"), scatter_dimension=0, tiled=True),
    )
    hidden_bias_total = lax.psum(grad_hidden_bias, ("img", "seq"))
    return (
        mixed,
        grad_tokens,
        owned[0],
        owned[1],
        owned[2],
        owned[3],
        owned[4],
        owned[5],
        hidden_bias_total,
    )


def solution(mesh):
    in_specs = (
        P("img", "seq", None),
        P("img"),
        P(("img", "seq"), None),
        P(("img", "seq"), None),
        P(("img", "seq"), None),
        P(("img", "seq"), None),
        P(("img", "seq"), None),
        P(("img", "seq"), None),
        P(),
        P("img", "seq", None),
    )
    out_specs = (
        P("img", "seq", None),
        P("img", "seq", None),
        P(("img", "seq"), None),
        P(("img", "seq"), None),
        P(("img", "seq"), None),
        P(("img", "seq"), None),
        P(("img", "seq"), None),
        P(("img", "seq"), None),
        P(),
    )
    shards = mesh.shape["img"] * mesh.shape["seq"]
    fits = mesh.shape["seq"] == 4 and shards == 2 * HEADS
    plan = whole_layer if fits else local
    return jax.shard_map(plan, mesh=mesh, in_specs=in_specs, out_specs=out_specs, check_vma=False)
```

```python
from functools import partial

import jax
import jax.numpy as jnp
from jax import lax
from jax.experimental import pallas as pl
from jax.experimental.pallas import tpu as pltpu
from jax.sharding import PartitionSpec as P

HEADS = 16
VALID = 729


masked_score = -1000000000.0
norm_epsilon = 1e-06


def layer_norm(values, gain_col, bias_col):
    average = jnp.mean(values, -1, keepdims=True)
    centered = values - average
    variance = jnp.mean(centered * centered, -1, keepdims=True)
    return centered * lax.rsqrt(variance + norm_epsilon) * gain_col + bias_col


def row_dot(left, right):
    return lax.dot_general(
        left, right, (((0,), (0,)), ((), ())), preferred_element_type=jnp.float32
    )


def last_dot(left, right):
    return lax.dot_general(
        left, right, (((1,), (1,)), ((), ())), preferred_element_type=jnp.float32
    )


def split_heads(tensor, images_here, count, head_count, head_dim):
    return tensor.reshape(images_here, count, head_count, head_dim).transpose(2, 0, 1, 3)


def join_heads(tensor):
    head_count, images_here, count, head_dim = tensor.shape
    return tensor.transpose(1, 2, 0, 3).reshape(images_here, count, head_count * head_dim)


VMEM_BYTES = 63 * 2**20
MESH_IDS = pl.DeviceIdType.MESH
F32 = jnp.float32
BF16 = jnp.bfloat16
LANES = 128
SLIVER = 16
PIECE = 48
BLOCK = 192
HEAD_ROWS = 80
NN = (((1,), (0,)), ((), ()))
NT = (((1,), (1,)), ((), ()))
TN = (((0,), (0,)), ((), ()))


def mm(left, right, dims):
    return lax.dot_general(left, right, dims, preferred_element_type=F32)


def normalize(values):
    average = jnp.mean(values, -1, keepdims=True)
    centered = values - average
    variance = jnp.mean(centered * centered, -1, keepdims=True)
    inverse = lax.rsqrt(variance + norm_epsilon)
    return centered * inverse, inverse


def norm_back(grad, gain, hat, inverse):
    scaled = grad * gain
    first = jnp.mean(scaled, -1, keepdims=True)
    second = jnp.mean(scaled * hat, -1, keepdims=True)
    return inverse * (scaled - first - hat * second)


def lane_ids(rows):
    return lax.broadcasted_iota(jnp.int32, (rows, LANES), 1)


def lane_window(tiles, start, width, lanes):
    tile, offset = divmod(start, LANES)
    if offset == 0:
        return tiles[tile]
    first = pltpu.roll(tiles[tile], LANES - offset, 1)
    if offset + width <= LANES:
        return first
    second = pltpu.roll(tiles[tile + 1], LANES - offset, 1)
    return jnp.where(lanes < LANES - offset, first, second)


def pack_lanes(parts, width, lanes):
    tiles = {}
    for n, part in enumerate(parts):
        tile, offset = divmod(n * width, LANES)
        if offset:
            part = pltpu.roll(part, offset, 1)
        ends = [(tile, lanes >= offset)]
        if offset + width > LANES:
            ends.append((tile + 1, lanes < offset + width - LANES))
        for to, where in ends:
            kept = jnp.where(where, part, 0.0)
            tiles[to] = tiles[to] + kept if to in tiles else kept
    return [tiles[to] for to in sorted(tiles)]


class Tiles:
    def __init__(self, ref, first, step, height):
        self.ref, self.first, self.step, self.height = ref, first, step, height
        self.wide = ref.shape[1] // LANES

    def __getitem__(self, tile):
        part, at = divmod(tile, self.wide)
        row = self.first + part * self.step
        return self.ref[row : row + self.height, at * LANES : (at + 1) * LANES]

    def fill(self, source):
        whole = self.wide * LANES
        rows, wide = source.shape
        for part in range(-(-wide // whole)):
            row = self.first + part * self.step
            width = min(whole, wide - part * whole)
            self.ref[row + rows // 16 * 16 : row + self.height, :] = jnp.zeros(
                (self.height - rows // 16 * 16, whole), F32
            )
            if width < whole:
                last = width // LANES * LANES
                self.ref[row : row + self.height, last : last + LANES] = jnp.zeros((self.height, LANES), F32)
            self.ref[row : row + rows, 0:width] = source[:, part * whole : part * whole + width].astype(F32)


def layer_kernel(
    dims,
    off_ref, w_qkv, w_out, w_fc1, w_fc2, gains, biases, fc1_bias, tok, cot,
    o_mixed, o_gtok, o_q, o_fo, o_1, o_2, o_fb, o_gains, o_biases,
    wq, wo, w1, w2, rq, ro, r1, r2, tmp,
    xs, gc, h1, h2, act, gp, dg, qkv, attm, att_t, lse,
    g1, g2, gq, y1, y2, yo, yq, z1, z2, zo, zq, s1, s2,
    sb_a, cr_a, xr_a, sb_b, cr_b, xr_b, pf, fb, prm, bh, sms, smr, shs, shr,
    ssem, rsem, lsem,
):
    slice_len, d, hd, f, qw, n_z = dims
    scale = hd ** (-0.5)
    mask_low = masked_score / scale
    chunk = 256
    rows = 4 * BLOCK
    i, s = lax.axis_index("img"), lax.axis_index("seq")
    z, y = lax.div(i, 2), lax.rem(i, 2)
    x, c = lax.div(s, 2), lax.rem(s, 2)
    k = 2 * c + x
    cy = c == y
    core_peer = (i, x * 2 + 1 - c)
    x_peer = (i, (1 - x) * 2 + c)
    y_peer = (z * 2 + 1 - y, s)
    rb = wq.shape[0] // (2 * n_z)
    own = rb // 4

    def z_at(t):
        return lax.rem(z + t + n_z, n_z)

    def z_dev(t):
        return (z_at(t) * 2 + y, s)

    def z_to(zt):
        return (zt * 2 + y, s)

    near = (
        z,
        jnp.where(z == 0, 1, z - 1),
        jnp.where(z == 0, 2, jnp.where(z == 3, 1, z + 1)),
        jnp.where(z <= 1, 3, 0),
    )
    middle = (z == 1) | (z == 2)
    end = jnp.where(z == 1, 0, 3)

    def s_at(t):
        return lax.rem(s + t + 4, 4)

    count = [0]

    def take(n=1):
        first = count[0]
        count[0] += n
        return first

    def copy(src, dst, index, device, at=None):
        return pltpu.make_async_remote_copy(
            src, dst, ssem.at[index], rsem.at[index if at is None else at], device_id=device, device_id_type=MESH_IDS
        )

    sends = []

    def send(src, dst, index, device, at=None):
        made = copy(src, dst, index, device, at)
        made.start()
        sends.append(made)

    def token_rows(j):
        return pl.ds(pl.multiple_of(j * BLOCK, BLOCK), BLOCK)

    half_block = BLOCK // 2
    halves = (slice(0, half_block), slice(half_block, BLOCK))

    def half_rows(j, p):
        return pl.ds(pl.multiple_of(j * BLOCK + p * half_block, 32), half_block)

    def img_rows(b):
        return pl.ds(pl.multiple_of(b * rb, 16), rb)

    def most_rows(b, most=rb - SLIVER):
        return pl.ds(pl.multiple_of(b * rb, 16), most)

    def sliver_rows(b):
        return pl.ds(pl.multiple_of(b * rb + rb - SLIVER, 16), SLIVER)

    barrier = pltpu.get_barrier_semaphore()
    partners = [(i, s_at(t)) for t in (1, 2, 3)] + [z_dev(t) for t in range(1, n_z)] + [y_peer]
    for partner in partners:
        pl.semaphore_signal(barrier, inc=1, device_id=partner, device_id_type=MESH_IDS)

    class Gather:
        def __init__(self, piece, recv, full, local_index):
            self.piece, self.recv, self.full = piece, recv, full
            self.width = full.shape[1]
            self.sp, self.sz, self.sy, self.ss = take(4), take(n_z), take(n_z), take(n_z)
            self.local = local_index
            self.started = []

        def pieces(self):
            self.own_piece().start()
            for t in (1, 2, 3):
                self.piece_to(t).start()

        def own_piece(self):
            return pltpu.make_async_copy(self.piece.at[s, 0:PIECE], self.recv.at[s], lsem.at[self.local])

        def piece_to(self, t):
            to = s_at(t)
            return copy(self.piece.at[to, 0:PIECE], self.recv.at[s], self.sp + t, (i, to))

        def assemble(self):
            self.own_piece().wait()
            for t in (1, 2, 3):
                self.piece_to(t).wait_send()
                came = self.recv.at[s_at(-t)]
                copy(came, came, self.sp + t, (i, s_at(-t))).wait_recv()
            part = rb // 4
            for j in range(4):
                tmp[part * j : part * j + PIECE, 0 : self.width] = self.recv[j].astype(F32)
            self.full[img_rows(i), :] = tmp[0:rb, 0 : self.width].astype(BF16)

        def block(self, zb, side):
            return self.full.at[img_rows(zb * 2 + side)]

        def most(self, zb, side):
            return self.full.at[most_rows(zb * 2 + side)]

        def sliver(self, zb, side):
            return self.full.at[sliver_rows(zb * 2 + side)]

        def slivers(self):
            whole, part = self.block(z, 1 - y), self.sliver(z, 1 - y)
            copy(whole, whole, self.sy, y_peer, self.sy + z).wait_recv()
            for u in (1, 2, 3):
                self.send(part, part, self.ss + u, z_to(near[u]), self.ss + z)

        def send(self, src, dst, index, device, at):
            made = copy(src, dst, index, device, at)
            made.start()
            self.started.append(made)

        def along_z(self):
            own = self.block(z, y)
            for u in (1, 2):
                self.send(own, own, self.sz + u, z_to(near[u]), self.sz + z)

            @pl.when(middle)
            def _():
                copy(own, own, self.sz + 3, z_to(near[3]), self.sz + z).start()

        def across_y(self):
            own = self.block(z, y)
            self.send(own, own, self.sy, y_peer, self.sy + z)

        def forward(self, *steps):
            for u in steps:
                zb = near[u]
                came = self.block(zb, y)
                copy(came, came, self.sz, z_to(zb), self.sz + zb).wait_recv()
                came = self.most(zb, y)
                copy(came, came, self.sy + u, y_peer, self.sy + zb).start()

        def relay(self):
            @pl.when(middle)
            def _():
                came = self.block(near[3], y)
                copy(came, came, self.sz, z_to(end), self.sz + near[3]).wait_recv()
                copy(came, came, self.sz, z_to(end), self.sz + near[3]).start()
                came = self.most(near[3], y)
                copy(came, came, self.sy + 3, y_peer, self.sy + near[3]).start()

        def forward_far(self):
            @pl.when(jnp.logical_not(middle))
            def _():
                self.forward(3)

        def finish(self):
            for u in (1, 2, 3):
                zb = near[u]
                came = self.most(zb, 1 - y)
                copy(came, came, self.sy, y_peer, self.sy + zb).wait_recv()
                came = self.sliver(zb, 1 - y)
                copy(came, came, self.ss, z_to(zb), self.ss + zb).wait_recv()

        def sent(self):
            for made in self.started:
                made.wait_send()

            @pl.when(middle)
            def _():
                own, came = self.block(z, y), self.block(near[3], y)
                copy(own, own, self.sz + 3, z_to(near[3]), self.sz + z).wait_send()
                copy(came, came, self.sz, z_to(end), self.sz + near[3]).wait_send()

            for u in (1, 2, 3):
                came = self.most(near[u], y)
                copy(came, came, self.sy + u, y_peer, self.sy + near[u]).wait_send()

    gather_q = Gather(yq, rq, wq, 0)
    gather_1 = Gather(y1, r1, w1, 1)
    gather_2 = Gather(y2, r2, w2, 2)
    o_piece, o_z, o_y = take(), take(n_z), take(n_z)

    def head_block(array, t):
        return array.at[pl.ds(pl.multiple_of(z_at(-t) * LANES, LANES), HEAD_ROWS)]

    po = yo.at[0, 0:PIECE]

    def o_start():
        @pl.when(cy)
        def _():
            pltpu.make_async_copy(po, ro.at[c], lsem.at[3]).start()

        @pl.when(jnp.logical_not(cy))
        def _():
            copy(po, ro.at[c], o_piece, core_peer).start()

    def o_assemble():
        @pl.when(jnp.logical_not(cy))
        def _():
            copy(po, ro.at[c], o_piece, core_peer).wait_send()

        for h in range(4):
            wo[h * LANES + HEAD_ROWS : (h + 1) * LANES, :] = jnp.zeros((LANES - HEAD_ROWS, d), BF16)

        @pl.when(cy)
        def _():
            pltpu.make_async_copy(po, ro.at[c], lsem.at[3]).wait()
            copy(po, ro.at[1 - c], o_piece, core_peer).wait_recv()
            for j in range(2):
                tmp[own * j : own * j + PIECE, :] = ro[j].astype(F32)
            wo[pl.ds(pl.multiple_of(z * LANES, LANES), HEAD_ROWS), :] = tmp[0:HEAD_ROWS, :].astype(BF16)

    def o_along_z():
        @pl.when(cy)
        def _():
            mine = head_block(wo, 0)
            for t in range(1, n_z):
                copy(mine, mine, o_z + t, z_dev(t)).start()
            copy(mine, mine, o_y, y_peer).start()

    def o_forward():
        @pl.when(cy)
        def _():
            for t in range(1, n_z):
                came = head_block(wo, t)
                copy(came, came, o_z + t, z_dev(-t)).wait_recv()
                copy(came, came, o_y + t, y_peer).start()

    def o_finish():
        @pl.when(jnp.logical_not(cy))
        def _():
            for t in range(n_z):
                came = head_block(wo, t)
                copy(came, came, o_y + t, y_peer).wait_recv()

    def o_sent():
        @pl.when(cy)
        def _():
            mine = head_block(wo, 0)
            for t in range(1, n_z):
                copy(mine, mine, o_z + t, z_dev(t)).wait_send()
            for t in range(n_z):
                came = head_block(wo, t)
                copy(came, came, o_y + t, y_peer).wait_send()

    class TokenGather:
        def __init__(self, full):
            self.full = full
            self.sx, self.sc, self.sd = take(2), take(2), take(2)

        def hop(self, j, p, index, device):
            rows_p = self.full.at[half_rows(j, p)]
            return copy(rows_p, rows_p, index + p, device)

        def start(self, *halves):
            for p in halves:
                self.hop(s, p, self.sx, x_peer).start()
                self.hop(s, p, self.sc, core_peer).start()

        def forward(self):
            for p in (0, 1):
                made = self.hop((1 - x) * 2 + c, p, self.sx, x_peer)
                made.wait_recv()
                self.hop((1 - x) * 2 + c, p, self.sd, core_peer).start()

        def wait_core(self):
            for p in (0, 1):
                self.hop(x * 2 + 1 - c, p, self.sc, core_peer).wait_recv()

        def wait_last(self):
            for p in (0, 1):
                self.hop((1 - x) * 2 + 1 - c, p, self.sd, core_peer).wait_recv()

        def take_step(self, t):
            pl.when(t == 1)(self.wait_core)
            pl.when(t == 2)(self.forward)
            pl.when(t == 3)(self.wait_last)

        def sent(self):
            for p in (0, 1):
                self.hop(s, p, self.sx, x_peer).wait_send()
                self.hop(s, p, self.sc, core_peer).wait_send()
                self.hop((1 - x) * 2 + c, p, self.sd, core_peer).wait_send()

        def finish(self):
            self.wait_core()
            self.wait_last()
            self.sent()

    class SeqSum:
        def __init__(self, partial, sb, cr, xr):
            self.partial, self.sb, self.cr, self.xr = partial, sb, cr, xr
            self.first, self.last = take(2), take(2)

        def to_core(self, slot):
            return copy(self.sb.at[slot], self.cr.at[slot], self.first + slot, core_peer)

        def to_chip(self, p):
            own_half = pl.ds(p * half_block, half_block)
            return copy(self.sb.at[2, own_half], self.xr.at[own_half], self.last + p, x_peer)

        def run(self, low=0, high=4):
            partial = self.partial

            def step(t, carry):
                away, slot = lax.rem(t, 2) == 0, lax.div(t, 2)
                if low < 2 < high:
                    pl.when(t == 2)(self.across)
                part = partial(jnp.where(t < 2, 1 - x, x) * 2 + jnp.where(away, 1 - c, c))

                @pl.when(away)
                def _():
                    self.sb[slot] = part.astype(BF16)
                    self.to_core(slot).start()

                @pl.when(jnp.logical_not(away))
                def _():
                    pf[slot] = part

                return carry

            lax.fori_loop(low, high, step, 0)

        def across(self):
            copy(self.cr.at[0], self.cr.at[0], self.first, core_peer).wait_recv()
            for p, at in enumerate(halves):
                self.sb[2, at, :] = (pf[0, at, :] + self.cr[0, at, :].astype(F32)).astype(BF16)
                self.to_chip(p).start()

        def finish(self, p):
            at = halves[p]
            if p == 0:
                copy(self.cr.at[1], self.cr.at[1], self.first + 1, core_peer).wait_recv()
            self.to_chip(p).wait_recv()
            self.to_chip(p).wait_send()
            self.to_core(p).wait_send()
            return pf[1, at, :] + self.cr[1, at, :].astype(F32) + self.xr[at, :].astype(F32)

    class Reduce:
        def __init__(self, grad, yr, zr, zs, fs, out):
            self.grad, self.yr, self.zr, self.zs, self.fs, self.out = grad, yr, zr, zs, fs, out
            self.most = rb if zs is None else rb - SLIVER
            self.width = grad.shape[1]
            self.sy, self.sz, self.sp, self.ss = take(n_z), take(n_z), take(4), take(n_z)

        def kept(self, j):
            return w1.at[pl.ds(pl.multiple_of(self.out + j * PIECE, 16), PIECE), 0 : self.width]

        def at(self, zb, side):
            return img_rows(zb * 2 + side)

        def across_y(self):
            for u in (3, 2, 1):
                b = near[u] * 2 + 1 - y
                send(self.grad.at[most_rows(b, self.most)], self.yr.at[u, 0 : self.most], self.sy + u, y_peer)
                if self.zs is not None:
                    send(self.grad.at[sliver_rows(b)], self.zs.at[z], self.ss + u, z_to(near[u]), self.ss + z)
            if self.zs is None:
                send(self.grad.at[img_rows(z * 2 + 1 - y)], self.yr.at[0], self.sy, y_peer)

        def across_last(self):
            b = z * 2 + 1 - y
            part = self.grad[sliver_rows(b), :].astype(F32)
            for u in (1, 2, 3):
                zb = near[u]
                copy(self.zs.at[zb], self.zs.at[zb], self.ss, z_to(zb), self.ss + zb).wait_recv()
                part += self.zs[zb].astype(F32)
            self.grad[sliver_rows(b), :] = part.astype(BF16)
            send(self.grad.at[img_rows(b)], self.yr.at[0], self.sy, y_peer)

        def along_z(self, *steps):
            for u in steps:
                came = self.yr.at[u, 0 : self.most]
                copy(came, came, self.sy + u, y_peer).wait_recv()
                mine, most = self.at(near[u], y), most_rows(near[u] * 2 + y, self.most)
                added = self.yr[u, 0 : self.most, :].astype(F32)
                self.grad[most, :] = (self.grad[most, :].astype(F32) + added).astype(BF16)
                if u < 3:
                    send(self.grad.at[mine], self.zr.at[z], self.sz + u, z_to(near[u]), self.sz + z)
                else:

                    @pl.when(jnp.logical_not(middle))
                    def _():
                        self.far().start()

        def far(self):
            rows_far = self.grad.at[self.at(near[3], y)]
            return copy(rows_far, self.zr.at[near[1]], self.sz + 3, z_to(near[1]), self.sz + near[1])

        def onward(self):
            rows_far = self.grad.at[self.at(near[3], y)]
            return copy(rows_far, self.zr.at[z], self.sz + 3, z_to(near[3]), self.sz + z)

        def relay(self):
            @pl.when(middle)
            def _():
                mine = self.at(near[3], y)
                copy(self.zr.at[z], self.zr.at[z], self.sz, z_to(end), self.sz + z).wait_recv()
                self.grad[mine, :] = (self.grad[mine, :].astype(F32) + self.zr[z].astype(F32)).astype(BF16)
                self.onward().start()

        def came_z(self, u):
            zb = near[u]
            copy(self.zr.at[zb], self.zr.at[zb], self.sz, z_to(zb), self.sz + zb).wait_recv()
            tmp[0:rb, 0 : self.width] += self.zr[zb].astype(F32)

        def pieces(self):
            copy(self.yr.at[0], self.yr.at[0], self.sy, y_peer).wait_recv()
            tmp[0:rb, 0 : self.width] = self.grad[self.at(z, y), :].astype(F32) + self.yr[0].astype(F32)
            self.came_z(1)
            self.came_z(2)

            @pl.when(middle)
            def _():
                self.came_z(3)

            part = rb // 4
            for j in range(4):
                self.fs[j] = tmp[part * j : part * j + PIECE, 0 : self.width].astype(BF16)
            pltpu.make_async_copy(self.fs.at[s], self.kept(s), lsem.at[4]).start()
            for t in (1, 2, 3):
                to = s_at(t)
                send(self.fs.at[to], self.kept(s), self.sp + t, (i, to))
            pltpu.make_async_copy(self.fs.at[s], self.kept(s), lsem.at[4]).wait()

        def sent(self):
            @pl.when(middle)
            def _():
                self.onward().wait_send()

            @pl.when(jnp.logical_not(middle))
            def _():
                self.far().wait_send()

        def finish(self):
            for t in (1, 2, 3):
                came = self.kept(s_at(-t))
                copy(came, came, self.sp + t, (i, s_at(-t))).wait_recv()

        def piece_tiles(self, j):
            row = self.out + j * PIECE
            return [
                w1[row : row + PIECE, t * LANES : (t + 1) * LANES].astype(F32) for t in range(self.width // LANES)
            ]

        def publish(self, tiles, out):
            for t, tile in enumerate(tiles):
                width = min(LANES, out.shape[1] - t * LANES)
                out[:, t * LANES : t * LANES + width] = tile[0:own, 0:width]

        def publish_wide(self, out):
            tiles = {}
            for j in range(4):
                tile, offset = divmod(j * f, LANES)
                for t, part in enumerate(self.piece_tiles(j)):
                    if offset:
                        part = pltpu.roll(part, offset, 1)
                    for to, where in ((tile + t, piece_lanes >= offset), (tile + t + 1, piece_lanes < offset)):
                        if to * LANES < 4 * f:
                            kept = jnp.where(where, part, 0.0)
                            tiles[to] = tiles[to] + kept if to in tiles else kept
            self.publish([tiles[to] for to in sorted(tiles)], out)

        def publish_heads(self, out):
            pieces = [self.piece_tiles(j) for j in range(4)]
            tiles = []
            for kind in range(3):
                parts = []
                for head in range(d // hd):
                    which, to = divmod(head, 4)
                    part = lane_window(pieces[2 * (to % 2) + to // 2], (4 * kind + which) * hd, hd, piece_lanes)
                    parts.append(jnp.where(piece_lanes < hd, part, 0.0))
                tiles += pack_lanes(parts, hd, piece_lanes)
            self.publish(tiles, out)

    reduce_2 = Reduce(g2, y2, z2, s2, r2, 0)
    reduce_1 = Reduce(g1, y1, z1, s1, r1, 4 * PIECE)
    reduce_q = Reduce(gq, yq, zq, None, rq, 8 * PIECE)
    go = wo
    ro_y, ro_z, ro_p = take(n_z), take(n_z), take()

    def ro_across_y():
        @pl.when(jnp.logical_not(cy))
        def _():
            for t in (*range(1, n_z), 0):
                copy(head_block(go, -t), yo.at[t], ro_y + t, y_peer).start()

    def ro_along_z():
        @pl.when(cy)
        def _():
            for t in range(1, n_z):
                copy(yo.at[t], yo.at[t], ro_y + t, y_peer).wait_recv()
                mine = pl.ds(pl.multiple_of(z_at(t) * LANES, LANES), HEAD_ROWS)
                go[mine, :] = (go[mine, :].astype(F32) + yo[t].astype(F32)).astype(BF16)
                copy(go.at[mine], zo.at[t - 1], ro_z + t, z_dev(t)).start()

    def ro_pieces():
        @pl.when(cy)
        def _():
            copy(yo.at[0], yo.at[0], ro_y, y_peer).wait_recv()
            mine = pl.ds(pl.multiple_of(z * LANES, LANES), HEAD_ROWS)
            total = go[mine, :].astype(F32) + yo[0].astype(F32)
            for t in range(1, n_z):
                copy(zo.at[t - 1], zo.at[t - 1], ro_z + t, z_dev(-t)).wait_recv()
                total += zo[t - 1].astype(F32)
            tmp[0:HEAD_ROWS, :] = total
            for j in range(2):
                ro[j] = tmp[own * j : own * j + PIECE, :].astype(BF16)
            pltpu.make_async_copy(ro.at[c], o_fo, lsem.at[5]).start()
            copy(ro.at[1 - c], o_fo, ro_p, core_peer).start()
            pltpu.make_async_copy(ro.at[c], o_fo, lsem.at[5]).wait()

    def ro_finish():
        @pl.when(cy)
        def _():
            for t in range(1, n_z):
                copy(head_block(go, -t), zo.at[t - 1], ro_z + t, z_dev(t)).wait_send()
            copy(ro.at[1 - c], o_fo, ro_p, core_peer).wait_send()

        @pl.when(jnp.logical_not(cy))
        def _():
            for t in range(n_z):
                copy(head_block(go, -t), yo.at[t], ro_y + t, y_peer).wait_send()
            copy(o_fo, o_fo, ro_p, core_peer).wait_recv()

    def arriving(t):
        return jnp.where(t < 2, x, 1 - x) * 2 + jnp.where(lax.rem(t, 2) == 0, c, 1 - c)

    def real_rows(j, width):
        t = lax.broadcasted_iota(jnp.int32, (BLOCK, width), 0)
        position = j * slice_len + t
        return (t < slice_len) & (position >= off_ref[0]) & (position < off_ref[0] + VALID)

    def half_of(rows_in, p):
        if p == 0:
            return rows_in[0, halves[0], :]
        pf[0, BLOCK - 16 : BLOCK, :] = jnp.zeros((16, d), F32)
        pf[0, half_block:slice_len, :] = rows_in[0, half_block:slice_len, :]
        return pf[0, halves[1], :]

    def put_half(rows_out, p, value):
        if p == 0:
            rows_out[0, halves[0], :] = value
        else:
            rows_out[0, half_block:slice_len, :] = value[0 : slice_len - half_block]

    tokens_in, cot_in = TokenGather(xs), TokenGather(gc)
    piece_lanes = lane_ids(PIECE)
    three = [Tiles(dg, PIECE * n, PIECE, PIECE) for n in range(3)]
    for n in range(3):
        three[n].fill(w_qkv.at[:, n * d : (n + 1) * d])
    small = Tiles(dg, 3 * PIECE, PIECE, PIECE)
    dg[3 * PIECE : 3 * PIECE + LANES, 0:LANES] = jnp.zeros((LANES, LANES), F32)
    dg[3 * PIECE : 3 * PIECE + 2, 0:own] = gains[...].astype(F32)
    dg[3 * PIECE + 2 : 3 * PIECE + 8, 0:own] = biases[...].astype(F32)
    dg[3 * PIECE : 3 * PIECE + LANES, 0:LANES] = dg[3 * PIECE : 3 * PIECE + LANES, 0:LANES].T
    for to in range(4):
        parts = []
        for n in range(12):
            kind, which = divmod(n, 4)
            head = 4 * which + 2 * (to % 2) + to // 2
            part = lane_window(three[kind], head * hd, hd, piece_lanes)
            parts.append(jnp.where(piece_lanes < hd, part, 0.0))
        tiles = pack_lanes(parts, hd, piece_lanes)
        tiles[-1] = tiles[-1] + pltpu.roll(small[0], 12 * hd % LANES, 1)
        for at, tile in enumerate(tiles):
            yq[to, 0:PIECE, at * LANES : (at + 1) * LANES] = tile.astype(BF16)
    pl.semaphore_wait(barrier, len(partners))
    gather_q.pieces()
    pf[0, BLOCK - 16 : BLOCK, :] = jnp.zeros((16, d), F32)
    pf[0, 0:slice_len, :] = tok[0].astype(F32)
    xs[token_rows(s), :] = pf[0].astype(BF16)
    tokens_in.start(0, 1)
    out_rows = Tiles(dg, 12 * PIECE, PIECE, PIECE)
    out_rows.fill(w_out)
    for at in range(d // LANES):
        yo[0, 0:PIECE, at * LANES : (at + 1) * LANES] = out_rows[at].astype(BF16)
    o_start()
    def cut_wide(weights, first, pieces, gather):
        wide = Tiles(dg, first * PIECE, PIECE, PIECE)
        wide.fill(weights)
        for to in range(4):
            for at in range(w1.shape[1] // LANES):
                start = to * f + at * LANES
                width = min(LANES, f - at * LANES)
                part = lane_window(wide, start, width, piece_lanes)
                if width < LANES:
                    part = jnp.where(piece_lanes < width, part, 0.0)
                pieces[to, 0:PIECE, at * LANES : (at + 1) * LANES] = part.astype(BF16)
        gather.pieces()

    sms[0] = jnp.zeros(sms.shape[1:], F32)
    shs[0] = jnp.zeros(shs.shape[1:], F32)
    tmp[...] = jnp.zeros(tmp.shape, F32)

    gather_q.assemble()
    gather_q.along_z()
    gather_q.across_y()
    o_assemble()
    o_along_z()
    cut_wide(w_fc1, 4, y1, gather_1)
    gather_q.forward(1)
    tokens_in.forward()
    cut_wide(w_fc2, 8, y2, gather_2)
    pf[1, BLOCK - 16 : BLOCK, :] = jnp.zeros((16, d), F32)
    pf[1, 0:slice_len, :] = cot[0].astype(F32)
    gc[token_rows(s), :] = jnp.where(real_rows(s, d), pf[1], 0.0).astype(BF16)
    cot_in.start(0, 1)
    gather_1.assemble()
    gather_q.slivers()
    gather_q.forward(2)
    gather_q.relay()
    gather_1.along_z()
    gather_1.across_y()
    gather_2.assemble()
    gather_q.forward_far()
    o_forward()
    gather_2.across_y()
    cot_in.forward()
    tokens_in.finish()
    gather_q.finish()

    packed = 3 * 4 * hd
    base = packed // LANES * LANES
    columns = wq[:, base : base + LANES].astype(F32)
    prm[...] = columns.T[packed - base : packed - base + 8, :]
    one_lane = lane_ids(1)
    for which, row in ((0, 3), (1, 4)):
        tiles = [prm[row : row + 1, LANES * t : LANES * (t + 1)] for t in range(d // LANES)]
        for head in range(d // hd):
            bh[which, head : head + 1, :] = lane_window(tiles, head * hd, hd, one_lane)
    gain_one, gain_two, shift_one = prm[0:1, :], prm[1:2, :], prm[2:3, :]
    bias_out, shift_two, bias_two = prm[5:6, :], prm[6:7, :], prm[7:8, :]

    lanes = lane_ids(BLOCK)

    def project(j, carry):
        hat, _ = normalize(xs[token_rows(j), :].astype(F32))
        low = (hat * gain_one + shift_one).astype(BF16)
        h1[token_rows(j), :] = low
        wide = mm(low, wq[...], NN)
        tiles = [wide[:, LANES * t : LANES * (t + 1)] for t in range(qw // LANES)]
        key_low = jnp.where(real_rows(j, LANES), 0.0, mask_low)
        for n in range(12):
            kind, head = divmod(n, 4)
            part = lane_window(tiles, n * hd, hd, lanes)
            if kind != 1:
                part = part + bh[kind // 2, pl.ds(4 * head + k, 1), :]
            beside = key_low if kind == 1 else jnp.ones_like(part)
            part = jnp.where(lanes < hd, part, jnp.where(lanes == hd, beside, 0.0))
            qkv[n, token_rows(j), :] = part.astype(BF16)
        return carry

    lax.fori_loop(0, 4, project, 0)
    gather_1.slivers()
    gather_2.along_z()
    half = rows // 2
    sublanes = lax.broadcasted_iota(jnp.int32, (LANES, half), 0)

    def attend(step, carry):
        head, part = lax.rem(step, 4), jnp.where(step < 4, 1 - x, x)
        at = pl.ds(pl.multiple_of(part * half, LANES), half)
        scores = mm(qkv[4 + head], qkv[head, at, :], NT)
        top = jnp.max(scores, 0, keepdims=True)
        weights = jnp.exp((scores - top) * scale).astype(BF16)
        summed = mm(qkv[8 + head], weights, TN)
        total = summed[hd : hd + 1, :]
        result = jnp.where(sublanes < hd, summed / total, 0.0)
        att_t[head, :, at] = result.astype(BF16)
        attm[at, pl.ds(pl.multiple_of(head * LANES, LANES), LANES)] = result.T.astype(BF16)
        lse[head, :, at] = top * scale + jnp.log(total)
        return carry

    lax.fori_loop(0, 4, attend, 0)
    gather_1.forward(1)
    o_finish()
    sum_one = SeqSum(lambda j: mm(attm[token_rows(j), :], wo[...], NN), sb_a, cr_a, xr_a)
    sum_one.run(0, 2)
    sum_one.across()
    lax.fori_loop(4, 8, attend, 0)
    sum_one.run(2, 4)
    gather_1.relay()
    gather_2.slivers()
    gather_1.forward(2)
    cot_in.finish()
    bias_parts = Tiles(dg, 14 * PIECE, 8, 8)
    bias_parts.fill(fc1_bias[...].astype(F32)[None])
    row_lanes = lane_ids(8)
    for at in range(w1.shape[1] // LANES):
        width = min(LANES, f - at * LANES)
        mine = jnp.zeros((8, LANES), F32)
        for to in range(4):
            part = lane_window(bias_parts, to * f + at * LANES, width, row_lanes)
            mine = jnp.where(s == to, part, mine)
        fb[:, at * LANES : (at + 1) * LANES] = jnp.where(row_lanes < width, mine, 0.0)[0:1]

    gather_1.forward_far()
    h2_in = TokenGather(h2)
    for p in (0, 1):
        middle_rows = xs[half_rows(s, p), :].astype(F32) + sum_one.finish(p) + bias_out
        put_half(o_mixed, p, middle_rows)
        hat, _ = normalize(middle_rows)
        h2[half_rows(s, p), :] = (hat * gain_two + shift_two).astype(BF16)
        h2_in.start(p)
    gather_2.forward(1)
    gather_1.finish()

    slope = (2.0 / 3.141592653589793) ** 0.5

    def widen(t, carry):
        h2_in.take_step(t)
        j = arriving(t)
        pre = mm(h2[token_rows(j), :], w1[...], NN) + fb[...]
        square = pre * pre
        curve = jnp.tanh(slope * pre * (1.0 + 0.044715 * square))
        half = 0.5 + 0.5 * curve
        act[token_rows(j), :] = (pre * half).astype(BF16)
        dg[token_rows(j), :] = half + 0.5 * slope * pre * (1.0 - curve * curve) * (1.0 + 0.134145 * square)
        return carry

    lax.fori_loop(0, 2, widen, 0)
    gather_2.forward(2)
    gather_2.relay()
    lax.fori_loop(2, 4, widen, 0)
    h2_in.sent()
    gather_2.forward_far()

    def column_products(left, right, out):
        def step(t, carry):
            at = pl.ds(pl.multiple_of(t * LANES, LANES), LANES)
            out[at, :] = mm(left[:, at], right[...], TN).astype(BF16)
            return carry

        lax.fori_loop(0, left.shape[1] // LANES, step, 0)

    column_products(gc, act, g2)
    reduce_2.across_y()
    gather_2.finish()

    def hidden_back(j):
        at = token_rows(j)
        low = (mm(gc[at, :], w2[...], NN) * dg[at, :]).astype(BF16)
        gp[at, :] = low
        column = jnp.sum(low.astype(F32), 0, keepdims=True)
        sms[0, 6:7, :] += column
        return mm(low, w1[...], NT)

    gather_1.sent()
    sum_two = SeqSum(hidden_back, sb_a, cr_a, xr_a)
    sum_two.run()
    reduce_2.across_last()
    column_products(h2, gp, g1)
    reduce_1.across_y()
    reduce_2.along_z(3)
    reduce_2.along_z(2)
    gb_in = TokenGather(gc)
    for p in (0, 1):
        grad_h = sum_two.finish(p)
        hat, inverse = normalize(half_of(o_mixed, p))
        kept = gc[half_rows(s, p), :].astype(F32)
        grad_x = kept + norm_back(grad_h, gain_two, hat, inverse)
        put_half(o_gtok, p, grad_x)
        low = grad_x.astype(BF16)
        gc[half_rows(s, p), :] = low
        gb_in.start(p)
        for row, column in ((1, grad_h * hat), (4, grad_h), (5, kept), (3, low.astype(F32))):
            sms[0, row : row + 1, :] += jnp.sum(column, 0, keepdims=True)

    sum_three = SeqSum(lambda j: mm(act[token_rows(j), :], w2[...], NT), sb_b, cr_b, xr_b)
    sum_three.run()
    reduce_2.along_z(1)
    reduce_1.across_last()

    def attended_back(t, carry):
        gb_in.take_step(t)
        j = arriving(t)
        attm[token_rows(j), :] = mm(gc[token_rows(j), :], wo[...], NT).astype(BF16)
        return carry

    lax.fori_loop(0, 4, attended_back, 0)
    gb_in.sent()

    o_sent()

    def out_products(head, carry):
        at = pl.ds(pl.multiple_of(head * LANES, LANES), LANES)
        go[at, :] = mm(att_t[head], gc[...], NN).astype(BF16)
        return carry

    lax.fori_loop(0, 4, out_products, 0)
    ro_across_y()
    reduce_2.relay()

    wide_lanes = lane_ids(rows)
    chunk_lanes = lane_ids(chunk)

    def attend_back(head, carry):
        grad_k = jnp.zeros((rows, LANES), F32)
        grad_v = jnp.zeros((rows, LANES), F32)
        grad_q = []
        for part in range(rows // chunk):
            at = slice(part * chunk, (part + 1) * chunk)
            query, grad_out = qkv[head, at, :], attm[at, pl.ds(pl.multiple_of(head * LANES, LANES), LANES)]
            scores = mm(qkv[4 + head], query, NT)
            probs = jnp.exp(scores * scale - lse[head, :, at])
            grad_p = mm(qkv[8 + head], grad_out, NT)
            delta = jnp.sum(probs * grad_p, 0, keepdims=True)
            grad_s = (probs * (grad_p - delta)).astype(BF16)
            grad_k += mm(grad_s, query, NN)
            grad_v += mm(probs.astype(BF16), grad_out, NN)
            grad_q.append(mm(qkv[4 + head], grad_s, TN))
        for part in range(rows // chunk):
            at = slice(part * chunk, (part + 1) * chunk)
            low = jnp.where(chunk_lanes < hd, grad_q[part].T * scale, 0.0).astype(BF16)
            qkv[head, at, :] = low
            shs[0, pl.ds(4 * head + k, 1), :] += jnp.sum(low.astype(F32), 0, keepdims=True)
        qkv[4 + head] = jnp.where(wide_lanes < hd, grad_k * scale, 0.0).astype(BF16)
        low = grad_v.astype(BF16)
        qkv[8 + head] = low
        shs[0, pl.ds(16 + 4 * head + k, 1), :] = jnp.sum(low.astype(F32), 0, keepdims=True)
        return carry

    reduce_1.along_z(3)
    lax.fori_loop(0, 2, attend_back, 0)
    reduce_1.along_z(2)
    lax.fori_loop(2, 4, attend_back, 0)
    reduce_1.along_z(1)
    reduce_1.relay()

    for p, at in enumerate(halves):
        total = half_of(o_mixed, p) + sum_three.finish(p) + bias_two
        put_half(o_mixed, p, jnp.where(real_rows(s, d)[at], total, 0.0))
    gpj = h2.at[:, 0:qw]

    def pack(j, carry):
        parts = [qkv[n, token_rows(j), :].astype(F32) for n in range(12)]
        for to, tile in enumerate(pack_lanes(parts, hd, lanes)):
            gpj[token_rows(j), LANES * to : LANES * (to + 1)] = tile.astype(BF16)
        return carry

    lax.fori_loop(0, 4, pack, 0)

    def tokens_back(j):
        part = mm(gpj[token_rows(j), :], wq[...], NT)
        hat, _ = normalize(xs[token_rows(j), :].astype(F32))
        sms[0, 0:1, :] += jnp.sum(part * hat, 0, keepdims=True)
        sms[0, 2:3, :] += jnp.sum(part, 0, keepdims=True)
        return part

    sum_four = SeqSum(tokens_back, sb_a, cr_a, xr_a)
    sum_four.run()
    sm_at, sh_at = take(7), take(7)

    def vectors(stage, slots, devices):
        for slot, device in zip(slots, devices, strict=True):
            send(sms.at[stage], smr.at[slot], sm_at + slot, device)
            send(shs.at[stage], shr.at[slot], sh_at + slot, device)

    def vectors_sum(stage, slots, devices):
        for slot, device in zip(slots, devices, strict=True):
            copy(smr.at[slot], smr.at[slot], sm_at + slot, device).wait_recv()
            copy(shr.at[slot], shr.at[slot], sh_at + slot, device).wait_recv()
        total, heads = sms[stage], shs[stage]
        for slot in slots:
            total += smr[slot]
            heads += shr[slot]
        return total, heads

    z_to_all, z_from_all = [z_dev(t) for t in (1, 2, 3)], [z_dev(-t) for t in (1, 2, 3)]
    s_to_all, s_from_all = [(i, s_at(t)) for t in (1, 2, 3)], [(i, s_at(-t)) for t in (1, 2, 3)]
    vectors(0, (0,), (y_peer,))
    column_products(h1, gpj, gq)
    reduce_q.across_y()
    sms[1], shs[1] = vectors_sum(0, (0,), (y_peer,))
    vectors(1, (1, 2, 3), z_to_all)
    ro_along_z()
    reduce_2.pieces()
    reduce_q.along_z(3, 2)
    reduce_q.relay()
    for p in (0, 1):
        grad_h = sum_four.finish(p)
        hat, inverse = normalize(xs[half_rows(s, p), :].astype(F32))
        put_half(o_gtok, p, half_of(o_gtok, p) + norm_back(grad_h, gain_one, hat, inverse))
    reduce_q.along_z(1)
    sms[2], shs[2] = vectors_sum(1, (1, 2, 3), z_from_all)
    vectors(2, (4, 5, 6), s_to_all)
    reduce_1.pieces()
    reduce_2.finish()
    reduce_2.publish_wide(o_2)
    ro_pieces()
    reduce_q.pieces()
    reduce_1.finish()
    reduce_1.publish_wide(o_1)
    summed_rows, by_head = vectors_sum(2, (4, 5, 6), s_from_all)
    prm[pl.ds(s, 1), :] = sms[2, 6:7, :]
    for t in (1, 2, 3):
        prm[pl.ds(s_at(-t), 1), :] = smr[3 + t, 6:7, :]
    mine = smr.at[1]
    for to, row in enumerate((0, 1, 2, None, None, 3, 4, 5)):
        if row is not None:
            mine[to : to + 1, :] = summed_rows[row : row + 1, :]
    for which in range(2):
        heads = [by_head[16 * which + head : 16 * which + head + 1, :] for head in range(d // hd)]
        for to, tile in enumerate(pack_lanes(heads, hd, one_lane)):
            mine[3 + which : 4 + which, to * LANES : (to + 1) * LANES] = tile
    start = (i * 4 + s) * own
    turned = pltpu.roll(mine[0:8, :], lax.rem(d - start, d), 1)
    o_gains[...] = turned[0:2, 0:own]
    o_biases[...] = turned[2:8, 0:own]
    spread = {}
    for j in range(4):
        tile, offset = divmod(j * f, LANES)
        for t in range(w1.shape[1] // LANES):
            part = prm[j : j + 1, t * LANES : (t + 1) * LANES]
            if offset:
                part = pltpu.roll(part, offset, 1)
            for to, where in ((tile + t, one_lane >= offset), (tile + t + 1, one_lane < offset)):
                if to * LANES < 4 * f:
                    kept = jnp.where(where, part, 0.0)
                    spread[to] = spread[to] + kept if to in spread else kept
    for to, tile in spread.items():
        width = min(LANES, 4 * f - to * LANES)
        o_fb[:, to * LANES : to * LANES + width] = tile[:, 0:width]
    ro_finish()
    reduce_q.finish()
    reduce_q.publish_heads(o_q)
    for part in (gather_q, gather_2, reduce_q, reduce_1, reduce_2):
        part.sent()
    for made in sends:
        made.wait_send()


def hand_over(mixed, tokens, g_qkv, g_1, g_2, g_out, g_gains, g_biases, g_fb, *outs):
    o_mixed, o_tokens, o_qkv, o_1, o_2, o_out, o_gains, o_biases, o_fb = outs
    o_qkv[...] = g_qkv[...]
    o_1[...] = g_1[...]
    o_2[...] = g_2[...]
    o_mixed[:, 0, :] = mixed[0]
    o_tokens[:, 0, :] = tokens[0]
    o_out[...] = g_out[0 : o_out.shape[0], :].astype(F32)
    o_gains[...] = g_gains[...]
    o_biases[...] = g_biases[...]
    o_fb[...] = g_fb[0]


def whole_layer(tokens, offsets, w_qkv, w_out, w_fc1, w_fc2, gains, biases, fc1_bias, cotangent):
    _, slice_len, d = tokens.shape
    hd = d // HEADS
    own, wide = w_fc1.shape
    f = wide // 4
    f_pad = -(-f // LANES) * LANES
    packed = 12 * hd
    qw = -(-(packed + 8) // LANES) * LANES
    n_z = lax.axis_size("img") // 2
    rb = own * 4
    rows = 4 * BLOCK

    hbm = pl.BlockSpec(memory_space=pl.ANY)
    vmem = pl.BlockSpec(memory_space=pltpu.VMEM)
    outs = [
        ((1, slice_len, d), F32, vmem),
        ((1, slice_len, d), F32, vmem),
        ((own, 3 * d), F32, vmem),
        ((PIECE, d), BF16, hbm),
        ((own, wide), F32, vmem),
        ((own, wide), F32, vmem),
        ((1, wide), F32, vmem),
        ((2, own), F32, vmem),
        ((6, own), F32, vmem),
    ]
    low = [
        (d, qw), (4 * LANES, d), (d, f_pad), (d, f_pad),
        (4, PIECE, qw), (2, PIECE, d), (4, PIECE, f_pad), (4, PIECE, f_pad),
    ]
    scratch = [pltpu.VMEM(shape, BF16) for shape in low]
    scratch += [pltpu.VMEM((160, max(d, f_pad)), F32)]
    scratch += [pltpu.VMEM((rows, w), BF16) for w in (d, d, d, d, f_pad, f_pad)]
    scratch += [pltpu.VMEM((rows, f_pad), F32)]
    scratch += [
        pltpu.VMEM((12, rows, LANES), BF16),
        pltpu.VMEM((rows, 4 * LANES), BF16),
        pltpu.VMEM((4, LANES, rows), BF16),
        pltpu.VMEM((4, 1, rows), F32),
    ]
    scratch += [pltpu.VMEM(shape, BF16) for shape in ((d, f_pad), (d, f_pad), (d, qw))]
    scratch += [pltpu.VMEM((n_z, h, w), BF16) for h, w in ((rb, f_pad), (rb, f_pad), (HEAD_ROWS, d), (rb, qw))]
    scratch += [pltpu.VMEM((n_z, h, w), BF16) for h, w in ((rb, f_pad), (rb, f_pad), (HEAD_ROWS, d), (rb, qw))]
    scratch += [pltpu.VMEM((n_z, SLIVER, w), BF16) for w in (f_pad, f_pad)]
    for _ in range(2):
        scratch += [pltpu.VMEM((n, BLOCK, d), BF16) for n in (3, 2)] + [pltpu.VMEM((BLOCK, d), BF16)]
    scratch += [
        pltpu.VMEM((2, BLOCK, d), F32),
        pltpu.VMEM((1, f_pad), F32),
        pltpu.VMEM((8, d), F32),
        pltpu.VMEM((2, 16, LANES), F32),
        pltpu.VMEM((3, 8, d), F32),
        pltpu.VMEM((7, 8, d), F32),
        pltpu.VMEM((3, 32, LANES), F32),
        pltpu.VMEM((7, 32, LANES), F32),
        pltpu.SemaphoreType.DMA((200,)),
        pltpu.SemaphoreType.DMA((200,)),
        pltpu.SemaphoreType.DMA((8,)),
    ]
    mixed, grad_tokens, gq, go, g1, g2, g_fb, g_gains, g_biases = pl.pallas_call(
        partial(layer_kernel, (slice_len, d, hd, f, qw, n_z)),
        out_shape=[jax.ShapeDtypeStruct(shape, kind) for shape, kind, _ in outs],
        in_specs=[pl.BlockSpec(memory_space=pltpu.SMEM)] + [vmem] * 9,
        out_specs=[spec for _, _, spec in outs],
        scratch_shapes=scratch,
        compiler_params=pltpu.CompilerParams(
            collective_id=0, has_side_effects=True, vmem_limit_bytes=VMEM_BYTES
        ),
    )(offsets, w_qkv, w_out, w_fc1, w_fc2, gains.T, biases.T, fc1_bias, tokens, cotangent)

    rows_out = jax.ShapeDtypeStruct((slice_len, 1, d), F32)
    same = [jax.ShapeDtypeStruct(made.shape, F32) for made in (gq, g1, g2)]
    rest = [jax.ShapeDtypeStruct(shape, F32) for shape in ((own, d), (2, own), (6, own), (wide,))]
    mixed, grad_tokens, gq, g1, g2, go, g_gains, g_biases, g_fb = pl.pallas_call(
        hand_over,
        out_shape=[rows_out, rows_out, *same, *rest],
        in_specs=[vmem] * 9,
        out_specs=[vmem] * 9,
    )(mixed, grad_tokens, gq, g1, g2, go, g_gains, g_biases, g_fb)
    mixed, grad_tokens = mixed.reshape(tokens.shape), grad_tokens.reshape(tokens.shape)
    return mixed, grad_tokens, gq, go, g1, g2, g_gains.T, g_biases.T, g_fb


def local(tokens, offsets, w_qkv, w_out, w_fc1, w_fc2, gains, biases, fc1_bias, cotangent):
    images_here, slice_len, model_width = tokens.shape
    head_count = HEADS
    head_dim = model_width // head_count
    length = slice_len * lax.axis_size("seq")
    row_count = images_here * slice_len
    score_scale = head_dim ** (-0.5)
    gathered = (
        lax.all_gather(w_qkv, ("img", "seq"), axis=0, tiled=True),
        lax.all_gather(w_out, ("img", "seq"), axis=0, tiled=True),
        lax.all_gather(w_fc1, ("img", "seq"), axis=0, tiled=True),
        lax.all_gather(w_fc2, ("img", "seq"), axis=0, tiled=True),
        lax.all_gather(gains, ("img", "seq"), axis=0, tiled=True),
        lax.all_gather(biases, ("img", "seq"), axis=0, tiled=True),
    )
    wide_qkv, wide_out, wide_fc1, wide_fc2, gain_all, bias_all = gathered
    gain_cols = gain_all.astype(jnp.float32)
    bias_cols = bias_all.astype(jnp.float32)
    starts = offsets[:, None]
    positions = lax.axis_index("seq") * slice_len + jnp.arange(slice_len, dtype=jnp.int32)
    own_valid = (positions[None, :] >= starts) & (positions[None, :] < starts + VALID)
    row_valid = own_valid.astype(jnp.float32)
    key_pos = jnp.arange(length, dtype=jnp.int32)
    key_valid = (key_pos[None, :] >= starts) & (key_pos[None, :] < starts + VALID)
    inputs = tokens.astype(jnp.float32).reshape(row_count, model_width)
    h_one, norm_one_back = jax.vjp(layer_norm, inputs, gain_cols[:, 0], bias_cols[:, 0])
    h_one_low = h_one.astype(jnp.bfloat16)
    qkv_bias = jnp.concatenate([bias_cols[:, 1], jnp.zeros_like(bias_cols[:, 1]), bias_cols[:, 2]])
    projected = (
        jnp.dot(h_one_low, wide_qkv, preferred_element_type=jnp.float32) + qkv_bias
    ).astype(jnp.bfloat16)
    query_rows = projected[:, :model_width]
    key_rows = projected[:, model_width : 2 * model_width].reshape(
        images_here, slice_len, model_width
    )
    value_rows = projected[:, 2 * model_width :].reshape(images_here, slice_len, model_width)
    keys_all, values_all = (
        lax.all_gather(key_rows, "seq", axis=1, tiled=True),
        lax.all_gather(value_rows, "seq", axis=1, tiled=True),
    )
    query_heads = split_heads(query_rows, images_here, slice_len, head_count, head_dim)
    key_heads = split_heads(keys_all, images_here, length, head_count, head_dim)
    value_heads = split_heads(values_all, images_here, length, head_count, head_dim)

    def head_scores(head_query_rows, head_key_rows, mask):
        scores = (
            jnp.einsum(
                "asl,aul->asu", head_query_rows, head_key_rows, preferred_element_type=jnp.float32
            )
            * score_scale
        )
        return jnp.where(mask[:, None, :], scores, masked_score)

    def forward_head(head_args):
        head_query_rows, head_key_rows, head_value_rows = head_args
        scores = head_scores(head_query_rows, head_key_rows, key_valid)
        maxima = jnp.max(scores, -1, keepdims=True)
        exponent = jnp.exp(scores - maxima)
        totals_row = jnp.sum(exponent, -1, keepdims=True)
        probs = exponent / totals_row
        attended_head = jnp.einsum(
            "owz,ozf->owf",
            probs.astype(jnp.bfloat16),
            head_value_rows,
            preferred_element_type=jnp.float32,
        )
        return (attended_head, maxima[..., 0] + jnp.log(totals_row[..., 0]))

    attended_heads, log_total = lax.map(forward_head, (query_heads, key_heads, value_heads))
    attended = join_heads(attended_heads).reshape(row_count, model_width).astype(jnp.bfloat16)
    middle = (
        inputs + jnp.dot(attended, wide_out, preferred_element_type=jnp.float32) + bias_cols[:, 3]
    )
    h_two, norm_two_back = jax.vjp(layer_norm, middle, gain_cols[:, 1], bias_cols[:, 4])
    h_two_low = h_two.astype(jnp.bfloat16)
    preact = jnp.dot(h_two_low, wide_fc1, preferred_element_type=jnp.float32) + fc1_bias.astype(
        jnp.float32
    )
    activated, gelu_back = jax.vjp(partial(jax.nn.gelu, approximate=True), preact)
    activated_low = activated.astype(jnp.bfloat16)
    branch_two = last_dot(activated_low, wide_fc2) + bias_cols[:, 5]
    valid_rows = row_valid.reshape(row_count, 1)
    mixed = (valid_rows * (middle + branch_two)).reshape(images_here, slice_len, model_width)
    wide_qkv, wide_out, wide_fc1, wide_fc2 = (
        lax.all_gather(w_qkv, ("img", "seq"), axis=0, tiled=True),
        lax.all_gather(w_out, ("img", "seq"), axis=0, tiled=True),
        lax.all_gather(w_fc1, ("img", "seq"), axis=0, tiled=True),
        lax.all_gather(w_fc2, ("img", "seq"), axis=0, tiled=True),
    )
    grad_output = cotangent.astype(jnp.float32).reshape(row_count, model_width) * valid_rows
    grad_branch = grad_output.astype(jnp.bfloat16)
    grad_bias_two = jnp.sum(grad_branch.astype(jnp.float32), 0)
    grad_fc2_local = row_dot(grad_branch, activated_low)
    grad_activated = jnp.dot(grad_branch, wide_fc2, preferred_element_type=jnp.float32)
    (grad_preact,) = gelu_back(grad_activated)
    preact_low = grad_preact.astype(jnp.bfloat16)
    grad_hidden_bias = jnp.sum(preact_low.astype(jnp.float32), 0)
    grad_fc1_local = row_dot(h_two_low, preact_low)
    grad_h_two = last_dot(preact_low, wide_fc1)
    grad_middle_norm, grad_gain_two, grad_shift_two = norm_two_back(grad_h_two)
    grad_middle = grad_output + grad_middle_norm
    grad_branch_one = grad_middle.astype(jnp.bfloat16)
    grad_out_bias = jnp.sum(grad_branch_one.astype(jnp.float32), 0)
    output_gradient_shard = row_dot(attended, grad_branch_one)
    grad_attended = last_dot(grad_branch_one, wide_out).astype(jnp.bfloat16)
    grad_att_heads = split_heads(grad_attended, images_here, slice_len, head_count, head_dim)

    def backward_head(head_args):
        head_query_rows, head_key_rows, head_value_rows, head_gradient, total_head = head_args
        scores = head_scores(head_query_rows, head_key_rows, key_valid)
        probs = jnp.exp(scores - total_head[..., None])
        grad_probs = jnp.einsum(
            "asl,aul->asu", head_gradient, head_value_rows, preferred_element_type=jnp.float32
        )
        grad_scores = probs * (grad_probs - jnp.sum(probs * grad_probs, -1, keepdims=True))
        reduced_scores = grad_scores.astype(jnp.bfloat16)
        grad_query = (
            jnp.einsum(
                "owz,ozf->owf", reduced_scores, head_key_rows, preferred_element_type=jnp.float32
            )
            * score_scale
        )
        grad_key = (
            jnp.einsum(
                "xzl,xzv->xlv", reduced_scores, head_query_rows, preferred_element_type=jnp.float32
            )
            * score_scale
        )
        grad_value = jnp.einsum(
            "xzl,xzv->xlv",
            probs.astype(jnp.bfloat16),
            head_gradient,
            preferred_element_type=jnp.float32,
        )
        return (grad_query, grad_key, grad_value)

    grad_q_heads, grad_k_heads, grad_v_heads = lax.map(
        backward_head, (query_heads, key_heads, value_heads, grad_att_heads, log_total)
    )
    key_gradient_rows, grad_values = (
        lax.psum_scatter(
            join_heads(grad_k_heads).astype(jnp.bfloat16), "seq", scatter_dimension=1, tiled=True
        ).astype(jnp.float32),
        lax.psum_scatter(
            join_heads(grad_v_heads).astype(jnp.bfloat16), "seq", scatter_dimension=1, tiled=True
        ).astype(jnp.float32),
    )
    grad_projected = jnp.concatenate(
        [
            join_heads(grad_q_heads).reshape(row_count, model_width),
            key_gradient_rows.reshape(row_count, model_width),
            grad_values.reshape(row_count, model_width),
        ],
        1,
    ).astype(jnp.bfloat16)
    grad_query_bias = jnp.sum(grad_projected[:, :model_width].astype(jnp.float32), 0)
    grad_value_bias = jnp.sum(grad_projected[:, 2 * model_width :].astype(jnp.float32), 0)
    grad_qkv_local = row_dot(h_one_low, grad_projected)
    grad_h_one = last_dot(grad_projected, wide_qkv)
    grad_input_norm, grad_gain_one, grad_shift_one = norm_one_back(grad_h_one)
    grad_tokens = (grad_middle + grad_input_norm).reshape(images_here, slice_len, model_width)
    grad_gain_local = jnp.stack([grad_gain_one, grad_gain_two], 1)
    grad_bias_local = jnp.stack(
        [
            grad_shift_one,
            grad_query_bias,
            grad_value_bias,
            grad_out_bias,
            grad_shift_two,
            grad_bias_two,
        ],
        1,
    )
    owned = (
        lax.psum_scatter(grad_qkv_local, ("img", "seq"), scatter_dimension=0, tiled=True),
        lax.psum_scatter(output_gradient_shard, ("img", "seq"), scatter_dimension=0, tiled=True),
        lax.psum_scatter(grad_fc1_local, ("img", "seq"), scatter_dimension=0, tiled=True),
        lax.psum_scatter(grad_fc2_local, ("img", "seq"), scatter_dimension=0, tiled=True),
        lax.psum_scatter(grad_gain_local, ("img", "seq"), scatter_dimension=0, tiled=True),
        lax.psum_scatter(grad_bias_local, ("img", "seq"), scatter_dimension=0, tiled=True),
    )
    hidden_bias_total = lax.psum(grad_hidden_bias, ("img", "seq"))
    return (
        mixed,
        grad_tokens,
        owned[0],
        owned[1],
        owned[2],
        owned[3],
        owned[4],
        owned[5],
        hidden_bias_total,
    )


def solution(mesh):
    in_specs = (
        P("img", "seq", None),
        P("img"),
        P(("img", "seq"), None),
        P(("img", "seq"), None),
        P(("img", "seq"), None),
        P(("img", "seq"), None),
        P(("img", "seq"), None),
        P(("img", "seq"), None),
        P(),
        P("img", "seq", None),
    )
    out_specs = (
        P("img", "seq", None),
        P("img", "seq", None),
        P(("img", "seq"), None),
        P(("img", "seq"), None),
        P(("img", "seq"), None),
        P(("img", "seq"), None),
        P(("img", "seq"), None),
        P(("img", "seq"), None),
        P(),
    )
    shards = mesh.shape["img"] * mesh.shape["seq"]
    fits = mesh.shape["seq"] == 4 and shards == 2 * HEADS
    plan = whole_layer if fits else local
    return jax.shard_map(plan, mesh=mesh, in_specs=in_specs, out_specs=out_specs, check_vma=False)
```
